256 devices in a mesh: seq: 64 (over z_hi, x, y, core), head: 4 (over z_lo).
Axes of the slice: x: 4, y: 4, z: 8 (z_hi: 2, z_lo: 4; z = z_hi * 4 + z_lo), core: 2. Of those that a mesh axis runs over, the one named last changes fastest.
Arguments:
- video_query: bfloat16 [32768, 3072], P('seq', 'head'), may hold values from -18 to 18
- video_key: bfloat16 [32768, 3072], P('seq', 'head'), may hold values from -18 to 18
- video_value: bfloat16 [32768, 3072], P('seq', 'head'), may hold values from -6 to 6
- video_grad_out: bfloat16 [32768, 3072], P('seq', 'head'), may hold values from -6 to 6
- audio_query: bfloat16 [512, 3072], P('seq', 'head'), may hold values from -18 to 18
- audio_key: bfloat16 [512, 3072], P('seq', 'head'), may hold values from -18 to 18
- audio_value: bfloat16 [512, 3072], P('seq', 'head'), may hold values from -6 to 6
- audio_grad_out: bfloat16 [512, 3072], P('seq', 'head'), may hold values from -6 to 6
- video_query_gain: float32 [3072], P('head'), may hold values from 0.25 to 1.75
- video_key_gain: float32 [3072], P('head'), may hold values from 0.25 to 1.75
- audio_query_gain: float32 [3072], P('head'), may hold values from 0.25 to 1.75
- audio_key_gain: float32 [3072], P('head'), may hold values from 0.25 to 1.75
Outputs:
- video_out: bfloat16 [32768, 3072], P('seq', 'head')
- audio_out: bfloat16 [512, 3072], P('seq', 'head')
- grad_video_query: bfloat16 [32768, 3072], P('seq', 'head')
- grad_video_key: bfloat16 [32768, 3072], P('seq', 'head')
- grad_video_value: bfloat16 [32768, 3072], P('seq', 'head')
- grad_audio_query: bfloat16 [512, 3072], P('seq', 'head')
- grad_audio_key: bfloat16 [512, 3072], P('seq', 'head')
- grad_audio_value: bfloat16 [512, 3072], P('seq', 'head')
The draws below stay inside these ranges and needn't reach their ends.
All inputs are finite; a program needn't handle non-finite values.
Results may differ from the reference program's by a relative error of at most 0.034.
Values may be sent and summed in bfloat16 or wider, within the bound.
A program may use at most 128 MiB of HBM per device.

```python
import math
import jax
import jax.numpy as jnp
from jax import lax

HEADS = 24
HEAD_DIM = 128
VIDEO = 32768
AUDIO = 512


def rising(width):
    return jnp.exp(jnp.log(3.0) * jnp.arange(width, dtype=jnp.float32) / (width - 1))


def focused_keys(key, salt, rows, focus):
    width = HEADS * HEAD_DIM
    stream = jax.random.fold_in(key, salt)
    base = jnp.clip(jax.random.normal(stream, (rows, width), jnp.float32), -6.0, 6.0)
    index = jnp.arange(rows)
    picked = (index % 41 == 0).astype(jnp.float32)
    level = 0.2 * (index // 41 % 3).astype(jnp.float32)
    head_of = jnp.arange(width) // HEAD_DIM
    inside = (head_of[None, :] == (index % HEADS)[:, None]).astype(jnp.float32)
    shrink = inside + (1.0 - inside) * level[:, None]
    factor = 1.0 - focus * picked[:, None] * (1.0 - shrink)
    return base * factor * rising(width)[None, :]


def mixed_queries(own_key, rows, focus):
    width = HEADS * HEAD_DIM
    own = jnp.clip(jax.random.normal(own_key, (rows, width), jnp.float32), -6.0, 6.0) * rising(width)[None, :]
    index = jnp.arange(rows)
    chosen = focus * (index % 53 == 0).astype(jnp.float32)
    return own * (1.0 - chosen[:, None])


def draw_video_query(key, part):
    focus = 0.0
    key = jax.random.fold_in(key, 5)
    return mixed_queries(key, VIDEO, focus).astype(jnp.bfloat16)


def draw_audio_key(key, part):
    focus = 0.0
    return focused_keys(key, 11, AUDIO, focus).astype(jnp.bfloat16)


def draw_audio_query(key, part):
    focus = 0.0
    key = jax.random.fold_in(key, 7)
    return mixed_queries(key, AUDIO, focus).astype(jnp.bfloat16)


def draw_video_key(key, part):
    focus = 0.0
    return focused_keys(key, 23, VIDEO, focus).astype(jnp.bfloat16)


def levels(stream_key, dims, shards, low, largest):
    def one(dim, shards_of):
        heights = jax.random.uniform(jax.random.fold_in(jax.random.fold_in(stream_key, 6), dim), (shards_of,), jnp.float32, low / len(shards), largest / len(shards))
        return jnp.repeat(jnp.exp(heights), dims[dim] // shards_of).reshape((-1,) + (1,) * (len(dims) - dim - 1))

    level = one(*shards[0])
    for cut in shards[1:]:
        level = level * one(*cut)
    return level


def scatter_about(key, shape, scale, reach, split=(), kind=jnp.bfloat16):
    values = scale * jax.random.normal(key, shape, jnp.float32)
    if split:
        values = values * levels(key, shape, split, -0.22, 0.18)
    return jnp.clip(values, -reach, reach).astype(kind)


def setup_inputs(seed: int = 0) -> dict:
    key_list = jax.random.split(jax.random.key(seed), 13)
    return {
        "video_query": draw_video_query(jax.random.fold_in(key_list[12], 71), 0),
        "video_key": draw_video_key(jax.random.fold_in(key_list[12], 71), 0),
        "video_value": scatter_about(key_list[2], (VIDEO, HEADS * HEAD_DIM), 1.0, 6.0, ((0, 64), (1, 4))),
        "video_grad_out": scatter_about(key_list[3], (VIDEO, HEADS * HEAD_DIM), 1.0, 6.0, ((0, 64), (1, 4))),
        "audio_query": draw_audio_query(jax.random.fold_in(key_list[12], 71), 0),
        "audio_key": draw_audio_key(jax.random.fold_in(key_list[12], 71), 0),
        "audio_value": scatter_about(key_list[6], (AUDIO, HEADS * HEAD_DIM), 1.0, 6.0, ((0, 64), (1, 4))),
        "audio_grad_out": scatter_about(key_list[7], (AUDIO, HEADS * HEAD_DIM), 1.0, 6.0, ((0, 64), (1, 4))),
        "video_query_gain": jnp.clip(1.0 + 0.15 * jax.random.normal(key_list[8], (HEADS * HEAD_DIM,), jnp.float32), 0.25, 1.75),
        "video_key_gain": jnp.clip(1.0 + 0.15 * jax.random.normal(key_list[9], (HEADS * HEAD_DIM,), jnp.float32), 0.25, 1.75),
        "audio_query_gain": jnp.clip(1.0 + 0.15 * jax.random.normal(key_list[10], (HEADS * HEAD_DIM,), jnp.float32), 0.25, 1.75),
        "audio_key_gain": jnp.clip(1.0 + 0.15 * jax.random.normal(key_list[11], (HEADS * HEAD_DIM,), jnp.float32), 0.25, 1.75),
    }


EPS = 1e-06

def inverse_rms(raw):
    values = raw.astype(jnp.float32)
    return lax.rsqrt(lax.optimization_barrier(jnp.mean(values * values, axis=1, keepdims=True)) + EPS)

def by_heads(array):
    return array.reshape(array.shape[0], HEADS, HEAD_DIM).transpose(1, 0, 2)

def from_heads(array):
    return array.transpose(1, 0, 2).reshape(array.shape[1], HEADS * HEAD_DIM)

def norm_back(raw, inv_row, gain, grad):
    values = raw.astype(jnp.float32)
    inner = lax.optimization_barrier(jnp.sum(values * gain * grad, axis=1, keepdims=True))
    cube = inv_row * inv_row * inv_row
    return (inv_row * gain * grad - values * cube * inner / (HEADS * HEAD_DIM)).astype(jnp.bfloat16)

def one_head(pieces):
    vq, vk, vv, vdo, aq, ak, av, ado = pieces
    factor = 1.0 / math.sqrt(HEAD_DIM)
    scores = jnp.dot(vq, ak.T, preferred_element_type=jnp.float32) * factor
    expo = jnp.exp(scores - lax.optimization_barrier(jnp.max(scores, axis=1, keepdims=True)))
    probs = expo / lax.optimization_barrier(jnp.sum(expo, axis=1, keepdims=True))
    probs_low = probs.astype(jnp.bfloat16)
    video_out = jnp.dot(probs_low, av, preferred_element_type=jnp.float32).astype(jnp.bfloat16)
    row_dot = lax.optimization_barrier(jnp.sum(vdo.astype(jnp.float32) * video_out.astype(jnp.float32), axis=1, keepdims=True))
    dprob = jnp.dot(vdo, av.T, preferred_element_type=jnp.float32)
    dscore = (probs * (dprob - row_dot)).astype(jnp.bfloat16)
    grad_vq = jnp.dot(dscore, ak, preferred_element_type=jnp.float32) * factor
    grad_ak = jnp.dot(dscore.T, vq, preferred_element_type=jnp.float32) * factor
    grad_av = jnp.dot(probs_low.T, vdo, preferred_element_type=jnp.float32).astype(jnp.bfloat16)
    scores_a = jnp.dot(aq, vk.T, preferred_element_type=jnp.float32) * factor
    top = lax.optimization_barrier(jnp.max(scores_a, axis=1, keepdims=True))
    expo_a = jnp.exp(scores_a - top)
    total = lax.optimization_barrier(jnp.sum(expo_a, axis=1, keepdims=True))
    numer = jnp.dot(expo_a.astype(jnp.bfloat16), vv, preferred_element_type=jnp.float32)
    audio_out = (numer / total).astype(jnp.bfloat16)
    lse = top + jnp.log(total)
    probs_a = jnp.exp(scores_a - lse)
    probs_a_low = probs_a.astype(jnp.bfloat16)
    grad_vv = jnp.dot(probs_a_low.T, ado, preferred_element_type=jnp.float32).astype(jnp.bfloat16)
    row_dot_a = lax.optimization_barrier(jnp.sum(ado.astype(jnp.float32) * audio_out.astype(jnp.float32), axis=1, keepdims=True))
    dprob_a = jnp.dot(ado, vv.T, preferred_element_type=jnp.float32)
    dscore_a = (probs_a * (dprob_a - row_dot_a)).astype(jnp.bfloat16)
    grad_aq = jnp.dot(dscore_a, vk, preferred_element_type=jnp.float32) * factor
    grad_vk = jnp.dot(dscore_a.T, aq, preferred_element_type=jnp.float32) * factor
    return (video_out, audio_out, grad_vq, grad_vk, grad_vv, grad_aq, grad_ak, grad_av)

def reference(video_query, video_key, video_value, video_grad_out, audio_query, audio_key, audio_value, audio_grad_out, video_query_gain, video_key_gain, audio_query_gain, audio_key_gain):
    raws = (video_query, video_key, audio_query, audio_key)
    gains = (video_query_gain, video_key_gain, audio_query_gain, audio_key_gain)
    inverses = [inverse_rms(raw) for raw in raws]
    normed = [(raw.astype(jnp.float32) * inv_row * gain).astype(jnp.bfloat16) for raw, inv_row, gain in zip(raws, inverses, gains)]
    pieces = (by_heads(normed[0]), by_heads(normed[1]), by_heads(video_value), by_heads(video_grad_out), by_heads(normed[2]), by_heads(normed[3]), by_heads(audio_value), by_heads(audio_grad_out))
    results = lax.map(one_head, pieces)
    video_out, audio_out, grad_vq, grad_vk, grad_vv, grad_aq, grad_ak, grad_av = [from_heads(item) for item in results]
    grads = (grad_vq, grad_vk, grad_aq, grad_ak)
    finals = [norm_back(raw, inv_row, gain, grad) for raw, inv_row, gain, grad in zip(raws, inverses, gains, grads)]
    return (video_out, audio_out, finals[0], finals[1], grad_vv, finals[2], finals[3], grad_av)
```

```python
import math

import jax
import jax.numpy as jnp
from jax import lax
from jax.experimental import pallas as pl
from jax.experimental.pallas import tpu as pltpu
from jax.sharding import PartitionSpec as P

HEADS = 24
D = 128
WIDTH = HEADS * D
EPS = 1e-06
FACTOR = 1.0 / math.sqrt(D)
KLOG = FACTOR * math.log2(math.e)
ROWS = 512
TOK = 512
LOCAL = 768
HALF = 384
NH = 6
F32 = jnp.float32
BF16 = jnp.bfloat16
MESH = pl.DeviceIdType.MESH
NT = (((1,), (1,)), ((), ()))
TN = (((0,), (0,)), ((), ()))
NN = (((1,), (0,)), ((), ()))


def dot(a, b, dims):
    return lax.dot_general(a, b, dims, preferred_element_type=F32)


def col(row):
    return jnp.transpose(jnp.broadcast_to(row, (D, ROWS)))


def row_of(square):
    return jnp.sum(jnp.transpose(square), axis=0, keepdims=True)


def kernel(
    vq, vk, vv, vdo, aq, ak, av, ado, gvq_gain, gvk_gain, gaq_gain, gak_gain,
    video_out, out_gvq, out_gvk, out_gvv, out_small,
    G, CXs, CXr, HS, HI, HA, vqn, vkn, inv_col, E, DP, ST, SR, WT,
    GQ, GK, IA, Xs, Xr, R, RB1, RB2, S, RB3, TZ, RB4, FS, FR, sm,
    send, recv,
):
    s = lax.axis_index("seq")
    hd = lax.axis_index("head")
    c = s % 2
    y = (s // 2) % 4
    x = (s // 8) % 4
    zh = s // 32
    p = x + c * (y - x)
    q = y + c * (x - y)
    o = 1 - c

    def at(zz, pp, qq):
        xx = pp + c * (qq - pp)
        yy = qq + c * (pp - qq)
        return {"seq": ((zz * 4 + xx) * 4 + yy) * 2 + c}

    sib = {"seq": s + 1 - 2 * c}
    opp = at(1 - zh, p, q)
    opp_sib = {"seq": s + 1 - 2 * c + 32 - 64 * zh}
    ring_p = [at(zh, (p + k) % 4, q) for k in (1, 2, 3)]
    ring_q = [at(zh, p, (q + k) % 4) for k in (1, 2, 3)]
    heads = [{"head": (hd + k) % 4} for k in (1, 2, 3)]
    pn, pb = (p + 1) % 4, (p + 3) % 4
    qn, qb = (q + 1) % 4, (q + 3) % 4
    q2 = (q + 2) % 4
    right_p, left_p = ring_p[0], ring_p[2]
    right_q, left_q = ring_q[0], ring_q[2]

    barrier = pltpu.get_barrier_semaphore()
    partners = [sib, opp, opp_sib] + ring_p + ring_q + heads
    for partner in partners:
        pl.semaphore_signal(barrier, inc=1, device_id=partner, device_id_type=MESH)
    pl.semaphore_wait(barrier, len(partners))

    count = [0]

    def copy(src, dst, to, slot=None):
        if slot is None:
            slot = count[0]
            count[0] += 1
        made = pltpu.make_async_remote_copy(
            src_ref=src,
            dst_ref=dst,
            send_sem=send.at[slot],
            recv_sem=recv.at[slot],
            device_id=to,
            device_id_type=MESH,
        )
        return made

    def go(*copies):
        for one in copies:
            one.start()
        return copies

    def done(copies):
        for one in copies:
            one.wait()

    my_half = pl.ds(pl.multiple_of(c * HALF, D), HALF)
    its_half = pl.ds(pl.multiple_of(o * HALF, D), HALF)

    def ag_core(ch, refs):
        for a, ref in enumerate(refs):
            CXs[ch, a] = ref[:, its_half].astype(F32)
        return go(copy(CXs.at[ch], CXr.at[ch], sib))

    def ag_z(ch, refs):
        for a, ref in enumerate(refs):
            mine = ref[:, my_half].astype(F32)
            other = CXr[ch, a]
            low = jnp.where(c == 0, mine, other)
            high = jnp.where(c == 0, other, mine)
            G[c, ch, q, p, zh, a] = jnp.concatenate([low, high], axis=0).astype(BF16)
        block = G.at[c, ch, q, p, zh]
        return go(copy(block, block, opp))

    def ag_p1(ch):
        block = G.at[c, ch, q, p]
        return go(copy(block, block, right_p), copy(block, block, left_p))

    def ag_p2(ch):
        one, two = G.at[c, ch, q, pb, 0], G.at[c, ch, q, pn, 1]
        return go(copy(one, one, right_p), copy(two, two, left_p))

    def forward(ch, i):
        block = G.at[c, ch, i]
        return go(copy(block, block, sib))

    def ag_q1(ch):
        block = G.at[c, ch, q]
        return go(copy(block, block, right_q), copy(block, block, left_q))

    def ag_q2(ch):
        one, two = G.at[c, ch, qb, 0:2], G.at[c, ch, qn, 2:4]
        return go(copy(one, one, right_q), copy(two, two, left_q))

    core0 = ag_core(0, (av, ado))

    HS[hd] = jnp.zeros((16, 512), F32)
    for i, raw in enumerate((vq, vk)):
        total = jnp.zeros((ROWS, D), F32)
        for b in range(NH):
            block = raw[:, b * D : (b + 1) * D].astype(F32)
            total = total + block * block
        HS[hd, i : i + 1, :] = row_of(total)
    for i, raw in enumerate((aq, ak)):
        block = raw[...].astype(F32)
        total = jnp.sum(block * block, axis=1, keepdims=True)
        HS[hd, 8:16, i * D : (i + 1) * D] = jnp.broadcast_to(total, (8, D))
    sums = go(*[copy(HS.at[hd], HS.at[hd], to) for to in heads])

    done(core0)
    z0 = ag_z(0, (av, ado))
    done(sums)
    total = HS[0] + HS[1] + HS[2] + HS[3]
    inv = lax.rsqrt(total / WIDTH + EPS)
    inv_a = [inv[8:16, 0:D], inv[8:16, D : 2 * D]]
    for i, (raw, gain) in enumerate(((aq, gaq_gain), (ak, gak_gain))):
        wide = jnp.concatenate([inv_a[i]] * NH, axis=1)
        sm[i] = (raw[...].astype(F32) * wide * gain[...]).astype(BF16).astype(F32)
    normed_audio = (sm.at[0], sm.at[1])
    core1 = ag_core(1, normed_audio)
    done(z0)
    p10 = ag_p1(0)
    done(core1)
    z1 = ag_z(1, normed_audio)

    for i, (raw, gain, out) in enumerate(((vq, gvq_gain, vqn), (vk, gvk_gain, vkn))):
        inv_col[i] = col(inv[i : i + 1, :])
        for b in range(NH):
            at_b = slice(b * D, (b + 1) * D)
            out[:, at_b] = (raw[:, at_b].astype(F32) * inv_col[i] * gain[:, at_b]).astype(BF16)

    done(p10)
    p20 = ag_p2(0)
    done(z1)
    p11 = ag_p1(1)
    done(p20)
    q10 = ag_q1(0)
    f0 = forward(0, q)
    done(p11)
    p21 = ag_p2(1)
    done(p21)
    q11 = ag_q1(1)
    f1 = forward(1, q)
    done(q10)
    q20 = ag_q2(0)
    f0 += forward(0, qn) + forward(0, qb)
    done(q11)
    q21 = ag_q2(1)
    f1 += forward(1, qn) + forward(1, qb)
    done(q20)
    f0 += forward(0, q2)
    done(q21)
    f1 += forward(1, q2)

    def lanes_of(i):
        return pl.ds(pl.multiple_of(i * D, D), D)

    ST[...] = jnp.zeros_like(ST)

    def first_pass(h, j):
        head = 3 * h + j
        lanes, jl = lanes_of(head), lanes_of(j)
        for t in range(2):
            chunk = slice(256 * t, 256 * (t + 1))
            qs = G[h, 1, 2 * t : 2 * t + 2, :, :, 0, :, jl].reshape(256, D)
            dos = G[h, 0, 2 * t : 2 * t + 2, :, :, 1, :, jl].reshape(256, D)
            scores = dot(vkn[:, lanes], qs, NT) * KLOG
            top = jnp.max(scores, axis=0, keepdims=True)
            expo = jnp.exp2(scores - top)
            dprob = dot(vv[:, lanes], dos, NT)
            E[head, :, chunk] = expo
            DP[head, :, chunk] = dprob
            row = pl.ds(head, 1)
            ST[0, 0, row, chunk] = top
            ST[0, 1, row, chunk] = jnp.sum(expo, axis=0, keepdims=True)
            ST[0, 2, row, chunk] = jnp.sum(expo * dprob, axis=0, keepdims=True)

    def loop(body):
        def step(j, carry):
            body(j)
            return carry

        lax.fori_loop(0, 3, step, 0)

    loop(lambda j: first_pass(c, j))
    done(f0)
    done(f1)
    loop(lambda j: first_pass(o, j))

    def stats_start(level, to):
        return go(*[copy(ST.at[level], SR.at[level, k], one) for k, one in enumerate(to)])

    def stats_merge(level, copies):
        done(copies)
        tops = [ST[level, 0]] + [SR[level, k, 0] for k in range(3)]
        top = jnp.maximum(jnp.maximum(tops[0], tops[1]), jnp.maximum(tops[2], tops[3]))
        weights = [jnp.exp2(one - top) for one in tops]
        ST[level + 1, 0] = top
        for n in (1, 2):
            total = ST[level, n] * weights[0]
            for k in range(3):
                total = total + SR[level, k, n] * weights[k + 1]
            ST[level + 1, n] = total

    level0 = stats_start(0, (sib, opp, opp_sib))

    IA[...] = jnp.zeros_like(IA)

    def cross_slot(ch, j):
        return base_cross + 3 * ch + j

    base_cross = count[0]
    count[0] += 6

    def cross(ch, j):
        return copy(Xs.at[ch, j], Xr.at[ch, j], sib, slot=cross_slot(ch, j))

    def video_pass(h, j, own):
        head = 3 * h + j
        lanes, jl = lanes_of(head), lanes_of(j)
        keys = G[h, 1, :, :, :, 1, :, jl].reshape(TOK, D)
        values = G[h, 0, :, :, :, 0, :, jl].reshape(TOK, D)
        grad_k = grad_v = None
        for t in range(2):
            chunk = slice(256 * t, 256 * (t + 1))
            qs, dos = vqn[chunk, lanes], vdo[chunk, lanes]
            scores = dot(keys, qs, NT) * KLOG
            top = jnp.max(scores, axis=0, keepdims=True)
            expo = jnp.exp2(scores - top)
            probs = expo * (1.0 / jnp.sum(expo, axis=0, keepdims=True))
            low = probs.astype(BF16)
            dprob = dot(values, dos, NT)
            inner = jnp.sum(probs * dprob, axis=0, keepdims=True)
            ds = (probs * (dprob - inner)).astype(BF16)
            video_out[chunk, lanes] = dot(low, values, TN).astype(BF16)
            grad_q = dot(ds, keys, TN) * FACTOR
            GQ[chunk, lanes] = grad_q
            IA[0, chunk] += vq[chunk, lanes].astype(F32) * gvq_gain[:, lanes] * grad_q
            more_k, more_v = dot(ds, qs, NN), dot(low, dos, NN)
            grad_k = more_k if grad_k is None else grad_k + more_k
            grad_v = more_v if grad_v is None else grad_v + more_v
        put(0, h, j, own, slice(0, 4), 0, grad_k * FACTOR)
        put(0, h, j, own, slice(0, 4), 1, grad_v)

    def put(ch, h, j, own, chunks, a, value):
        rows = slice(128 * chunks.start, 128 * chunks.stop)
        if own:
            value = value + Xr[ch, j, a, rows].astype(F32)
            shape = (chunks.stop - chunks.start, 4, 2, 16, D)
            R[ch, chunks, :, :, a, :, lanes_of(j)] = value.reshape(shape).astype(BF16)
        else:
            Xs[ch, j, a, rows] = value.astype(BF16)

    def theirs(ch, work):
        def body(j):
            work(o, j, False)
            cross(ch, j).start()

        loop(body)

    def ours(ch, work):
        def body(j):
            cross(ch, j).wait()
            work(c, j, True)

        loop(body)

    theirs(0, video_pass)
    stats_merge(0, level0)
    level1 = stats_start(1, ring_p)
    ours(0, video_pass)
    stats_merge(1, level1)
    level2 = stats_start(2, ring_q)

    def rs_q1(ch):
        return go(
            copy(R.at[ch, q2, 0:2], RB1.at[ch, 0], right_q),
            copy(R.at[ch, q2, 2:4], RB1.at[ch, 1], left_q),
        )

    def rs_q2(ch, copies):
        done(copies)
        one = R[ch, qn, 0:2].astype(F32) + RB1[ch, 0].astype(F32)
        R[ch, qn, 0:2] = one.astype(BF16)
        two = R[ch, qb, 2:4].astype(F32) + RB1[ch, 1].astype(F32)
        R[ch, qb, 2:4] = two.astype(BF16)
        return go(
            copy(R.at[ch, qn], RB2.at[ch, 0], right_q),
            copy(R.at[ch, qb], RB2.at[ch, 1], left_q),
        )

    def rs_p(ch, copies):
        done(copies)
        total = R[ch, q].astype(F32) + RB2[ch, 0].astype(F32) + RB2[ch, 1].astype(F32)
        S[ch] = total.astype(BF16)
        return go(
            *[copy(S.at[ch, (p + k + 1) % 4], RB3.at[ch, k], ring_p[k]) for k in range(3)]
        )

    def rs_z(ch, copies):
        done(copies)
        total = S[ch, p].astype(F32)
        for k in range(3):
            total = total + RB3[ch, k].astype(F32)
        TZ[ch] = total.astype(BF16)
        return go(copy(TZ.at[ch, 1 - zh], RB4.at[ch], opp))

    def rs_core(ch, copies):
        done(copies)
        FS[ch] = TZ[ch, zh].astype(F32) + RB4[ch].astype(F32)
        theirs_rows = pl.ds(pl.multiple_of(o * 8, 8), 8)
        return go(copy(FS.at[ch, :, theirs_rows], FR.at[ch], sib))

    def rs_end(ch, copies, slots):
        done(copies)
        mine = pl.ds(pl.multiple_of(c * 8, 8), 8)
        for a, slot in enumerate(slots):
            sm[slot, :, my_half] = FS[ch, a, mine]
            sm[slot, :, its_half] = FR[ch, a]

    a1 = rs_q1(0)
    stats_merge(2, level2)

    total = ST[3, 1]
    safe = jnp.where(total == 0.0, 1.0, total)
    WT[0] = jnp.exp2(ST[0, 0] - ST[3, 0]) / safe
    WT[1] = ST[3, 2] / safe

    def second_pass(h, j, own):
        head = 3 * h + j
        lanes, jl = lanes_of(head), lanes_of(j)
        vks, vvs = vkn[:, lanes], vv[:, lanes]
        grad_k = grad_v = None
        for t in range(2):
            chunk = slice(256 * t, 256 * (t + 1))
            chunks = slice(2 * t, 2 * t + 2)
            row = pl.ds(head, 1)
            qs = G[h, 1, chunks, :, :, 0, :, jl].reshape(256, D)
            dos = G[h, 0, chunks, :, :, 1, :, jl].reshape(256, D)
            probs = E[head, :, chunk] * WT[0, row, chunk]
            low = probs.astype(BF16)
            ds = (probs * (DP[head, :, chunk] - WT[1, row, chunk])).astype(BF16)
            put(1, h, j, own, chunks, 0, dot(low, vvs, TN))
            put(1, h, j, own, chunks, 1, dot(ds, vks, TN) * FACTOR)
            more_k, more_v = dot(ds, qs, NN), dot(low, dos, NN)
            grad_k = more_k if grad_k is None else grad_k + more_k
            grad_v = more_v if grad_v is None else grad_v + more_v
        grad_k = grad_k * FACTOR
        out_gvv[:, lanes] = grad_v.astype(BF16)
        GK[:, lanes] = grad_k
        IA[1] += vk[:, lanes].astype(F32) * gvk_gain[:, lanes] * grad_k

    theirs(1, second_pass)
    a2 = rs_q2(0, a1)
    ours(1, second_pass)
    b1 = rs_q1(1)
    HI[hd] = jnp.zeros((8, 512), F32)
    HI[hd, 0:1, :] = row_of(IA[0])
    HI[hd, 1:2, :] = row_of(IA[1])
    inners = go(*[copy(HI.at[hd], HI.at[hd], to) for to in heads])
    a3 = rs_p(0, a2)
    b2 = rs_q2(1, b1)
    done(inners)
    inner = (HI[0] + HI[1] + HI[2] + HI[3]) / WIDTH

    def video_final(i, raw, gain, grad, out):
        inv_i = inv_col[i]
        scale = inv_i * inv_i * inv_i * col(inner[i : i + 1, :])
        for b in range(NH):
            at_b = slice(b * D, (b + 1) * D)
            value = inv_i * gain[:, at_b] * grad[:, at_b] - raw[:, at_b].astype(F32) * scale
            out[:, at_b] = value.astype(BF16)

    a4 = rs_z(0, a3)
    video_final(0, vq, gvq_gain, GQ, out_gvq)
    b3 = rs_p(1, b2)
    a5 = rs_core(0, a4)
    video_final(1, vk, gvk_gain, GK, out_gvk)
    b4 = rs_z(1, b3)
    rs_end(0, a5, (3, 4))
    b5 = rs_core(1, b4)
    rs_end(1, b5, (5, 2))
    parts = ((aq, gaq_gain, sm[2]), (ak, gak_gain, sm[3]))
    for i, (raw, gain, grad) in enumerate(parts):
        total = jnp.sum(raw[...].astype(F32) * gain[...] * grad, axis=1, keepdims=True)
        HA[hd, i] = jnp.broadcast_to(total, (8, D))
    small = go(*[copy(HA.at[hd], HA.at[hd], to) for to in heads])
    out_small[0] = sm[5]
    out_small[3] = sm[4]
    done(small)
    for i, (raw, gain, grad) in enumerate(parts):
        total = (HA[0, i] + HA[1, i] + HA[2, i] + HA[3, i]) / WIDTH
        wide = jnp.concatenate([inv_a[i]] * NH, axis=1)
        scale = jnp.concatenate([inv_a[i] * inv_a[i] * inv_a[i] * total] * NH, axis=1)
        out_small[1 + i] = wide * gain[...] * grad - raw[...].astype(F32) * scale


def shards(*args):
    arrays, gains = args[:8], [gain.reshape(1, LOCAL) for gain in args[8:]]
    big = jax.ShapeDtypeStruct((ROWS, LOCAL), BF16)
    vmem = pltpu.VMEM
    scratch = [
        vmem((2, 2, 4, 4, 2, 2, 16, HALF), BF16),
        vmem((2, 2, 8, HALF), F32),
        vmem((2, 2, 8, HALF), F32),
        vmem((4, 16, 512), F32),
        vmem((4, 8, 512), F32),
        vmem((4, 2, 8, D), F32),
        vmem((ROWS, LOCAL), BF16),
        vmem((ROWS, LOCAL), BF16),
        vmem((2, ROWS, D), F32),
        vmem((NH, ROWS, TOK), F32),
        vmem((NH, ROWS, TOK), F32),
        vmem((4, 3, 8, TOK), F32),
        vmem((3, 3, 3, 8, TOK), F32),
        vmem((2, 8, TOK), F32),
        vmem((ROWS, LOCAL), F32),
        vmem((ROWS, LOCAL), F32),
        vmem((2, ROWS, D), F32),
        vmem((2, 3, 2, TOK, D), BF16),
        vmem((2, 3, 2, TOK, D), BF16),
        vmem((2, 4, 4, 2, 2, 16, HALF), BF16),
        vmem((2, 2, 2, 2, 2, 16, HALF), BF16),
        vmem((2, 2, 4, 2, 2, 16, HALF), BF16),
        vmem((2, 4, 2, 2, 16, HALF), BF16),
        vmem((2, 3, 2, 2, 16, HALF), BF16),
        vmem((2, 2, 2, 16, HALF), BF16),
        vmem((2, 2, 16, HALF), BF16),
        vmem((2, 2, 16, HALF), F32),
        vmem((2, 2, 8, HALF), F32),
        vmem((6, 8, LOCAL), F32),
        pltpu.SemaphoreType.DMA((80,)),
        pltpu.SemaphoreType.DMA((80,)),
    ]
    spec = pl.BlockSpec(memory_space=pltpu.VMEM)
    made = pl.pallas_call(
        kernel,
        out_shape=(big, big, big, big, jax.ShapeDtypeStruct((4, 8, LOCAL), F32)),
        in_specs=[spec] * 12,
        out_specs=(spec,) * 5,
        scratch_shapes=scratch,
        compiler_params=pltpu.CompilerParams(
            collective_id=0, has_side_effects=True, vmem_limit_bytes=56 * 1024 * 1024
        ),
    )(*arrays, *gains)
    video_out, gvq, gvk, gvv, small = made
    small = small.astype(BF16)
    return video_out, small[0], gvq, gvk, gvv, small[1], small[2], small[3]


def solution(mesh):
    both = P("seq", "head")
    return jax.shard_map(
        shards,
        mesh=mesh,
        in_specs=(both,) * 8 + (P("head"),) * 4,
        out_specs=(both,) * 8,
        check_vma=False,
    )
```

```python
import math

import jax
import jax.numpy as jnp
from jax import lax
from jax.experimental import pallas as pl
from jax.experimental.pallas import tpu as pltpu
from jax.sharding import PartitionSpec as P

HEADS = 24
D = 128
WIDTH = HEADS * D
EPS = 1e-06
FACTOR = 1.0 / math.sqrt(D)
KLOG = FACTOR * math.log2(math.e)
ROWS = 512
TOK = 512
LOCAL = 768
HALF = 384
NH = 6
F32 = jnp.float32
BF16 = jnp.bfloat16
MESH = pl.DeviceIdType.MESH
NT = (((1,), (1,)), ((), ()))
TN = (((0,), (0,)), ((), ()))
NN = (((1,), (0,)), ((), ()))


def dot(a, b, dims):
    return lax.dot_general(a, b, dims, preferred_element_type=F32)


def col(row):
    return jnp.transpose(jnp.broadcast_to(row, (D, ROWS)))


def row_of(square):
    return jnp.sum(jnp.transpose(square), axis=0, keepdims=True)


def kernel(
    vq_in, vk_in, vv_in, vdo_in, aq, ak, av, ado, gain0, gain1, gain2, gain3,
    video_out_hbm, gvq_hbm, gvk_hbm, gvv_hbm, out_small,
    vq, vk, vv, vdo, video_out, out_gvq, out_gvk, out_gvv, GN, RA,
    G, PK, PR, HSA, HS, HI, HAs, HAr, vqn, vkn, inv_col, E, DP, EV, DV, SV, ST, SR, WT,
    GQ, GK, IA, Xs, Xr, R, RB1, RB2, S, RB3, TZ, RB4, FS, FR, sm,
    send, recv, local,
):
    s = lax.axis_index("seq")
    hd = lax.axis_index("head")
    c = s % 2
    y = (s // 2) % 4
    x = (s // 8) % 4
    zh = s // 32
    p = x + c * (y - x)
    q = y + c * (x - y)
    o = 1 - c

    def at(zz, pp, qq):
        xx = pp + c * (qq - pp)
        yy = qq + c * (pp - qq)
        return {"seq": ((zz * 4 + xx) * 4 + yy) * 2 + c}

    sib = {"seq": s + 1 - 2 * c}
    opp = at(1 - zh, p, q)
    opp_sib = {"seq": s + 1 - 2 * c + 32 - 64 * zh}
    ring_p = [at(zh, (p + k) % 4, q) for k in (1, 2, 3)]
    ring_q = [at(zh, p, (q + k) % 4) for k in (1, 2, 3)]
    heads = [{"head": (hd + k) % 4} for k in (1, 2, 3)]
    heads_sib = [{"seq": s + 1 - 2 * c, "head": (hd + k) % 4} for k in (1, 2, 3)]
    pn, pb, p2 = (p + 1) % 4, (p + 3) % 4, (p + 2) % 4
    qn, qb, q2 = (q + 1) % 4, (q + 3) % 4, (q + 2) % 4
    right_q, left_q = ring_q[0], ring_q[2]

    barrier = pltpu.get_barrier_semaphore()
    partners = [sib, opp, opp_sib] + ring_p + ring_q + heads + heads_sib
    for partner in partners:
        pl.semaphore_signal(barrier, inc=1, device_id=partner, device_id_type=MESH)
    loads = [
        pltpu.make_async_copy(src, dst, local.at[i])
        for i, (src, dst) in enumerate(((vq_in, vq), (vk_in, vk), (vv_in, vv), (vdo_in, vdo)))
    ]
    for one in loads:
        one.start()
    for i, gain in enumerate((gain0, gain1, gain2, gain3)):
        GN[i : i + 1, :] = gain[...].reshape(1, LOCAL)
    gvq_gain, gvk_gain, gaq_gain, gak_gain = (GN.at[i : i + 1] for i in range(4))

    count = [0]

    def slots(n):
        first = count[0]
        count[0] += n
        return first

    def copy(src, dst, to, slot=None):
        slot = slots(1) if slot is None else slot
        return pltpu.make_async_remote_copy(
            src_ref=src,
            dst_ref=dst,
            send_sem=send.at[slot],
            recv_sem=recv.at[slot],
            device_id=to,
            device_id_type=MESH,
        )

    def go(*copies):
        for one in copies:
            one.start()
        return copies

    def done(copies):
        for one in copies:
            one.wait()

    half_of = [pl.ds(pl.multiple_of(i * HALF, D), HALF) for i in (c, o)]

    def pack(n, refs):
        for i, half in enumerate(half_of):
            rows = [ref[:, half].astype(F32) for ref in refs]
            PK[n, i] = jnp.concatenate(rows, axis=0).astype(BF16)

    def ag_first(n):
        return go(
            copy(PK.at[n, 1], PR.at[n, 0], sib),
            copy(PK.at[n, 0], PR.at[n, 1], opp),
            copy(PK.at[n, 1], PR.at[n, 2], opp_sib),
        )

    def chip_rows(mine, other, a):
        mine = mine.astype(F32)[8 * a : 8 * a + 8]
        other = other.astype(F32)[8 * a : 8 * a + 8]
        low = jnp.where(c == 0, mine, other)
        high = jnp.where(c == 0, other, mine)
        return jnp.concatenate([low, high], axis=0)

    def ag_p(ch, copies):
        done(copies)
        for a in range(2):
            G[c, ch, q, p, zh, a] = chip_rows(PK[ch, 0], PR[ch, 0], a).astype(BF16)
            G[c, ch, q, p, 1 - zh, a] = chip_rows(PR[ch, 1], PR[ch, 2], a).astype(BF16)
        block = G.at[c, ch, q, p]
        return go(*[copy(block, block, to) for to in ring_p])

    def forward(ch, i):
        block = G.at[c, ch, i]
        return go(copy(block, block, sib))

    def ag_q1(ch, copies):
        done(copies)
        block = G.at[c, ch, q]
        return go(copy(block, block, right_q), copy(block, block, left_q))

    def ag_q2(ch, copies):
        done(copies)
        one, two = G.at[c, ch, qb, 0:2], G.at[c, ch, qn, 2:4]
        return go(copy(one, one, right_q), copy(two, two, left_q))

    pack(0, (av, ado))
    for i, raw in enumerate((aq, ak)):
        block = raw[...].astype(F32)
        total = jnp.sum(block * block, axis=1, keepdims=True)
        HSA[hd, i] = jnp.broadcast_to(total, (8, D))
    pl.semaphore_wait(barrier, len(partners))
    sums_a = go(*[copy(HSA.at[hd], HSA.at[hd], to) for to in heads])
    first0 = ag_first(0)
    pack(2, (aq, ak))
    raws = go(copy(PK.at[2, 1], PR.at[2, 0], sib))

    HS[hd] = jnp.zeros((8, 512), F32)

    def video_sum(i, raw):
        loads[i].wait()
        total = jnp.zeros((ROWS, D), F32)
        for b in range(NH):
            block = raw[:, b * D : (b + 1) * D].astype(F32)
            total = total + block * block
        HS[hd, i : i + 1, :] = row_of(total)

    video_sum(0, vq)
    done(sums_a)
    inv_a = []
    for i, (raw, gain) in enumerate(((aq, gaq_gain), (ak, gak_gain))):
        total = HSA[0, i] + HSA[1, i] + HSA[2, i] + HSA[3, i]
        inv_a.append(lax.rsqrt(total / WIDTH + EPS))
        wide = jnp.concatenate([inv_a[i]] * NH, axis=1)
        sm[i] = (raw[...].astype(F32) * wide * gain[...]).astype(BF16).astype(F32)
    pack(1, (sm.at[0], sm.at[1]))
    first1 = ag_first(1)
    ring0 = ag_p(0, first0)
    video_sum(1, vk)
    sums = go(*[copy(HS.at[hd], HS.at[hd], to) for to in heads])
    ring1 = ag_p(1, first1)
    q10 = ag_q1(0, ring0)
    f0 = [forward(0, q)]
    done(sums)
    total = HS[0] + HS[1] + HS[2] + HS[3]
    inv = lax.rsqrt(total / WIDTH + EPS)

    def norm_video(i, raw, gain, out):
        inv_col[i] = col(inv[i : i + 1, :])
        for b in range(NH):
            at_b = slice(b * D, (b + 1) * D)
            out[:, at_b] = (raw[:, at_b].astype(F32) * inv_col[i] * gain[:, at_b]).astype(BF16)

    norm_video(1, vk, gvk_gain, vkn)
    q11 = ag_q1(1, ring1)
    f1 = [forward(1, q)]
    norm_video(0, vq, gvq_gain, vqn)

    def lanes_of(i):
        return pl.ds(pl.multiple_of(i * D, D), D)

    ST[...] = jnp.zeros_like(ST)

    def first_pass(h, j, i):
        head = 3 * h + j
        lanes, jl, chunk = lanes_of(head), lanes_of(j), lanes_of(i)
        keys = G[h, 1, i, :, :, 1, :, jl].reshape(D, D)
        values = G[h, 0, i, :, :, 0, :, jl].reshape(D, D)
        scores = dot(keys, vqn[:, lanes], NT) * KLOG
        top = jnp.max(scores, axis=0, keepdims=True)
        expo = jnp.exp2(scores - top)
        dprob = dot(values, vdo[:, lanes], NT)
        EV[head, chunk, :] = expo
        DV[head, chunk, :] = dprob
        row = pl.ds(i, 1)
        SV[0, head, row, :] = top
        SV[1, head, row, :] = jnp.sum(expo, axis=0, keepdims=True)
        SV[2, head, row, :] = jnp.sum(expo * dprob, axis=0, keepdims=True)
        qs = G[h, 1, i, :, :, 0, :, jl].reshape(D, D)
        dos = G[h, 0, i, :, :, 1, :, jl].reshape(D, D)
        scores = dot(vkn[:, lanes], qs, NT) * KLOG
        top = jnp.max(scores, axis=0, keepdims=True)
        expo = jnp.exp2(scores - top)
        dprob = dot(vv[:, lanes], dos, NT)
        E[head, :, chunk] = expo
        DP[head, :, chunk] = dprob
        row = pl.ds(head, 1)
        ST[0, 0, i, row, :] = top
        ST[0, 1, i, row, :] = jnp.sum(expo, axis=0, keepdims=True)
        ST[0, 2, i, row, :] = jnp.sum(expo * dprob, axis=0, keepdims=True)

    def loop(body):
        def step(j, carry):
            body(j)
            return carry

        lax.fori_loop(0, 3, step, 0)

    def first(h, *chunks):
        for i in chunks:
            loop(lambda j: first_pass(h, j, i))

    loads[2].wait()
    loads[3].wait()
    first(c, q)
    q20 = ag_q2(0, q10)
    f0 += [forward(0, qn), forward(0, qb)]
    q21 = ag_q2(1, q11)
    f1 += [forward(1, qn), forward(1, qb)]
    first(c, qn, qb)
    done(q20)
    f0.append(forward(0, q2))
    done(q21)
    f1.append(forward(1, q2))
    done(f0[0] + f1[0])
    first(o, p)
    first(c, q2)
    done(f0[1] + f1[1])
    first(o, pn)
    done(f0[2] + f1[2])
    first(o, pb)
    done(f0[3] + f1[3])
    first(o, p2)

    def stats_start(level, to):
        return go(*[copy(ST.at[level], SR.at[level, k], one) for k, one in enumerate(to)])

    def stats_merge(level, copies):
        done(copies)
        tops = [ST[level, 0]] + [SR[level, k, 0] for k in range(3)]
        top = jnp.maximum(jnp.maximum(tops[0], tops[1]), jnp.maximum(tops[2], tops[3]))
        weights = [jnp.exp2(one - top) for one in tops]
        ST[level + 1, 0] = top
        for n in (1, 2):
            total = ST[level, n] * weights[0]
            for k in range(3):
                total = total + SR[level, k, n] * weights[k + 1]
            ST[level + 1, n] = total

    level0 = stats_start(0, (sib, opp, opp_sib))
    done(raws)
    for i, gain in enumerate((gaq_gain, gak_gain)):
        RA[i] = chip_rows(PK[2, 0], PR[2, 0], i) * gain[:, half_of[0]]

    IA[...] = jnp.zeros_like(IA)
    base_cross = slots(6)

    def cross(ch, j):
        return copy(Xs.at[ch, j], Xr.at[ch, j], sib, slot=base_cross + 3 * ch + j)

    def put(ch, j, own, chunks, a, value):
        rows = slice(128 * chunks.start, 128 * chunks.stop)
        if own:
            value = value + Xr[ch, j, a, rows].astype(F32)
            shape = (chunks.stop - chunks.start, 4, 2, 16, D)
            R[ch, j, chunks, :, :, a] = value.reshape(shape).astype(BF16)
        else:
            Xs[ch, j, a, rows] = value.astype(BF16)

    def theirs(ch, work):
        def body(j):
            work(o, j, False)
            cross(ch, j).start()

        loop(body)

    def ours(ch, work):
        def body(j):
            cross(ch, j).wait()
            work(c, j, True)
            go(*rs_q1(ch, j))

        loop(body)

    base_q1 = slots(12)

    def rs_q1(ch, j):
        slot = base_q1 + 6 * ch + 2 * j
        return (
            copy(R.at[ch, j, q2, 0:2], RB1.at[ch, 0, j], right_q, slot=slot),
            copy(R.at[ch, j, q2, 2:4], RB1.at[ch, 1, j], left_q, slot=slot + 1),
        )

    def rs_q2(ch):
        copies = []
        for j in range(3):
            done(rs_q1(ch, j))
            one = R[ch, j, qn, 0:2].astype(F32) + RB1[ch, 0, j].astype(F32)
            R[ch, j, qn, 0:2] = one.astype(BF16)
            two = R[ch, j, qb, 2:4].astype(F32) + RB1[ch, 1, j].astype(F32)
            R[ch, j, qb, 2:4] = two.astype(BF16)
            copies += go(
                copy(R.at[ch, j, qn], RB2.at[ch, 0, j], right_q),
                copy(R.at[ch, j, qb], RB2.at[ch, 1, j], left_q),
            )
        return copies

    def rs_p(ch, copies):
        for j in range(3):
            done(copies[2 * j : 2 * j + 2])
            total = R[ch, j, q].astype(F32) + RB2[ch, 0, j].astype(F32) + RB2[ch, 1, j].astype(F32)
            S[ch, :, j] = total.astype(BF16)
        return go(
            *[copy(S.at[ch, (p + k + 1) % 4], RB3.at[ch, k], ring_p[k]) for k in range(3)]
        )

    def rs_z(ch, copies):
        done(copies)
        total = S[ch, p].astype(F32)
        for k in range(3):
            total = total + RB3[ch, k].astype(F32)
        low = total.astype(BF16)
        TZ[ch, 0] = low[:, 0]
        TZ[ch, 1] = low[:, 1]
        return go(copy(TZ.at[ch, 1 - zh], RB4.at[ch], opp))

    def rs_core(ch, copies):
        done(copies)
        total = TZ[ch, zh].astype(F32) + RB4[ch].astype(F32)
        for j in range(3):
            FS[ch, :, :, j * D : (j + 1) * D] = total[j]
        theirs_rows = pl.ds(pl.multiple_of(o * 8, 8), 8)
        rows = go(copy(FS.at[ch, :, theirs_rows], FR.at[ch], sib))
        total = jnp.sum(RA[1 - ch] * FS[ch, ch], axis=1, keepdims=True)
        HAs[ch] = jnp.broadcast_to(total, (16, D)).reshape(2, 8, D)
        HAr[ch, 2 * hd + c] = HAs[ch, c]
        mine, its = HAs.at[ch, c], HAs.at[ch, o]
        slot = HAr.at[ch, 2 * hd + c]
        rows += go(copy(its, slot, sib))
        rows += go(*[copy(mine, slot, to) for to in heads])
        rows += go(*[copy(its, slot, to) for to in heads_sib])
        return rows

    def rs_end(ch, copies, slots):
        done(copies)
        mine = pl.ds(pl.multiple_of(c * 8, 8), 8)
        for a, slot in enumerate(slots):
            sm[slot, :, half_of[0]] = FS[ch, a, mine]
            sm[slot, :, half_of[1]] = FR[ch, a]

    def video_pass(h, j, own):
        head = 3 * h + j
        lanes, jl = lanes_of(head), lanes_of(j)
        keys = G[h, 1, :, :, :, 1, :, jl].reshape(TOK, D)
        values = G[h, 0, :, :, :, 0, :, jl].reshape(TOK, D)
        tops = SV[0, head]
        weights = jnp.exp2(tops - jnp.max(tops, axis=0, keepdims=True))
        over = 1.0 / jnp.sum(weights * SV[1, head], axis=0, keepdims=True)
        weights = weights * over
        inner = jnp.sum(weights * SV[2, head], axis=0, keepdims=True)
        grad_k = grad_v = None
        for t in range(2):
            chunk = slice(256 * t, 256 * (t + 1))
            qs, dos = vqn[chunk, lanes], vdo[chunk, lanes]
            probs = jnp.concatenate(
                [EV[head, D * i : D * i + D, chunk] * weights[i : i + 1, chunk] for i in range(4)],
                axis=0,
            )
            low = probs.astype(BF16)
            ds = (probs * (DV[head, :, chunk] - inner[:, chunk])).astype(BF16)
            more_k, more_v = dot(ds, qs, NN), dot(low, dos, NN)
            grad_k = more_k if grad_k is None else grad_k + more_k
            grad_v = more_v if grad_v is None else grad_v + more_v
            video_out[chunk, lanes] = dot(low, values, TN).astype(BF16)
            grad_q = dot(ds, keys, TN) * FACTOR
            GQ[chunk, lanes] = grad_q
            IA[0, chunk] += vq[chunk, lanes].astype(F32) * gvq_gain[:, lanes] * grad_q
        put(0, j, own, slice(0, 4), 0, grad_k * FACTOR)
        put(0, j, own, slice(0, 4), 1, grad_v)

    def store(i, src, dst):
        one = pltpu.make_async_copy(src, dst, local.at[4 + i])
        one.start()
        return one

    def inner_start(i):
        HI[i, hd] = jnp.zeros((8, 512), F32)
        HI[i, hd, 0:1, :] = row_of(IA[i])
        return go(*[copy(HI.at[i, hd], HI.at[i, hd], to) for to in heads])

    def video_final(i, copies, raw, gain, grad, out):
        done(copies)
        inner = (HI[i, 0] + HI[i, 1] + HI[i, 2] + HI[i, 3]) / WIDTH
        inv_i = inv_col[i]
        scale = inv_i * inv_i * inv_i * col(inner[0:1, :])
        for b in range(NH):
            at_b = slice(b * D, (b + 1) * D)
            value = inv_i * gain[:, at_b] * grad[:, at_b] - raw[:, at_b].astype(F32) * scale
            out[:, at_b] = value.astype(BF16)

    theirs(0, video_pass)
    stats_merge(0, level0)
    level1 = stats_start(1, ring_p)
    ours(0, video_pass)
    stats_merge(1, level1)
    level2 = stats_start(2, ring_q)
    stores = [store(0, video_out, video_out_hbm)]
    inner0 = inner_start(0)
    a2 = rs_q2(0)
    stats_merge(2, level2)

    total = ST[3, 1]
    safe = jnp.where(total == 0.0, 1.0, total)
    WT[0] = jnp.exp2(ST[0, 0] - ST[3, 0]) / safe
    WT[1] = ST[3, 2] / safe

    def audio_probs(head, t):
        row = pl.ds(head, 1)
        weight, shift = (
            jnp.concatenate([WT[n, 2 * t, row, :], WT[n, 2 * t + 1, row, :]], axis=1)
            for n in (0, 1)
        )
        chunk = slice(256 * t, 256 * (t + 1))
        probs = E[head, :, chunk] * weight
        ds = (probs * (DP[head, :, chunk] - shift)).astype(BF16)
        return probs.astype(BF16), ds

    def audio_pass(h, j, own):
        head = 3 * h + j
        lanes = lanes_of(head)
        for t in range(2):
            low, ds = audio_probs(head, t)
            chunks = slice(2 * t, 2 * t + 2)
            put(1, j, own, chunks, 0, dot(low, vv[:, lanes], TN))
            put(1, j, own, chunks, 1, dot(ds, vkn[:, lanes], TN) * FACTOR)

    def row_pass(h, j):
        head = 3 * h + j
        lanes, jl = lanes_of(head), lanes_of(j)
        grad_k = grad_v = None
        for t in range(2):
            low, ds = audio_probs(head, t)
            chunks = slice(2 * t, 2 * t + 2)
            qs = G[h, 1, chunks, :, :, 0, :, jl].reshape(256, D)
            dos = G[h, 0, chunks, :, :, 1, :, jl].reshape(256, D)
            more_k, more_v = dot(ds, qs, NN), dot(low, dos, NN)
            grad_k = more_k if grad_k is None else grad_k + more_k
            grad_v = more_v if grad_v is None else grad_v + more_v
        grad_k = grad_k * FACTOR
        out_gvv[:, lanes] = grad_v.astype(BF16)
        GK[:, lanes] = grad_k
        IA[1] += vk[:, lanes].astype(F32) * gvk_gain[:, lanes] * grad_k

    theirs(1, audio_pass)
    ours(1, audio_pass)
    b2 = rs_q2(1)
    a3 = rs_p(0, a2)
    loop(lambda j: row_pass(0, j))
    b3 = rs_p(1, b2)
    a4 = rs_z(0, a3)
    loop(lambda j: row_pass(1, j))
    inner1 = inner_start(1)
    b4 = rs_z(1, b3)
    stores.append(store(1, out_gvv, gvv_hbm))
    a5 = rs_core(0, a4)
    video_final(0, inner0, vq, gvq_gain, GQ, out_gvq)
    stores.append(store(2, out_gvq, gvq_hbm))
    b5 = rs_core(1, b4)
    video_final(1, inner1, vk, gvk_gain, GK, out_gvk)
    stores.append(store(3, out_gvk, gvk_hbm))
    rs_end(0, a5, (3, 4))
    rs_end(1, b5, (5, 2))
    out_small[0] = sm[5]
    out_small[3] = sm[4]
    parts = ((aq, gaq_gain, sm[2]), (ak, gak_gain, sm[3]))
    for i, (raw, gain, grad) in enumerate(parts):
        total = HAr[1 - i, 0]
        for k in range(1, 8):
            total = total + HAr[1 - i, k]
        total = total / WIDTH
        wide = jnp.concatenate([inv_a[i]] * NH, axis=1)
        scale = jnp.concatenate([inv_a[i] * inv_a[i] * inv_a[i] * total] * NH, axis=1)
        out_small[1 + i] = wide * gain[...] * grad - raw[...].astype(F32) * scale
    for one in stores:
        one.wait()


def write_kernel(
    a, b, c, d, small, out_a, out_b, out_c, out_d, small_0, small_1, small_2, small_3, held, sems
):
    parts = ROWS // 2
    ins, outs = [], []
    for i, (src, dst) in enumerate(((a, out_a), (b, out_b), (c, out_c), (d, out_d))):
        for k in range(2):
            rows = slice(k * parts, (k + 1) * parts)
            n = 2 * i + k
            ins.append(pltpu.make_async_copy(src.at[rows], held.at[i, rows], sems.at[0, n]))
            outs.append(pltpu.make_async_copy(held.at[i, rows], dst.at[rows], sems.at[1, n]))
    for one in ins:
        one.start()
    for i, out in enumerate((small_0, small_1, small_2, small_3)):
        out[...] = small[i].astype(BF16)
    for one, two in zip(ins, outs):
        one.wait()
        two.start()
    for two in outs:
        two.wait()


def shards(*args):
    big = jax.ShapeDtypeStruct((ROWS, LOCAL), BF16)
    vmem = pltpu.VMEM
    wide = vmem((ROWS, LOCAL), BF16)
    scratch = [wide] * 8 + [
        vmem((8, LOCAL), F32),
        vmem((2, 16, HALF), F32),
        vmem((2, 2, 4, 4, 2, 2, 16, HALF), BF16),
        vmem((3, 2, 16, HALF), BF16),
        vmem((3, 3, 16, HALF), BF16),
        vmem((4, 2, 8, D), F32),
        vmem((4, 8, 512), F32),
        vmem((2, 4, 8, 512), F32),
        vmem((2, 2, 8, D), F32),
        vmem((2, 8, 8, D), F32),
        vmem((ROWS, LOCAL), BF16),
        vmem((ROWS, LOCAL), BF16),
        vmem((2, ROWS, D), F32),
        vmem((NH, ROWS, TOK), F32),
        vmem((NH, ROWS, TOK), F32),
        vmem((NH, TOK, ROWS), F32),
        vmem((NH, TOK, ROWS), F32),
        vmem((3, NH, 4, ROWS), F32),
        vmem((4, 3, 4, 8, D), F32),
        vmem((3, 3, 3, 4, 8, D), F32),
        vmem((2, 4, 8, D), F32),
        vmem((ROWS, LOCAL), F32),
        vmem((ROWS, LOCAL), F32),
        vmem((2, ROWS, D), F32),
        vmem((2, 3, 2, TOK, D), BF16),
        vmem((2, 3, 2, TOK, D), BF16),
        vmem((2, 3, 4, 4, 2, 2, 16, D), BF16),
        vmem((2, 2, 3, 2, 2, 2, 16, D), BF16),
        vmem((2, 2, 3, 4, 2, 2, 16, D), BF16),
        vmem((2, 4, 3, 2, 2, 16, D), BF16),
        vmem((2, 3, 3, 2, 2, 16, D), BF16),
        vmem((2, 2, 3, 2, 16, D), BF16),
        vmem((2, 3, 2, 16, D), BF16),
        vmem((2, 2, 16, HALF), F32),
        vmem((2, 2, 8, HALF), F32),
        vmem((6, 8, LOCAL), F32),
        pltpu.SemaphoreType.DMA((128,)),
        pltpu.SemaphoreType.DMA((128,)),
        pltpu.SemaphoreType.DMA((8,)),
    ]
    spec = pl.BlockSpec(memory_space=pltpu.VMEM)
    anywhere = pl.BlockSpec(memory_space=pl.ANY)
    made = pl.pallas_call(
        kernel,
        out_shape=(big, big, big, big, jax.ShapeDtypeStruct((4, 8, LOCAL), F32)),
        in_specs=[anywhere] * 4 + [spec] * 8,
        out_specs=(anywhere,) * 4 + (spec,),
        scratch_shapes=scratch,
        compiler_params=pltpu.CompilerParams(
            collective_id=0, has_side_effects=True, vmem_limit_bytes=60 * 1024 * 1024
        ),
    )(*args)
    small = jax.ShapeDtypeStruct((8, LOCAL), BF16)
    wrote = pl.pallas_call(
        write_kernel,
        out_shape=(big,) * 4 + (small,) * 4,
        in_specs=[anywhere] * 4 + [spec],
        out_specs=(anywhere,) * 4 + (spec,) * 4,
        scratch_shapes=[vmem((4, ROWS, LOCAL), BF16), pltpu.SemaphoreType.DMA((2, 8))],
    )(*made)
    video_out, gvq, gvk, gvv, audio_out, gaq, gak, gav = wrote
    return video_out, audio_out, gvq, gvk, gvv, gaq, gak, gav


def solution(mesh):
    both = P("seq", "head")
    return jax.shard_map(
        shards,
        mesh=mesh,
        in_specs=(both,) * 8 + (P("head"),) * 4,
        out_specs=(both,) * 8,
        check_vma=False,
    )
```

```python
import math

import jax
import jax.numpy as jnp
from jax import lax
from jax.experimental import pallas as pl
from jax.experimental.pallas import tpu as pltpu
from jax.sharding import PartitionSpec as P

HEADS = 24
D = 128
WIDTH = HEADS * D
EPS = 1e-06
FACTOR = 1.0 / math.sqrt(D)
KLOG = FACTOR * math.log2(math.e)
ROWS = 512
TOK = 512
LOCAL = 768
HALF = 384
NH = 6
F32 = jnp.float32
BF16 = jnp.bfloat16
MESH = pl.DeviceIdType.MESH
NT = (((1,), (1,)), ((), ()))
TN = (((0,), (0,)), ((), ()))
NN = (((1,), (0,)), ((), ()))


def dot(a, b, dims):
    return lax.dot_general(a, b, dims, preferred_element_type=F32)


def col(row):
    return jnp.transpose(jnp.broadcast_to(row, (D, ROWS)))


def row_of(square):
    return jnp.sum(jnp.transpose(square), axis=0, keepdims=True)


def fold(op, array):
    while array.shape[0] > 8:
        half = array.shape[0] // 2
        array = op(array[:half], array[half:])
    if op is jnp.maximum:
        return jnp.max(array, axis=0, keepdims=True)
    return jnp.sum(array, axis=0, keepdims=True)


def kernel(
    vq_in, vk_in, vv_in, vdo_in, aq, ak, av, ado, gain0, gain1, gain2, gain3,
    video_out_hbm, gvq_hbm, gvk_hbm, gvv_hbm, out_small,
    vq, vk, vv, vdo, video_out, out_gvq, out_gvk, out_gvv, GN, RA,
    G, PK, PR, HSA, HS, HI, HAs, HAr, vqn, vkn, vvT, vkT, inv_col, E, DP, EV, DV, SV, ST, SR, WT,
    GQ, GK, IA, Xs, Xr, R, RB1, RB2, S, RB3, TZ, RB4, FS, FR, sm,
    send, recv, local,
):
    s = lax.axis_index("seq")
    hd = lax.axis_index("head")
    c = s % 2
    y = (s // 2) % 4
    x = (s // 8) % 4
    zh = s // 32
    p = x + c * (y - x)
    q = y + c * (x - y)
    o = 1 - c

    def at(zz, pp, qq):
        xx = pp + c * (qq - pp)
        yy = qq + c * (pp - qq)
        return {"seq": ((zz * 4 + xx) * 4 + yy) * 2 + c}

    sib = {"seq": s + 1 - 2 * c}
    opp = at(1 - zh, p, q)
    opp_sib = {"seq": s + 1 - 2 * c + 32 - 64 * zh}
    ring_p = [at(zh, (p + k) % 4, q) for k in (1, 2, 3)]
    ring_q = [at(zh, p, (q + k) % 4) for k in (1, 2, 3)]
    heads = [{"head": (hd + k) % 4} for k in (1, 2, 3)]
    heads_sib = [{"seq": s + 1 - 2 * c, "head": (hd + k) % 4} for k in (1, 2, 3)]
    pn, pb, p2 = (p + 1) % 4, (p + 3) % 4, (p + 2) % 4
    qn, qb, q2 = (q + 1) % 4, (q + 3) % 4, (q + 2) % 4
    right_q, left_q = ring_q[0], ring_q[2]

    barrier = pltpu.get_barrier_semaphore()
    partners = [sib, opp, opp_sib] + ring_p + ring_q + heads + heads_sib
    for partner in partners:
        pl.semaphore_signal(barrier, inc=1, device_id=partner, device_id_type=MESH)
    loads = [
        pltpu.make_async_copy(src, dst, local.at[i])
        for i, (src, dst) in enumerate(((vq_in, vq), (vk_in, vk), (vv_in, vv), (vdo_in, vdo)))
    ]
    for one in loads:
        one.start()
    for i, gain in enumerate((gain0, gain1, gain2, gain3)):
        GN[i : i + 1, :] = gain[...].reshape(1, LOCAL)
    gvq_gain, gvk_gain, gaq_gain, gak_gain = (GN.at[i : i + 1] for i in range(4))

    count = [0]

    def slots(n):
        first = count[0]
        count[0] += n
        return first

    def copy(src, dst, to, slot=None):
        slot = slots(1) if slot is None else slot
        return pltpu.make_async_remote_copy(
            src_ref=src,
            dst_ref=dst,
            send_sem=send.at[slot],
            recv_sem=recv.at[slot],
            device_id=to,
            device_id_type=MESH,
        )

    def go(*copies):
        for one in copies:
            one.start()
        return copies

    def done(copies):
        for one in copies:
            one.wait()

    half_of = [pl.ds(pl.multiple_of(i * HALF, D), HALF) for i in (c, o)]

    def pack(n, refs):
        for i, half in enumerate(half_of):
            rows = [ref[:, half].astype(F32) for ref in refs]
            PK[n, i] = jnp.concatenate(rows, axis=0).astype(BF16)

    def ag_first(n):
        return go(
            copy(PK.at[n, 1], PR.at[n, 0], sib),
            copy(PK.at[n, 0], PR.at[n, 1], opp),
            copy(PK.at[n, 1], PR.at[n, 2], opp_sib),
        )

    def chip_rows(mine, other, a):
        mine = mine.astype(F32)[8 * a : 8 * a + 8]
        other = other.astype(F32)[8 * a : 8 * a + 8]
        low = jnp.where(c == 0, mine, other)
        high = jnp.where(c == 0, other, mine)
        return jnp.concatenate([low, high], axis=0)

    def ag_p(ch, copies):
        done(copies)
        for a in range(2):
            G[c, ch, q, p, zh, a] = chip_rows(PK[ch, 0], PR[ch, 0], a).astype(BF16)
            G[c, ch, q, p, 1 - zh, a] = chip_rows(PR[ch, 1], PR[ch, 2], a).astype(BF16)
        block = G.at[c, ch, q, p]
        return go(*[copy(block, block, to) for to in ring_p])

    def forward(ch, i):
        block = G.at[c, ch, i]
        return go(copy(block, block, sib))

    def ag_q1(ch, copies):
        done(copies)
        block = G.at[c, ch, q]
        return go(copy(block, block, right_q), copy(block, block, left_q))

    def ag_q2(ch, copies):
        done(copies)
        one, two = G.at[c, ch, qb, 0:2], G.at[c, ch, qn, 2:4]
        return go(copy(one, one, right_q), copy(two, two, left_q))

    pack(0, (av, ado))
    for i, raw in enumerate((aq, ak)):
        block = raw[...].astype(F32)
        total = jnp.sum(block * block, axis=1, keepdims=True)
        HSA[hd, i] = jnp.broadcast_to(total, (8, D))
    pl.semaphore_wait(barrier, len(partners))
    sums_a = go(*[copy(HSA.at[hd], HSA.at[hd], to) for to in heads])
    first0 = ag_first(0)
    pack(2, (aq, ak))
    raws = go(copy(PK.at[2, 1], PR.at[2, 0], sib))

    HS[hd] = jnp.zeros((8, 512), F32)

    def video_sum(i, raw):
        loads[i].wait()
        total = jnp.zeros((ROWS, D), F32)
        for b in range(NH):
            block = raw[:, b * D : (b + 1) * D].astype(F32)
            total = total + block * block
        HS[hd, i : i + 1, :] = row_of(total)

    video_sum(0, vq)
    done(sums_a)
    inv_a = []
    for i, (raw, gain) in enumerate(((aq, gaq_gain), (ak, gak_gain))):
        total = HSA[0, i] + HSA[1, i] + HSA[2, i] + HSA[3, i]
        inv_a.append(lax.rsqrt(total / WIDTH + EPS))
        wide = jnp.concatenate([inv_a[i]] * NH, axis=1)
        sm[i] = (raw[...].astype(F32) * wide * gain[...]).astype(BF16).astype(F32)
    pack(1, (sm.at[0], sm.at[1]))
    first1 = ag_first(1)
    ring0 = ag_p(0, first0)
    video_sum(1, vk)
    sums = go(*[copy(HS.at[hd], HS.at[hd], to) for to in heads])
    ring1 = ag_p(1, first1)
    q10 = ag_q1(0, ring0)
    f0 = [forward(0, q)]
    done(sums)
    total = HS[0] + HS[1] + HS[2] + HS[3]
    inv = lax.rsqrt(total / WIDTH + EPS)

    def norm_video(i, raw, gain, out):
        inv_col[i] = col(inv[i : i + 1, :])
        for b in range(NH):
            at_b = slice(b * D, (b + 1) * D)
            out[:, at_b] = (raw[:, at_b].astype(F32) * inv_col[i] * gain[:, at_b]).astype(BF16)

    norm_video(1, vk, gvk_gain, vkn)
    q11 = ag_q1(1, ring1)
    f1 = [forward(1, q)]
    norm_video(0, vq, gvq_gain, vqn)
    for b in range(NH):
        at_b = slice(b * D, (b + 1) * D)
        vkT[at_b, :] = jnp.transpose(vkn[:, at_b])

    def lanes_of(i):
        return pl.ds(pl.multiple_of(i * D, D), D)

    ST[...] = jnp.zeros_like(ST)

    def video_first(h, j, i):
        head = 3 * h + j
        lanes, jl, chunk = lanes_of(head), lanes_of(j), lanes_of(i)
        keys = G[h, 1, i, :, :, 1, :, jl].reshape(D, D)
        values = G[h, 0, i, :, :, 0, :, jl].reshape(D, D)
        scores = dot(keys, vqn[:, lanes], NT) * KLOG
        dprob = dot(values, vdo[:, lanes], NT)
        top = fold(jnp.maximum, scores)
        expo = jnp.exp2(scores - top)
        EV[head, chunk, :] = expo
        DV[head, chunk, :] = dprob
        row = pl.ds(i, 1)
        SV[0, head, row, :] = top
        SV[1, head, row, :] = fold(jnp.add, expo)
        SV[2, head, row, :] = fold(jnp.add, expo * dprob)

    def audio_first(h, j, i):
        head = 3 * h + j
        lanes, jl, chunk = lanes_of(head), lanes_of(j), lanes_of(i)
        qs = G[h, 1, i, :, :, 0, :, jl].reshape(D, D)
        dos = G[h, 0, i, :, :, 1, :, jl].reshape(D, D)
        scores = dot(vkn[:, lanes], qs, NT) * KLOG
        dprob = dot(vv[:, lanes], dos, NT)
        top = fold(jnp.maximum, scores)
        expo = jnp.exp2(scores - top)
        E[head, :, chunk] = expo
        DP[head, :, chunk] = dprob
        row = pl.ds(head, 1)
        ST[0, 0, i, row, :] = top
        ST[0, 1, i, row, :] = fold(jnp.add, expo)
        ST[0, 2, i, row, :] = fold(jnp.add, expo * dprob)

    def loop(body):
        def step(j, carry):
            body(j)
            return carry

        lax.fori_loop(0, 3, step, 0)

    def audio(h, *chunks):
        for i in chunks:
            loop(lambda j: audio_first(h, j, i))

    def video(h, *chunks):
        for i in chunks:
            loop(lambda j: video_first(h, j, i))

    loads[2].wait()
    for b in range(NH):
        at_b = slice(b * D, (b + 1) * D)
        vvT[at_b, :] = jnp.transpose(vv[:, at_b])
    audio(c, q)
    loads[3].wait()
    video(c, q)
    q20 = ag_q2(0, q10)
    f0 += [forward(0, qn), forward(0, qb)]
    q21 = ag_q2(1, q11)
    f1 += [forward(1, qn), forward(1, qb)]
    audio(c, qn, qb)
    video(c, qn)
    done(q20)
    f0.append(forward(0, q2))
    done(q21)
    f1.append(forward(1, q2))
    video(c, qb)
    audio(c, q2)
    for n, i in enumerate((p, pn, pb, p2)):
        done(f0[n] + f1[n])
        audio(o, i)

    def stats_start(level, to):
        return go(*[copy(ST.at[level], SR.at[level, k], one) for k, one in enumerate(to)])

    def stats_merge(level, copies):
        done(copies)
        tops = [ST[level, 0]] + [SR[level, k, 0] for k in range(3)]
        top = jnp.maximum(jnp.maximum(tops[0], tops[1]), jnp.maximum(tops[2], tops[3]))
        weights = [jnp.exp2(one - top) for one in tops]
        ST[level + 1, 0] = top
        for n in (1, 2):
            total = ST[level, n] * weights[0]
            for k in range(3):
                total = total + SR[level, k, n] * weights[k + 1]
            ST[level + 1, n] = total

    level0 = stats_start(0, (sib, opp, opp_sib))
    video(c, q2)
    video(o, p, pn, pb, p2)
    done(raws)
    for i, gain in enumerate((gaq_gain, gak_gain)):
        RA[i] = chip_rows(PK[2, 0], PR[2, 0], i) * gain[:, half_of[0]]

    IA[...] = jnp.zeros_like(IA)
    base_cross = slots(6)

    def cross(ch, j):
        return copy(Xs.at[ch, j], Xr.at[ch, j], sib, slot=base_cross + 3 * ch + j)

    def put(ch, j, own, chunks, a, value):
        rows = slice(128 * chunks.start, 128 * chunks.stop)
        if own:
            value = value + Xr[ch, j, a, rows].astype(F32)
            shape = (chunks.stop - chunks.start, 4, 2, 16, D)
            R[ch, j, chunks, :, :, a] = value.reshape(shape).astype(BF16)
        else:
            Xs[ch, j, a, rows] = value.astype(BF16)

    def theirs(ch, work):
        def body(j):
            work(o, j, False)
            cross(ch, j).start()

        loop(body)

    def ours(ch, work):
        def body(j):
            cross(ch, j).wait()
            work(c, j, True)
            go(*rs_q1(ch, j))

        loop(body)

    base_q1 = slots(12)

    def rs_q1(ch, j):
        slot = base_q1 + 6 * ch + 2 * j
        return (
            copy(R.at[ch, j, q2, 0:2], RB1.at[ch, 0, j], right_q, slot=slot),
            copy(R.at[ch, j, q2, 2:4], RB1.at[ch, 1, j], left_q, slot=slot + 1),
        )

    def rs_q2(ch):
        copies = []
        for j in range(3):
            done(rs_q1(ch, j))
            one = R[ch, j, qn, 0:2].astype(F32) + RB1[ch, 0, j].astype(F32)
            R[ch, j, qn, 0:2] = one.astype(BF16)
            two = R[ch, j, qb, 2:4].astype(F32) + RB1[ch, 1, j].astype(F32)
            R[ch, j, qb, 2:4] = two.astype(BF16)
            copies += go(
                copy(R.at[ch, j, qn], RB2.at[ch, 0, j], right_q),
                copy(R.at[ch, j, qb], RB2.at[ch, 1, j], left_q),
            )
        return copies

    def rs_p(ch, copies):
        for j in range(3):
            done(copies[2 * j : 2 * j + 2])
            total = R[ch, j, q].astype(F32) + RB2[ch, 0, j].astype(F32) + RB2[ch, 1, j].astype(F32)
            S[ch, :, j] = total.astype(BF16)
        return go(
            *[copy(S.at[ch, (p + k + 1) % 4], RB3.at[ch, k], ring_p[k]) for k in range(3)]
        )

    def rs_z(ch, copies):
        done(copies)
        total = S[ch, p].astype(F32)
        for k in range(3):
            total = total + RB3[ch, k].astype(F32)
        low = total.astype(BF16)
        TZ[ch, 0] = low[:, 0]
        TZ[ch, 1] = low[:, 1]
        return go(copy(TZ.at[ch, 1 - zh], RB4.at[ch], opp))

    def rs_core(ch, copies):
        done(copies)
        total = TZ[ch, zh].astype(F32) + RB4[ch].astype(F32)
        for j in range(3):
            FS[ch, :, :, j * D : (j + 1) * D] = total[j]
        theirs_rows = pl.ds(pl.multiple_of(o * 8, 8), 8)
        rows = go(copy(FS.at[ch, :, theirs_rows], FR.at[ch], sib))
        total = jnp.sum(RA[1 - ch] * FS[ch, ch], axis=1, keepdims=True)
        HAs[ch] = jnp.broadcast_to(total, (16, D)).reshape(2, 8, D)
        HAr[ch, 2 * hd + c] = HAs[ch, c]
        mine, its = HAs.at[ch, c], HAs.at[ch, o]
        slot = HAr.at[ch, 2 * hd + c]
        rows += go(copy(its, slot, sib))
        rows += go(*[copy(mine, slot, to) for to in heads])
        rows += go(*[copy(its, slot, to) for to in heads_sib])
        return rows

    def rs_end(ch, copies, slots):
        done(copies)
        mine = pl.ds(pl.multiple_of(c * 8, 8), 8)
        for a, slot in enumerate(slots):
            sm[slot, :, half_of[0]] = FS[ch, a, mine]
            sm[slot, :, half_of[1]] = FR[ch, a]

    def video_probs(head):
        tops = SV[0, head]
        weights = jnp.exp2(tops - jnp.max(tops, axis=0, keepdims=True))
        over = 1.0 / jnp.sum(weights * SV[1, head], axis=0, keepdims=True)
        weights = weights * over
        inner = jnp.sum(weights * SV[2, head], axis=0, keepdims=True)
        for t in range(2):
            chunk = slice(256 * t, 256 * (t + 1))
            probs = jnp.concatenate(
                [EV[head, D * i : D * i + D, chunk] * weights[i : i + 1, chunk] for i in range(4)],
                axis=0,
            )
            ds = (probs * (DV[head, :, chunk] - inner[:, chunk])).astype(BF16)
            yield chunk, probs.astype(BF16), ds

    def video_pass(h, j, own):
        head = 3 * h + j
        lanes = lanes_of(head)
        grad_k = grad_v = None
        for chunk, low, ds in video_probs(head):
            more_k, more_v = dot(ds, vqn[chunk, lanes], NN), dot(low, vdo[chunk, lanes], NN)
            grad_k = more_k if grad_k is None else grad_k + more_k
            grad_v = more_v if grad_v is None else grad_v + more_v
        put(0, j, own, slice(0, 4), 0, grad_k * FACTOR)
        put(0, j, own, slice(0, 4), 1, grad_v)

    def video_rows(h, j):
        head = 3 * h + j
        lanes, jl = lanes_of(head), lanes_of(j)
        keys = jnp.transpose(G[h, 1, :, :, :, 1, :, jl].reshape(TOK, D))
        values = jnp.transpose(G[h, 0, :, :, :, 0, :, jl].reshape(TOK, D))
        for chunk, low, ds in video_probs(head):
            video_out[chunk, lanes] = jnp.transpose(dot(values, low, NN)).astype(BF16)
            grad_q = jnp.transpose(dot(keys, ds, NN)) * FACTOR
            GQ[chunk, lanes] = grad_q
            IA[0, chunk] += vq[chunk, lanes].astype(F32) * gvq_gain[:, lanes] * grad_q

    def store(i, src, dst):
        one = pltpu.make_async_copy(src, dst, local.at[4 + i])
        one.start()
        return one

    def inner_start(i):
        HI[i, hd] = jnp.zeros((8, 512), F32)
        HI[i, hd, 0:1, :] = row_of(IA[i])
        return go(*[copy(HI.at[i, hd], HI.at[i, hd], to) for to in heads])

    def video_final(i, copies, raw, gain, grad, out):
        done(copies)
        inner = (HI[i, 0] + HI[i, 1] + HI[i, 2] + HI[i, 3]) / WIDTH
        inv_i = inv_col[i]
        scale = inv_i * inv_i * inv_i * col(inner[0:1, :])
        for b in range(NH):
            at_b = slice(b * D, (b + 1) * D)
            value = inv_i * gain[:, at_b] * grad[:, at_b] - raw[:, at_b].astype(F32) * scale
            out[:, at_b] = value.astype(BF16)

    theirs(0, video_pass)
    stats_merge(0, level0)
    level1 = stats_start(1, ring_p)
    ours(0, video_pass)
    stats_merge(1, level1)
    level2 = stats_start(2, ring_q)
    a2 = rs_q2(0)
    stats_merge(2, level2)

    total = ST[3, 1]
    safe = jnp.where(total == 0.0, 1.0, total)
    WT[0] = jnp.exp2(ST[0, 0] - ST[3, 0]) / safe
    WT[1] = ST[3, 2] / safe

    def audio_probs(head, t):
        row = pl.ds(head, 1)
        weight, shift = (
            jnp.concatenate([WT[n, 2 * t, row, :], WT[n, 2 * t + 1, row, :]], axis=1)
            for n in (0, 1)
        )
        chunk = slice(256 * t, 256 * (t + 1))
        probs = E[head, :, chunk] * weight
        ds = (probs * (DP[head, :, chunk] - shift)).astype(BF16)
        return probs.astype(BF16), ds

    def audio_pass(h, j, own):
        head = 3 * h + j
        lanes = lanes_of(head)
        for t in range(2):
            low, ds = audio_probs(head, t)
            chunks = slice(2 * t, 2 * t + 2)
            put(1, j, own, chunks, 0, jnp.transpose(dot(vvT[lanes, :], low, NN)))
            put(1, j, own, chunks, 1, jnp.transpose(dot(vkT[lanes, :], ds, NN)) * FACTOR)

    def row_pass(h, j):
        head = 3 * h + j
        lanes, jl = lanes_of(head), lanes_of(j)
        grad_k = grad_v = None
        for t in range(2):
            low, ds = audio_probs(head, t)
            chunks = slice(2 * t, 2 * t + 2)
            qs = G[h, 1, chunks, :, :, 0, :, jl].reshape(256, D)
            dos = G[h, 0, chunks, :, :, 1, :, jl].reshape(256, D)
            more_k, more_v = dot(ds, qs, NN), dot(low, dos, NN)
            grad_k = more_k if grad_k is None else grad_k + more_k
            grad_v = more_v if grad_v is None else grad_v + more_v
        grad_k = grad_k * FACTOR
        out_gvv[:, lanes] = grad_v.astype(BF16)
        GK[:, lanes] = grad_k
        IA[1] += vk[:, lanes].astype(F32) * gvk_gain[:, lanes] * grad_k

    theirs(1, audio_pass)
    ours(1, audio_pass)
    b2 = rs_q2(1)
    a3 = rs_p(0, a2)
    loop(lambda j: video_rows(0, j))
    b3 = rs_p(1, b2)
    a4 = rs_z(0, a3)
    loop(lambda j: video_rows(1, j))
    inner0 = inner_start(0)
    stores = [store(0, video_out, video_out_hbm)]
    b4 = rs_z(1, b3)
    a5 = rs_core(0, a4)
    loop(lambda j: row_pass(0, j))
    loop(lambda j: row_pass(1, j))
    inner1 = inner_start(1)
    stores.append(store(1, out_gvv, gvv_hbm))
    b5 = rs_core(1, b4)
    video_final(0, inner0, vq, gvq_gain, GQ, out_gvq)
    stores.append(store(2, out_gvq, gvq_hbm))
    video_final(1, inner1, vk, gvk_gain, GK, out_gvk)
    stores.append(store(3, out_gvk, gvk_hbm))
    rs_end(0, a5, (3, 4))
    rs_end(1, b5, (5, 2))
    out_small[0] = sm[5]
    out_small[3] = sm[4]
    parts = ((aq, gaq_gain, sm[2]), (ak, gak_gain, sm[3]))
    for i, (raw, gain, grad) in enumerate(parts):
        total = HAr[1 - i, 0]
        for k in range(1, 8):
            total = total + HAr[1 - i, k]
        total = total / WIDTH
        wide = jnp.concatenate([inv_a[i]] * NH, axis=1)
        scale = jnp.concatenate([inv_a[i] * inv_a[i] * inv_a[i] * total] * NH, axis=1)
        out_small[1 + i] = wide * gain[...] * grad - raw[...].astype(F32) * scale
    for one in stores:
        one.wait()


def write_kernel(
    a, b, c, d, small, out_a, out_b, out_c, out_d, small_0, small_1, small_2, small_3, held, sems
):
    parts = ROWS // 4
    ins, outs = [], []
    for i, (src, dst) in enumerate(((a, out_a), (b, out_b), (c, out_c), (d, out_d))):
        for k in range(4):
            rows = slice(k * parts, (k + 1) * parts)
            n = 4 * i + k
            ins.append(pltpu.make_async_copy(src.at[rows], held.at[i, rows], sems.at[0, n]))
            outs.append(pltpu.make_async_copy(held.at[i, rows], dst.at[rows], sems.at[1, n]))
    for one in ins:
        one.start()
    for i, out in enumerate((small_0, small_1, small_2, small_3)):
        out[...] = small[i].astype(BF16)
    for one, two in zip(ins, outs):
        one.wait()
        two.start()
    for two in outs:
        two.wait()


def shards(*args):
    big = jax.ShapeDtypeStruct((ROWS, LOCAL), BF16)
    vmem = pltpu.VMEM
    wide = vmem((ROWS, LOCAL), BF16)
    scratch = [wide] * 8 + [
        vmem((8, LOCAL), F32),
        vmem((2, 16, HALF), F32),
        vmem((2, 2, 4, 4, 2, 2, 16, HALF), BF16),
        vmem((3, 2, 16, HALF), BF16),
        vmem((3, 3, 16, HALF), BF16),
        vmem((4, 2, 8, D), F32),
        vmem((4, 8, 512), F32),
        vmem((2, 4, 8, 512), F32),
        vmem((2, 2, 8, D), F32),
        vmem((2, 8, 8, D), F32),
        vmem((ROWS, LOCAL), BF16),
        vmem((ROWS, LOCAL), BF16),
        vmem((LOCAL, ROWS), BF16),
        vmem((LOCAL, ROWS), BF16),
        vmem((2, ROWS, D), F32),
        vmem((NH, ROWS, TOK), F32),
        vmem((NH, ROWS, TOK), F32),
        vmem((NH, TOK, ROWS), F32),
        vmem((NH, TOK, ROWS), F32),
        vmem((3, NH, 4, ROWS), F32),
        vmem((4, 3, 4, 8, D), F32),
        vmem((3, 3, 3, 4, 8, D), F32),
        vmem((2, 4, 8, D), F32),
        vmem((ROWS, LOCAL), F32),
        vmem((ROWS, LOCAL), F32),
        vmem((2, ROWS, D), F32),
        vmem((2, 3, 2, TOK, D), BF16),
        vmem((2, 3, 2, TOK, D), BF16),
        vmem((2, 3, 4, 4, 2, 2, 16, D), BF16),
        vmem((2, 2, 3, 2, 2, 2, 16, D), BF16),
        vmem((2, 2, 3, 4, 2, 2, 16, D), BF16),
        vmem((2, 4, 3, 2, 2, 16, D), BF16),
        vmem((2, 3, 3, 2, 2, 16, D), BF16),
        vmem((2, 2, 3, 2, 16, D), BF16),
        vmem((2, 3, 2, 16, D), BF16),
        vmem((2, 2, 16, HALF), F32),
        vmem((2, 2, 8, HALF), F32),
        vmem((6, 8, LOCAL), F32),
        pltpu.SemaphoreType.DMA((128,)),
        pltpu.SemaphoreType.DMA((128,)),
        pltpu.SemaphoreType.DMA((8,)),
    ]
    spec = pl.BlockSpec(memory_space=pltpu.VMEM)
    anywhere = pl.BlockSpec(memory_space=pl.ANY)
    made = pl.pallas_call(
        kernel,
        out_shape=(big, big, big, big, jax.ShapeDtypeStruct((4, 8, LOCAL), F32)),
        in_specs=[anywhere] * 4 + [spec] * 8,
        out_specs=(anywhere,) * 4 + (spec,),
        scratch_shapes=scratch,
        compiler_params=pltpu.CompilerParams(
            collective_id=0, has_side_effects=True, vmem_limit_bytes=60 * 1024 * 1024
        ),
    )(*args)
    small = jax.ShapeDtypeStruct((8, LOCAL), BF16)
    wrote = pl.pallas_call(
        write_kernel,
        out_shape=(big,) * 4 + (small,) * 4,
        in_specs=[anywhere] * 4 + [spec],
        out_specs=(anywhere,) * 4 + (spec,) * 4,
        scratch_shapes=[vmem((4, ROWS, LOCAL), BF16), pltpu.SemaphoreType.DMA((2, 16))],
    )(*made)
    video_out, gvq, gvk, gvv, audio_out, gaq, gak, gav = wrote
    return video_out, audio_out, gvq, gvk, gvv, gaq, gak, gav


def solution(mesh):
    both = P("seq", "head")
    return jax.shard_map(
        shards,
        mesh=mesh,
        in_specs=(both,) * 8 + (P("head"),) * 4,
        out_specs=(both,) * 8,
        check_vma=False,
    )
```

```python
import math

import jax
import jax.numpy as jnp
from jax import lax
from jax.experimental import pallas as pl
from jax.experimental.pallas import tpu as pltpu
from jax.sharding import PartitionSpec as P

HEADS = 24
D = 128
WIDTH = HEADS * D
EPS = 1e-06
FACTOR = 1.0 / math.sqrt(D)
KLOG = FACTOR * math.log2(math.e)
ROWS = 512
TOK = 512
LOCAL = 768
HALF = 384
NH = 6
F32 = jnp.float32
BF16 = jnp.bfloat16
MESH = pl.DeviceIdType.MESH
NT = (((1,), (1,)), ((), ()))
TN = (((0,), (0,)), ((), ()))
NN = (((1,), (0,)), ((), ()))


def dot(a, b, dims):
    return lax.dot_general(a, b, dims, preferred_element_type=F32)


def col(row):
    return jnp.transpose(jnp.broadcast_to(row, (D, ROWS)))


def row_of(square):
    return jnp.sum(jnp.transpose(square), axis=0, keepdims=True)


def fold(op, array):
    while array.shape[0] > 8:
        half = array.shape[0] // 2
        array = op(array[:half], array[half:])
    if op is jnp.maximum:
        return jnp.max(array, axis=0, keepdims=True)
    return jnp.sum(array, axis=0, keepdims=True)


def kernel(
    vq_in, vk_in, vv_in, vdo_in, aq, ak, av, ado, gain0, gain1, gain2, gain3,
    video_out_hbm, gvq_hbm, gvk_hbm, gvv_hbm, out_small,
    vq, vk, vv, vdo, video_out, out_gvq, out_gvk, out_gvv, GN, RA,
    G, PK, PR, HSA, HS, HI, HAs, HAr, vqn, vkn, vvT, vkT, inv_col, E, DP, EV, DV, SV, ST, SR, WT,
    GQ, GK, IA, Xs, Xr, R, RB1, RB2, S, RB3, TZ, RB4, FS, FR, sm,
    send, recv, local,
):
    s = lax.axis_index("seq")
    hd = lax.axis_index("head")
    c = s % 2
    y = (s // 2) % 4
    x = (s // 8) % 4
    zh = s // 32
    p = x + c * (y - x)
    q = y + c * (x - y)
    o = 1 - c

    def at(zz, pp, qq):
        xx = pp + c * (qq - pp)
        yy = qq + c * (pp - qq)
        return {"seq": ((zz * 4 + xx) * 4 + yy) * 2 + c}

    sib = {"seq": s + 1 - 2 * c}
    opp = at(1 - zh, p, q)
    opp_sib = {"seq": s + 1 - 2 * c + 32 - 64 * zh}
    ring_p = [at(zh, (p + k) % 4, q) for k in (1, 2, 3)]
    ring_q = [at(zh, p, (q + k) % 4) for k in (1, 2, 3)]
    heads = [{"head": (hd + k) % 4} for k in (1, 2, 3)]
    heads_sib = [{"seq": s + 1 - 2 * c, "head": (hd + k) % 4} for k in (1, 2, 3)]
    pn, pb, p2 = (p + 1) % 4, (p + 3) % 4, (p + 2) % 4
    qn, qb, q2 = (q + 1) % 4, (q + 3) % 4, (q + 2) % 4
    right_q, left_q = ring_q[0], ring_q[2]

    barrier = pltpu.get_barrier_semaphore()
    partners = [sib, opp, opp_sib] + ring_p + ring_q + heads + heads_sib
    for partner in partners:
        pl.semaphore_signal(barrier, inc=1, device_id=partner, device_id_type=MESH)
    loads = [
        pltpu.make_async_copy(src, dst, local.at[i])
        for i, (src, dst) in enumerate(((vq_in, vq), (vk_in, vk), (vv_in, vv), (vdo_in, vdo)))
    ]
    for one in loads:
        one.start()
    for i, gain in enumerate((gain0, gain1, gain2, gain3)):
        GN[i : i + 1, :] = gain[...].reshape(1, LOCAL)
    gvq_gain, gvk_gain, gaq_gain, gak_gain = (GN.at[i : i + 1] for i in range(4))

    count = [0]

    def slots(n):
        first = count[0]
        count[0] += n
        return first

    def copy(src, dst, to, slot=None):
        slot = slots(1) if slot is None else slot
        return pltpu.make_async_remote_copy(
            src_ref=src,
            dst_ref=dst,
            send_sem=send.at[slot],
            recv_sem=recv.at[slot],
            device_id=to,
            device_id_type=MESH,
        )

    def go(*copies):
        for one in copies:
            one.start()
        return copies

    def done(copies):
        for one in copies:
            one.wait()

    half_of = [pl.ds(pl.multiple_of(i * HALF, D), HALF) for i in (c, o)]

    def pack(n, refs):
        for i, half in enumerate(half_of):
            rows = [ref[:, half].astype(F32) for ref in refs]
            PK[n, i] = jnp.concatenate(rows, axis=0).astype(BF16)

    def ag_first(n):
        return go(
            copy(PK.at[n, 1], PR.at[n, 0], sib),
            copy(PK.at[n, 0], PR.at[n, 1], opp),
            copy(PK.at[n, 1], PR.at[n, 2], opp_sib),
        )

    def chip_rows(mine, other, a):
        mine = mine.astype(F32)[8 * a : 8 * a + 8]
        other = other.astype(F32)[8 * a : 8 * a + 8]
        low = jnp.where(c == 0, mine, other)
        high = jnp.where(c == 0, other, mine)
        return jnp.concatenate([low, high], axis=0)

    def ag_p(ch, copies):
        done(copies)
        for a in range(2):
            G[c, ch, q, p, zh, a] = chip_rows(PK[ch, 0], PR[ch, 0], a).astype(BF16)
            G[c, ch, q, p, 1 - zh, a] = chip_rows(PR[ch, 1], PR[ch, 2], a).astype(BF16)
        block = G.at[c, ch, q, p]
        return go(*[copy(block, block, to) for to in ring_p])

    base_f = slots(8)

    def forward(ch, n):
        i = (q + n + (n // 2) * (5 - 2 * n)) % 4
        block = G.at[c, ch, i]
        return copy(block, block, sib, slot=base_f + 4 * ch + n)

    def ag_q1(ch, copies):
        done(copies)
        block = G.at[c, ch, q]
        return go(copy(block, block, right_q), copy(block, block, left_q))

    def ag_q2(ch, copies):
        done(copies)
        one, two = G.at[c, ch, qb, 0:2], G.at[c, ch, qn, 2:4]
        return go(copy(one, one, right_q), copy(two, two, left_q))

    pack(0, (av, ado))
    for i, raw in enumerate((aq, ak)):
        block = raw[...].astype(F32)
        total = jnp.sum(block * block, axis=1, keepdims=True)
        HSA[hd, i] = jnp.broadcast_to(total, (8, D))
    pl.semaphore_wait(barrier, len(partners))
    sums_a = go(*[copy(HSA.at[hd], HSA.at[hd], to) for to in heads])
    first0 = ag_first(0)
    pack(2, (aq, ak))
    raws = go(copy(PK.at[2, 1], PR.at[2, 0], sib))

    HS[hd] = jnp.zeros((8, 512), F32)

    def video_sum(i, raw):
        loads[i].wait()
        total = jnp.zeros((ROWS, D), F32)
        for b in range(NH):
            block = raw[:, b * D : (b + 1) * D].astype(F32)
            total = total + block * block
        HS[hd, i : i + 1, :] = row_of(total)

    video_sum(0, vq)
    done(sums_a)
    inv_a = []
    for i, (raw, gain) in enumerate(((aq, gaq_gain), (ak, gak_gain))):
        total = HSA[0, i] + HSA[1, i] + HSA[2, i] + HSA[3, i]
        inv_a.append(lax.rsqrt(total / WIDTH + EPS))
        wide = jnp.concatenate([inv_a[i]] * NH, axis=1)
        sm[i] = (raw[...].astype(F32) * wide * gain[...]).astype(BF16).astype(F32)
    pack(1, (sm.at[0], sm.at[1]))
    first1 = ag_first(1)
    ring0 = ag_p(0, first0)
    video_sum(1, vk)
    sums = go(*[copy(HS.at[hd], HS.at[hd], to) for to in heads])
    ring1 = ag_p(1, first1)
    q10 = ag_q1(0, ring0)
    go(forward(0, 0))
    done(sums)
    total = HS[0] + HS[1] + HS[2] + HS[3]
    inv = lax.rsqrt(total / WIDTH + EPS)

    def norm_video(i, raw, gain, out):
        inv_col[i] = col(inv[i : i + 1, :])
        for b in range(NH):
            at_b = slice(b * D, (b + 1) * D)
            out[:, at_b] = (raw[:, at_b].astype(F32) * inv_col[i] * gain[:, at_b]).astype(BF16)

    norm_video(1, vk, gvk_gain, vkn)
    q11 = ag_q1(1, ring1)
    go(forward(1, 0))
    norm_video(0, vq, gvq_gain, vqn)
    for b in range(NH):
        at_b = slice(b * D, (b + 1) * D)
        vkT[at_b, :] = jnp.transpose(vkn[:, at_b])

    def lanes_of(i):
        return pl.ds(pl.multiple_of(i * D, D), D)

    ST[...] = jnp.zeros_like(ST)

    def staged(units, make, use):
        held = None
        for unit in units:
            made = make(unit)
            if held is not None:
                use(*held)
            held = (unit, made)
        use(*held)

    def rows_of(ch, h, i, a, j):
        return G[h, ch, i, :, :, a, :, j * D : j * D + D].reshape(D, D)

    def some_rows(ch, h, ids, a, j):
        return jnp.concatenate([rows_of(ch, h, i, a, j) for i in ids], axis=0)

    def video(h, *ids):
        def make(j):
            lanes = lanes_of(3 * h + j)
            scores = dot(some_rows(1, h, ids, 1, j), vqn[:, lanes], NT) * KLOG
            return scores, dot(some_rows(0, h, ids, 0, j), vdo[:, lanes], NT)

        def use(j, made):
            scores, dprob = made
            head = 3 * h + j
            top = fold(jnp.maximum, scores)
            expo = jnp.exp2(scores - top)
            nothing = jnp.zeros_like(top)
            values = [top, fold(jnp.add, expo), fold(jnp.add, expo * dprob)]
            for n, i in enumerate(ids):
                part = slice(D * n, D * n + D)
                EV[head, lanes_of(i), :] = expo[part]
                DV[head, lanes_of(i), :] = dprob[part]
                for k in range(3):
                    SV[k, head, pl.ds(i, 1), :] = nothing if n and k else values[k]

        staged(range(3), make, use)

    def audio(h, *ids):
        def make(j):
            lanes = lanes_of(3 * h + j)
            scores = dot(vkn[:, lanes], some_rows(1, h, ids, 0, j), NT) * KLOG
            return scores, dot(vv[:, lanes], some_rows(0, h, ids, 1, j), NT)

        def use(j, made):
            scores, dprob = made
            head = 3 * h + j
            top = fold(jnp.maximum, scores)
            expo = jnp.exp2(scores - top)
            values = [top, fold(jnp.add, expo), fold(jnp.add, expo * dprob)]
            for n, i in enumerate(ids):
                part = slice(D * n, D * n + D)
                E[head, :, lanes_of(i)] = expo[:, part]
                DP[head, :, lanes_of(i)] = dprob[:, part]
                for k in range(3):
                    ST[0, k, i, pl.ds(head, 1), :] = values[k][:, part]

        staged(range(3), make, use)

    def pair(n):
        return (p + 3 * n) % 4, (p + 1 + n) % 4

    def twice(body):
        def step(n, carry):
            body(n)
            return carry

        lax.fori_loop(0, 2, step, 0)

    loads[2].wait()
    for b in range(NH):
        at_b = slice(b * D, (b + 1) * D)
        vvT[at_b, :] = jnp.transpose(vv[:, at_b])
    audio(c, q)
    loads[3].wait()
    video(c, q)
    q20 = ag_q2(0, q10)
    go(*[forward(0, n) for n in (1, 2)])
    q21 = ag_q2(1, q11)
    go(*[forward(1, n) for n in (1, 2)])
    audio(c, qn, qb)
    done(q20)
    go(forward(0, 3))
    done(q21)
    go(forward(1, 3))
    video(c, qn, qb)
    audio(c, q2)

    def their_audio(n):
        done([forward(ch, 2 * n + k) for ch in range(2) for k in range(2)])
        audio(o, *pair(n))

    twice(their_audio)

    def stats_start(level, to):
        return go(*[copy(ST.at[level], SR.at[level, k], one) for k, one in enumerate(to)])

    def stats_merge(level, copies):
        done(copies)
        tops = [ST[level, 0]] + [SR[level, k, 0] for k in range(3)]
        top = jnp.maximum(jnp.maximum(tops[0], tops[1]), jnp.maximum(tops[2], tops[3]))
        weights = [jnp.exp2(one - top) for one in tops]
        ST[level + 1, 0] = top
        for n in (1, 2):
            total = ST[level, n] * weights[0]
            for k in range(3):
                total = total + SR[level, k, n] * weights[k + 1]
            ST[level + 1, n] = total

    level0 = stats_start(0, (sib, opp, opp_sib))
    video(c, q2)
    twice(lambda n: video(o, *pair(n)))
    done(raws)
    for i, gain in enumerate((gaq_gain, gak_gain)):
        RA[i] = chip_rows(PK[2, 0], PR[2, 0], i) * gain[:, half_of[0]]

    IA[...] = jnp.zeros_like(IA)
    base_cross = slots(6)

    def cross(ch, j):
        return copy(Xs.at[ch, j], Xr.at[ch, j], sib, slot=base_cross + 3 * ch + j)

    def put(ch, j, own, chunks, a, value):
        rows = slice(128 * chunks.start, 128 * chunks.stop)
        if own:
            value = value + Xr[ch, j, a, rows].astype(F32)
            shape = (chunks.stop - chunks.start, 4, 2, 16, D)
            R[ch, j, chunks, :, :, a] = value.reshape(shape).astype(BF16)
        else:
            Xs[ch, j, a, rows] = value.astype(BF16)

    base_q1 = slots(12)

    def rs_q1(ch, j):
        slot = base_q1 + 6 * ch + 2 * j
        return (
            copy(R.at[ch, j, q2, 0:2], RB1.at[ch, 0, j], right_q, slot=slot),
            copy(R.at[ch, j, q2, 2:4], RB1.at[ch, 1, j], left_q, slot=slot + 1),
        )

    def rs_q2(ch):
        copies = []
        for j in range(3):
            done(rs_q1(ch, j))
            one = R[ch, j, qn, 0:2].astype(F32) + RB1[ch, 0, j].astype(F32)
            R[ch, j, qn, 0:2] = one.astype(BF16)
            two = R[ch, j, qb, 2:4].astype(F32) + RB1[ch, 1, j].astype(F32)
            R[ch, j, qb, 2:4] = two.astype(BF16)
            copies += go(
                copy(R.at[ch, j, qn], RB2.at[ch, 0, j], right_q),
                copy(R.at[ch, j, qb], RB2.at[ch, 1, j], left_q),
            )
        return copies

    def rs_p(ch, copies):
        for j in range(3):
            done(copies[2 * j : 2 * j + 2])
            total = R[ch, j, q].astype(F32) + RB2[ch, 0, j].astype(F32) + RB2[ch, 1, j].astype(F32)
            S[ch, :, j] = total.astype(BF16)
        return go(
            *[copy(S.at[ch, (p + k + 1) % 4], RB3.at[ch, k], ring_p[k]) for k in range(3)]
        )

    def rs_z(ch, copies):
        done(copies)
        total = S[ch, p].astype(F32)
        for k in range(3):
            total = total + RB3[ch, k].astype(F32)
        low = total.astype(BF16)
        TZ[ch, 0] = low[:, 0]
        TZ[ch, 1] = low[:, 1]
        return go(copy(TZ.at[ch, 1 - zh], RB4.at[ch], opp))

    def rs_core(ch, copies):
        done(copies)
        total = TZ[ch, zh].astype(F32) + RB4[ch].astype(F32)
        for j in range(3):
            FS[ch, :, :, j * D : (j + 1) * D] = total[j]
        theirs_rows = pl.ds(pl.multiple_of(o * 8, 8), 8)
        rows = go(copy(FS.at[ch, :, theirs_rows], FR.at[ch], sib))
        total = jnp.sum(RA[1 - ch] * FS[ch, ch], axis=1, keepdims=True)
        HAs[ch] = jnp.broadcast_to(total, (16, D)).reshape(2, 8, D)
        HAr[ch, 2 * hd + c] = HAs[ch, c]
        mine, its = HAs.at[ch, c], HAs.at[ch, o]
        slot = HAr.at[ch, 2 * hd + c]
        rows += go(copy(its, slot, sib))
        rows += go(*[copy(mine, slot, to) for to in heads])
        rows += go(*[copy(its, slot, to) for to in heads_sib])
        return rows

    def rs_end(ch, copies, slots):
        done(copies)
        mine = pl.ds(pl.multiple_of(c * 8, 8), 8)
        for a, slot in enumerate(slots):
            sm[slot, :, half_of[0]] = FS[ch, a, mine]
            sm[slot, :, half_of[1]] = FR[ch, a]

    units = [(j, t) for j in range(3) for t in range(2)]

    def video_probs(h, part):
        j, t = part
        head = 3 * h + j
        tops = SV[0, head]
        weights = jnp.exp2(tops - jnp.max(tops, axis=0, keepdims=True))
        over = 1.0 / jnp.sum(weights * SV[1, head], axis=0, keepdims=True)
        weights = weights * over
        inner = jnp.sum(weights * SV[2, head], axis=0, keepdims=True)
        chunk = slice(256 * t, 256 * (t + 1))
        probs = jnp.concatenate(
            [EV[head, D * i : D * i + D, chunk] * weights[i : i + 1, chunk] for i in range(4)],
            axis=0,
        )
        ds = (probs * (DV[head, :, chunk] - inner[:, chunk])).astype(BF16)
        return probs.astype(BF16), ds

    def finish(ch, j, own):
        go(*(rs_q1(ch, j) if own else (cross(ch, j),)))

    def video_pass(h, own):
        sums = {}

        def use(part, made):
            j, t = part
            low, ds = made
            chunk, lanes = slice(256 * t, 256 * (t + 1)), lanes_of(3 * h + j)
            grads = dot(ds, vqn[chunk, lanes], NN), dot(low, vdo[chunk, lanes], NN)
            if t == 0:
                sums[j] = grads
                return
            if own:
                cross(0, j).wait()
            put(0, j, own, slice(0, 4), 0, (sums[j][0] + grads[0]) * FACTOR)
            put(0, j, own, slice(0, 4), 1, sums[j][1] + grads[1])
            finish(0, j, own)

        staged(units, lambda part: video_probs(h, part), use)

    def video_rows(h):
        def use(part, made):
            j, t = part
            low, ds = made
            chunk, lanes = slice(256 * t, 256 * (t + 1)), lanes_of(3 * h + j)
            keys = jnp.transpose(some_rows(1, h, range(4), 1, j))
            values = jnp.transpose(some_rows(0, h, range(4), 0, j))
            video_out[chunk, lanes] = jnp.transpose(dot(values, low, NN)).astype(BF16)
            grad_q = jnp.transpose(dot(keys, ds, NN)) * FACTOR
            GQ[chunk, lanes] = grad_q
            IA[0, chunk] += vq[chunk, lanes].astype(F32) * gvq_gain[:, lanes] * grad_q

        staged(units, lambda part: video_probs(h, part), use)

    def store(i, src, dst):
        one = pltpu.make_async_copy(src, dst, local.at[4 + i])
        one.start()
        return one

    def inner_start(i):
        HI[i, hd] = jnp.zeros((8, 512), F32)
        HI[i, hd, 0:1, :] = row_of(IA[i])
        return go(*[copy(HI.at[i, hd], HI.at[i, hd], to) for to in heads])

    def video_final(i, copies, raw, gain, grad, out):
        done(copies)
        inner = (HI[i, 0] + HI[i, 1] + HI[i, 2] + HI[i, 3]) / WIDTH
        inv_i = inv_col[i]
        scale = inv_i * inv_i * inv_i * col(inner[0:1, :])
        for b in range(NH):
            at_b = slice(b * D, (b + 1) * D)
            value = inv_i * gain[:, at_b] * grad[:, at_b] - raw[:, at_b].astype(F32) * scale
            out[:, at_b] = value.astype(BF16)

    video_pass(o, False)
    stats_merge(0, level0)
    level1 = stats_start(1, ring_p)
    video_pass(c, True)
    stats_merge(1, level1)
    level2 = stats_start(2, ring_q)
    a2 = rs_q2(0)
    stats_merge(2, level2)

    total = ST[3, 1]
    safe = jnp.where(total == 0.0, 1.0, total)
    WT[0] = jnp.exp2(ST[0, 0] - ST[3, 0]) / safe
    WT[1] = ST[3, 2] / safe

    def audio_probs(h, part):
        j, t = part
        head = 3 * h + j
        row = pl.ds(head, 1)
        weight, shift = (
            jnp.concatenate([WT[n, 2 * t, row, :], WT[n, 2 * t + 1, row, :]], axis=1)
            for n in (0, 1)
        )
        chunk = slice(256 * t, 256 * (t + 1))
        probs = E[head, :, chunk] * weight
        ds = (probs * (DP[head, :, chunk] - shift)).astype(BF16)
        return probs.astype(BF16), ds

    def audio_pass(h, own):
        def use(part, made):
            j, t = part
            low, ds = made
            lanes = lanes_of(3 * h + j)
            chunks = slice(2 * t, 2 * t + 2)
            numer = jnp.transpose(dot(vvT[lanes, :], low, NN))
            grad_q = jnp.transpose(dot(vkT[lanes, :], ds, NN)) * FACTOR
            if own and t == 0:
                cross(1, j).wait()
            put(1, j, own, chunks, 0, numer)
            put(1, j, own, chunks, 1, grad_q)
            if t == 1:
                finish(1, j, own)

        staged(units, lambda part: audio_probs(h, part), use)

    def row_pass(h):
        sums = {}

        def use(part, made):
            j, t = part
            low, ds = made
            lanes = lanes_of(3 * h + j)
            ids = (2 * t, 2 * t + 1)
            grads = dot(ds, some_rows(1, h, ids, 0, j), NN), dot(low, some_rows(0, h, ids, 1, j), NN)
            if t == 0:
                sums[j] = grads
                return
            grad_k = (sums[j][0] + grads[0]) * FACTOR
            out_gvv[:, lanes] = (sums[j][1] + grads[1]).astype(BF16)
            GK[:, lanes] = grad_k
            IA[1] += vk[:, lanes].astype(F32) * gvk_gain[:, lanes] * grad_k

        staged(units, lambda part: audio_probs(h, part), use)

    audio_pass(o, False)
    audio_pass(c, True)
    b2 = rs_q2(1)
    a3 = rs_p(0, a2)
    video_rows(0)
    b3 = rs_p(1, b2)
    a4 = rs_z(0, a3)
    video_rows(1)
    inner0 = inner_start(0)
    stores = [store(0, video_out, video_out_hbm)]
    b4 = rs_z(1, b3)
    a5 = rs_core(0, a4)
    twice(row_pass)
    inner1 = inner_start(1)
    stores.append(store(1, out_gvv, gvv_hbm))
    b5 = rs_core(1, b4)
    video_final(0, inner0, vq, gvq_gain, GQ, out_gvq)
    stores.append(store(2, out_gvq, gvq_hbm))
    video_final(1, inner1, vk, gvk_gain, GK, out_gvk)
    stores.append(store(3, out_gvk, gvk_hbm))
    rs_end(0, a5, (3, 4))
    rs_end(1, b5, (5, 2))
    out_small[0] = sm[5]
    out_small[3] = sm[4]
    parts = ((aq, gaq_gain, sm[2]), (ak, gak_gain, sm[3]))
    for i, (raw, gain, grad) in enumerate(parts):
        total = HAr[1 - i, 0]
        for k in range(1, 8):
            total = total + HAr[1 - i, k]
        total = total / WIDTH
        wide = jnp.concatenate([inv_a[i]] * NH, axis=1)
        scale = jnp.concatenate([inv_a[i] * inv_a[i] * inv_a[i] * total] * NH, axis=1)
        out_small[1 + i] = wide * gain[...] * grad - raw[...].astype(F32) * scale
    for one in stores:
        one.wait()


def write_kernel(
    a, b, c, d, small, out_a, out_b, out_c, out_d, small_0, small_1, small_2, small_3, held, sems
):
    parts = ROWS // 4
    ins, outs = [], []
    for i, (src, dst) in enumerate(((a, out_a), (b, out_b), (c, out_c), (d, out_d))):
        for k in range(4):
            rows = slice(k * parts, (k + 1) * parts)
            n = 4 * i + k
            ins.append(pltpu.make_async_copy(src.at[rows], held.at[i, rows], sems.at[0, n]))
            outs.append(pltpu.make_async_copy(held.at[i, rows], dst.at[rows], sems.at[1, n]))
    for one in ins:
        one.start()
    for i, out in enumerate((small_0, small_1, small_2, small_3)):
        out[...] = small[i].astype(BF16)
    for one, two in zip(ins, outs):
        one.wait()
        two.start()
    for two in outs:
        two.wait()


def shards(*args):
    big = jax.ShapeDtypeStruct((ROWS, LOCAL), BF16)
    vmem = pltpu.VMEM
    wide = vmem((ROWS, LOCAL), BF16)
    scratch = [wide] * 8 + [
        vmem((8, LOCAL), F32),
        vmem((2, 16, HALF), F32),
        vmem((2, 2, 4, 4, 2, 2, 16, HALF), BF16),
        vmem((3, 2, 16, HALF), BF16),
        vmem((3, 3, 16, HALF), BF16),
        vmem((4, 2, 8, D), F32),
        vmem((4, 8, 512), F32),
        vmem((2, 4, 8, 512), F32),
        vmem((2, 2, 8, D), F32),
        vmem((2, 8, 8, D), F32),
        vmem((ROWS, LOCAL), BF16),
        vmem((ROWS, LOCAL), BF16),
        vmem((LOCAL, ROWS), BF16),
        vmem((LOCAL, ROWS), BF16),
        vmem((2, ROWS, D), F32),
        vmem((NH, ROWS, TOK), F32),
        vmem((NH, ROWS, TOK), F32),
        vmem((NH, TOK, ROWS), F32),
        vmem((NH, TOK, ROWS), F32),
        vmem((3, NH, 4, ROWS), F32),
        vmem((4, 3, 4, 8, D), F32),
        vmem((3, 3, 3, 4, 8, D), F32),
        vmem((2, 4, 8, D), F32),
        vmem((ROWS, LOCAL), F32),
        vmem((ROWS, LOCAL), F32),
        vmem((2, ROWS, D), F32),
        vmem((2, 3, 2, TOK, D), BF16),
        vmem((2, 3, 2, TOK, D), BF16),
        vmem((2, 3, 4, 4, 2, 2, 16, D), BF16),
        vmem((2, 2, 3, 2, 2, 2, 16, D), BF16),
        vmem((2, 2, 3, 4, 2, 2, 16, D), BF16),
        vmem((2, 4, 3, 2, 2, 16, D), BF16),
        vmem((2, 3, 3, 2, 2, 16, D), BF16),
        vmem((2, 2, 3, 2, 16, D), BF16),
        vmem((2, 3, 2, 16, D), BF16),
        vmem((2, 2, 16, HALF), F32),
        vmem((2, 2, 8, HALF), F32),
        vmem((6, 8, LOCAL), F32),
        pltpu.SemaphoreType.DMA((128,)),
        pltpu.SemaphoreType.DMA((128,)),
        pltpu.SemaphoreType.DMA((8,)),
    ]
    spec = pl.BlockSpec(memory_space=pltpu.VMEM)
    anywhere = pl.BlockSpec(memory_space=pl.ANY)
    made = pl.pallas_call(
        kernel,
        out_shape=(big, big, big, big, jax.ShapeDtypeStruct((4, 8, LOCAL), F32)),
        in_specs=[anywhere] * 4 + [spec] * 8,
        out_specs=(anywhere,) * 4 + (spec,),
        scratch_shapes=scratch,
        compiler_params=pltpu.CompilerParams(
            collective_id=0, has_side_effects=True, vmem_limit_bytes=60 * 1024 * 1024
        ),
    )(*args)
    small = jax.ShapeDtypeStruct((8, LOCAL), BF16)
    wrote = pl.pallas_call(
        write_kernel,
        out_shape=(big,) * 4 + (small,) * 4,
        in_specs=[anywhere] * 4 + [spec],
        out_specs=(anywhere,) * 4 + (spec,) * 4,
        scratch_shapes=[vmem((4, ROWS, LOCAL), BF16), pltpu.SemaphoreType.DMA((2, 16))],
    )(*made)
    video_out, gvq, gvk, gvv, audio_out, gaq, gak, gav = wrote
    return video_out, audio_out, gvq, gvk, gvv, gaq, gak, gav


def solution(mesh):
    both = P("seq", "head")
    return jax.shard_map(
        shards,
        mesh=mesh,
        in_specs=(both,) * 8 + (P("head"),) * 4,
        out_specs=(both,) * 8,
        check_vma=False,
    )
```

```python
import math

import jax
import jax.numpy as jnp
from jax import lax
from jax.experimental import pallas as pl
from jax.experimental.pallas import tpu as pltpu
from jax.sharding import PartitionSpec as P

HEADS = 24
D = 128
WIDTH = HEADS * D
EPS = 1e-06
FACTOR = 1.0 / math.sqrt(D)
KLOG = FACTOR * math.log2(math.e)
ROWS = 512
TOK = 512
LOCAL = 768
HALF = 384
NH = 6
F32 = jnp.float32
BF16 = jnp.bfloat16
MESH = pl.DeviceIdType.MESH
NT = (((1,), (1,)), ((), ()))
TN = (((0,), (0,)), ((), ()))
NN = (((1,), (0,)), ((), ()))


def dot(a, b, dims):
    return lax.dot_general(a, b, dims, preferred_element_type=F32)


def col(row):
    return jnp.transpose(jnp.broadcast_to(row, (D, ROWS)))


def row_of(square):
    return jnp.sum(jnp.transpose(square), axis=0, keepdims=True)


def fold(op, array):
    while array.shape[0] > 8:
        half = array.shape[0] // 2
        array = op(array[:half], array[half:])
    if op is jnp.maximum:
        return jnp.max(array, axis=0, keepdims=True)
    return jnp.sum(array, axis=0, keepdims=True)


def kernel(
    vq_in, vk_in, vv_in, vdo_in, aq, ak, av, ado, gain0, gain1, gain2, gain3,
    video_out, out_gvq, out_gvk, out_gvv, out_small,
    vq, vk, vv, vdo, GN, RA,
    G, PK, PR, HSA, HS, HI, HAs, HAr, vqn, vkn, vvT, vkT, inv_col, E, DP, EV, DV, SV, ST, SR, WT,
    GQ, GK, IA, Xs, Xr, R, RB1, RB2, S, RB3, TF, TZ, RB4, sm,
    send, recv, local,
):
    s = lax.axis_index("seq")
    hd = lax.axis_index("head")
    c = s % 2
    y = (s // 2) % 4
    x = (s // 8) % 4
    zh = s // 32
    p = x + c * (y - x)
    q = y + c * (x - y)
    o = 1 - c

    def at(zz, pp, qq):
        xx = pp + c * (qq - pp)
        yy = qq + c * (pp - qq)
        return {"seq": ((zz * 4 + xx) * 4 + yy) * 2 + c}

    sib = {"seq": s + 1 - 2 * c}
    opp = at(1 - zh, p, q)
    opp_sib = {"seq": s + 1 - 2 * c + 32 - 64 * zh}
    ring_p = [at(zh, (p + k) % 4, q) for k in (1, 2, 3)]
    ring_q = [at(zh, p, (q + k) % 4) for k in (1, 2, 3)]
    heads = [{"head": (hd + k) % 4} for k in (1, 2, 3)]
    near = [sib, opp, opp_sib]
    far = [[dict(to, head=(hd + k) % 4) for k in (1, 2, 3)] for to in near]
    pn, pb, p2 = (p + 1) % 4, (p + 3) % 4, (p + 2) % 4
    qn, qb, q2 = (q + 1) % 4, (q + 3) % 4, (q + 2) % 4
    right_q, left_q = ring_q[0], ring_q[2]

    barrier = pltpu.get_barrier_semaphore()
    partners = near + ring_p + ring_q + heads + far[0] + far[1] + far[2]
    for partner in partners:
        pl.semaphore_signal(barrier, inc=1, device_id=partner, device_id_type=MESH)
    loads = [
        pltpu.make_async_copy(src, dst, local.at[i])
        for i, (src, dst) in enumerate(((vq_in, vq), (vk_in, vk), (vv_in, vv), (vdo_in, vdo)))
    ]
    for one in loads:
        one.start()
    for i, gain in enumerate((gain0, gain1, gain2, gain3)):
        GN[i : i + 1, :] = gain[...].reshape(1, LOCAL)
    gvq_gain, gvk_gain, gaq_gain, gak_gain = (GN.at[i : i + 1] for i in range(4))

    count = [0]

    def slots(n):
        first = count[0]
        count[0] += n
        return first

    def copy(src, dst, to, slot=None):
        slot = slots(1) if slot is None else slot
        return pltpu.make_async_remote_copy(
            src_ref=src,
            dst_ref=dst,
            send_sem=send.at[slot],
            recv_sem=recv.at[slot],
            device_id=to,
            device_id_type=MESH,
        )

    def go(*copies):
        for one in copies:
            one.start()
        return copies

    def done(copies):
        for one in copies:
            one.wait()

    half_of = [pl.ds(pl.multiple_of(i * HALF, D), HALF) for i in (c, o)]

    def pack(n, refs):
        for i, half in enumerate(half_of):
            rows = [ref[:, half].astype(F32) for ref in refs]
            PK[n, i] = jnp.concatenate(rows, axis=0).astype(BF16)

    def ag_first(n):
        return go(
            copy(PK.at[n, 1], PR.at[n, 0], sib),
            copy(PK.at[n, 0], PR.at[n, 1], opp),
            copy(PK.at[n, 1], PR.at[n, 2], opp_sib),
        )

    def chip_rows(mine, other, a):
        mine = mine.astype(F32)[8 * a : 8 * a + 8]
        other = other.astype(F32)[8 * a : 8 * a + 8]
        low = jnp.where(c == 0, mine, other)
        high = jnp.where(c == 0, other, mine)
        return jnp.concatenate([low, high], axis=0)

    def ag_p(ch, copies):
        done(copies)
        for a in range(2):
            G[c, ch, q, p, zh, a] = chip_rows(PK[ch, 0], PR[ch, 0], a).astype(BF16)
            G[c, ch, q, p, 1 - zh, a] = chip_rows(PR[ch, 1], PR[ch, 2], a).astype(BF16)
        block = G.at[c, ch, q, p]
        return go(*[copy(block, block, to) for to in ring_p])

    base_f = slots(8)

    def forward(ch, n):
        i = (q + n + (n // 2) * (5 - 2 * n)) % 4
        block = G.at[c, ch, i]
        return copy(block, block, sib, slot=base_f + 4 * ch + n)

    def ag_q1(ch, copies):
        done(copies)
        block = G.at[c, ch, q]
        return go(copy(block, block, right_q), copy(block, block, left_q))

    def ag_q2(ch, copies):
        done(copies)
        one, two = G.at[c, ch, qb, 0:2], G.at[c, ch, qn, 2:4]
        return go(copy(one, one, right_q), copy(two, two, left_q))

    pack(0, (av, ado))
    for i, raw in enumerate((aq, ak)):
        block = raw[...].astype(F32)
        total = jnp.sum(block * block, axis=1, keepdims=True)
        HSA[hd, i] = jnp.broadcast_to(total, (8, D))
    pl.semaphore_wait(barrier, len(partners))
    sums_a = go(*[copy(HSA.at[hd], HSA.at[hd], to) for to in heads])
    first0 = ag_first(0)
    pack(2, (aq, ak))
    raws = ag_first(2)

    HS[hd] = jnp.zeros((8, 512), F32)

    def video_sum(i, raw):
        loads[i].wait()
        total = jnp.zeros((ROWS, D), F32)
        for b in range(NH):
            block = raw[:, b * D : (b + 1) * D].astype(F32)
            total = total + block * block
        HS[hd, i : i + 1, :] = row_of(total)

    video_sum(0, vq)
    done(sums_a)
    inv_a = []
    for i, (raw, gain) in enumerate(((aq, gaq_gain), (ak, gak_gain))):
        total = HSA[0, i] + HSA[1, i] + HSA[2, i] + HSA[3, i]
        inv_a.append(lax.rsqrt(total / WIDTH + EPS))
        wide = jnp.concatenate([inv_a[i]] * NH, axis=1)
        sm[i] = (raw[...].astype(F32) * wide * gain[...]).astype(BF16).astype(F32)
    pack(1, (sm.at[0], sm.at[1]))
    first1 = ag_first(1)
    ring0 = ag_p(0, first0)
    video_sum(1, vk)
    sums = go(*[copy(HS.at[hd], HS.at[hd], to) for to in heads])
    ring1 = ag_p(1, first1)
    q10 = ag_q1(0, ring0)
    go(forward(0, 0))
    done(sums)
    total = HS[0] + HS[1] + HS[2] + HS[3]
    inv = lax.rsqrt(total / WIDTH + EPS)

    def norm_video(i, raw, gain, out):
        inv_col[i] = col(inv[i : i + 1, :])
        for b in range(NH):
            at_b = slice(b * D, (b + 1) * D)
            out[:, at_b] = (raw[:, at_b].astype(F32) * inv_col[i] * gain[:, at_b]).astype(BF16)

    norm_video(1, vk, gvk_gain, vkn)
    q11 = ag_q1(1, ring1)
    go(forward(1, 0))
    norm_video(0, vq, gvq_gain, vqn)
    for b in range(NH):
        at_b = slice(b * D, (b + 1) * D)
        vkT[at_b, :] = jnp.transpose(vkn[:, at_b])

    def lanes_of(i):
        return pl.ds(pl.multiple_of(i * D, D), D)

    ST[...] = jnp.zeros_like(ST)

    def staged(units, make, use):
        held = None
        for unit in units:
            made = make(unit)
            if held is not None:
                use(*held)
            held = (unit, made)
        use(*held)

    def rows_of(ch, h, i, a, j):
        return G[h, ch, i, :, :, a, :, j * D : j * D + D].reshape(D, D)

    def some_rows(ch, h, ids, a, j):
        return jnp.concatenate([rows_of(ch, h, i, a, j) for i in ids], axis=0)

    def video(h, *ids):
        def make(j):
            lanes = lanes_of(3 * h + j)
            scores = dot(some_rows(1, h, ids, 1, j), vqn[:, lanes], NT) * KLOG
            return scores, dot(some_rows(0, h, ids, 0, j), vdo[:, lanes], NT)

        def use(j, made):
            scores, dprob = made
            head = 3 * h + j
            top = fold(jnp.maximum, scores)
            expo = jnp.exp2(scores - top)
            nothing = jnp.zeros_like(top)
            values = [top, fold(jnp.add, expo), fold(jnp.add, expo * dprob)]
            for n, i in enumerate(ids):
                part = slice(D * n, D * n + D)
                EV[head, lanes_of(i), :] = expo[part]
                DV[head, lanes_of(i), :] = dprob[part]
                for k in range(3):
                    SV[k, head, pl.ds(i, 1), :] = nothing if n and k else values[k]

        staged(range(3), make, use)

    def audio(h, *ids):
        def make(j):
            lanes = lanes_of(3 * h + j)
            scores = dot(vkn[:, lanes], some_rows(1, h, ids, 0, j), NT) * KLOG
            return scores, dot(vv[:, lanes], some_rows(0, h, ids, 1, j), NT)

        def use(j, made):
            scores, dprob = made
            head = 3 * h + j
            top = fold(jnp.maximum, scores)
            expo = jnp.exp2(scores - top)
            values = [top, fold(jnp.add, expo), fold(jnp.add, expo * dprob)]
            for n, i in enumerate(ids):
                part = slice(D * n, D * n + D)
                E[head, :, lanes_of(i)] = expo[:, part]
                DP[head, :, lanes_of(i)] = dprob[:, part]
                for k in range(3):
                    ST[0, k, i, pl.ds(head, 1), :] = values[k][:, part]

        staged(range(3), make, use)

    def pair(n):
        return (p + 3 * n) % 4, (p + 1 + n) % 4

    def twice(body):
        def step(n, carry):
            body(n)
            return carry

        lax.fori_loop(0, 2, step, 0)

    loads[2].wait()
    for b in range(NH):
        at_b = slice(b * D, (b + 1) * D)
        vvT[at_b, :] = jnp.transpose(vv[:, at_b])
    audio(c, q)
    loads[3].wait()
    video(c, q)
    q20 = ag_q2(0, q10)
    go(*[forward(0, n) for n in (1, 2)])
    q21 = ag_q2(1, q11)
    go(*[forward(1, n) for n in (1, 2)])
    audio(c, qn, qb)
    done(q20)
    go(forward(0, 3))
    done(q21)
    go(forward(1, 3))
    video(c, qn, qb)
    audio(c, q2)

    def their_audio(n):
        done([forward(ch, 2 * n + k) for ch in range(2) for k in range(2)])
        audio(o, *pair(n))

    twice(their_audio)

    def stats_start(level, to):
        return go(*[copy(ST.at[level], SR.at[level, k], one) for k, one in enumerate(to)])

    def stats_merge(level, copies):
        done(copies)
        tops = [ST[level, 0]] + [SR[level, k, 0] for k in range(3)]
        top = jnp.maximum(jnp.maximum(tops[0], tops[1]), jnp.maximum(tops[2], tops[3]))
        weights = [jnp.exp2(one - top) for one in tops]
        ST[level + 1, 0] = top
        for n in (1, 2):
            total = ST[level, n] * weights[0]
            for k in range(3):
                total = total + SR[level, k, n] * weights[k + 1]
            ST[level + 1, n] = total

    level0 = stats_start(0, (sib, opp, opp_sib))
    video(c, q2)
    twice(lambda n: video(o, *pair(n)))
    done(raws)
    for i, gain in enumerate((gaq_gain, gak_gain)):
        RA[zh, i] = chip_rows(PK[2, 0], PR[2, 0], i) * gain[:, half_of[0]]
        RA[1 - zh, i] = chip_rows(PR[2, 1], PR[2, 2], i) * gain[:, half_of[0]]

    IA[...] = jnp.zeros_like(IA)
    base_cross = slots(6)

    def cross(ch, j):
        return copy(Xs.at[ch, j], Xr.at[ch, j], sib, slot=base_cross + 3 * ch + j)

    def put(ch, j, own, chunks, a, value):
        rows = slice(128 * chunks.start, 128 * chunks.stop)
        if own:
            value = value + Xr[ch, j, a, rows].astype(F32)
            shape = (chunks.stop - chunks.start, 4, 2, 16, D)
            R[ch, j, chunks, :, :, a] = value.reshape(shape).astype(BF16)
        else:
            Xs[ch, j, a, rows] = value.astype(BF16)

    base_q1 = slots(12)

    def rs_q1(ch, j):
        slot = base_q1 + 6 * ch + 2 * j
        return (
            copy(R.at[ch, j, q2, 0:2], RB1.at[ch, 0, j], right_q, slot=slot),
            copy(R.at[ch, j, q2, 2:4], RB1.at[ch, 1, j], left_q, slot=slot + 1),
        )

    def rs_q2(ch):
        copies = []
        for j in range(3):
            done(rs_q1(ch, j))
            one = R[ch, j, qn, 0:2].astype(F32) + RB1[ch, 0, j].astype(F32)
            R[ch, j, qn, 0:2] = one.astype(BF16)
            two = R[ch, j, qb, 2:4].astype(F32) + RB1[ch, 1, j].astype(F32)
            R[ch, j, qb, 2:4] = two.astype(BF16)
            copies += go(
                copy(R.at[ch, j, qn], RB2.at[ch, 0, j], right_q),
                copy(R.at[ch, j, qb], RB2.at[ch, 1, j], left_q),
            )
        return copies

    def rs_p(ch, copies):
        for j in range(3):
            done(copies[2 * j : 2 * j + 2])
            total = R[ch, j, q].astype(F32) + RB2[ch, 0, j].astype(F32) + RB2[ch, 1, j].astype(F32)
            S[ch, :, j] = total.astype(BF16)
        return go(
            *[copy(S.at[ch, (p + k + 1) % 4], RB3.at[ch, k], ring_p[k]) for k in range(3)]
        )

    def rs_last(ch, copies):
        done(copies)
        total = S[ch, p].astype(F32)
        for k in range(3):
            total = total + RB3[ch, k].astype(F32)
        for zz in range(2):
            both = [jnp.concatenate([total[j, zz, a] for j in range(3)], axis=1) for a in range(2)]
            for cc in range(2):
                rows = slice(8 * cc, 8 * cc + 8)
                tile = jnp.concatenate([both[0][rows], both[1][rows]], axis=0)
                TF[ch, zz, cc] = tile
                TZ[ch, zz, cc] = tile.astype(BF16)
            inner = jnp.sum(RA[zz, 1 - ch] * both[ch], axis=1, keepdims=True)
            HAs[ch, zz] = jnp.broadcast_to(inner, (16, D)).reshape(2, 8, D)
        place = ((zh, c), (zh, o), (1 - zh, c), (1 - zh, o))
        rows = go(
            *[copy(TZ.at[ch, zz, cc], RB4.at[ch, k], near[k]) for k, (zz, cc) in enumerate(place[1:])]
        )
        sender = 4 * hd + 2 * zh + c
        slot = HAr.at[ch, sender]
        HAr[ch, sender] = HAs[ch, zh, c]
        targets = [(place[0], to) for to in heads]
        for k in range(3):
            targets += [(place[k + 1], to) for to in [near[k]] + far[k]]
        return rows + go(*[copy(HAs.at[ch, zz, cc], slot, to) for (zz, cc), to in targets])

    def rs_end(ch, copies, slots):
        done(copies)
        mine = TF[ch, zh, c] + RB4[ch, 1].astype(F32)
        other = RB4[ch, 0].astype(F32) + RB4[ch, 2].astype(F32)
        for a, slot in enumerate(slots):
            sm[slot, :, half_of[0]] = mine[8 * a : 8 * a + 8]
            sm[slot, :, half_of[1]] = other[8 * a : 8 * a + 8]

    units = [(j, t) for j in range(3) for t in range(2)]

    def video_probs(h, part):
        j, t = part
        head = 3 * h + j
        tops = SV[0, head]
        weights = jnp.exp2(tops - jnp.max(tops, axis=0, keepdims=True))
        over = 1.0 / jnp.sum(weights * SV[1, head], axis=0, keepdims=True)
        weights = weights * over
        inner = jnp.sum(weights * SV[2, head], axis=0, keepdims=True)
        chunk = slice(256 * t, 256 * (t + 1))
        probs = jnp.concatenate(
            [EV[head, D * i : D * i + D, chunk] * weights[i : i + 1, chunk] for i in range(4)],
            axis=0,
        )
        ds = (probs * (DV[head, :, chunk] - inner[:, chunk])).astype(BF16)
        return probs.astype(BF16), ds

    def finish(ch, j, own):
        go(*(rs_q1(ch, j) if own else (cross(ch, j),)))

    def video_pass(h, own):
        sums = {}

        def use(part, made):
            j, t = part
            low, ds = made
            chunk, lanes = slice(256 * t, 256 * (t + 1)), lanes_of(3 * h + j)
            grads = dot(ds, vqn[chunk, lanes], NN), dot(low, vdo[chunk, lanes], NN)
            if t == 0:
                sums[j] = grads
                return
            if own:
                cross(0, j).wait()
            put(0, j, own, slice(0, 4), 0, (sums[j][0] + grads[0]) * FACTOR)
            put(0, j, own, slice(0, 4), 1, sums[j][1] + grads[1])
            finish(0, j, own)

        staged(units, lambda part: video_probs(h, part), use)

    def video_rows(h):
        def use(part, made):
            j, t = part
            low, ds = made
            chunk, lanes = slice(256 * t, 256 * (t + 1)), lanes_of(3 * h + j)
            keys = jnp.transpose(some_rows(1, h, range(4), 1, j))
            values = jnp.transpose(some_rows(0, h, range(4), 0, j))
            video_out[chunk, lanes] = jnp.transpose(dot(values, low, NN)).astype(BF16)
            grad_q = jnp.transpose(dot(keys, ds, NN)) * FACTOR
            GQ[chunk, lanes] = grad_q
            IA[0, chunk] += vq[chunk, lanes].astype(F32) * gvq_gain[:, lanes] * grad_q

        staged(units, lambda part: video_probs(h, part), use)

    def inner_start(i):
        HI[i, hd] = jnp.zeros((8, 512), F32)
        HI[i, hd, 0:1, :] = row_of(IA[i])
        return go(*[copy(HI.at[i, hd], HI.at[i, hd], to) for to in heads])

    def video_final(i, copies, raw, gain, grad, out):
        done(copies)
        inner = (HI[i, 0] + HI[i, 1] + HI[i, 2] + HI[i, 3]) / WIDTH
        inv_i = inv_col[i]
        scale = inv_i * inv_i * inv_i * col(inner[0:1, :])
        for b in range(NH):
            at_b = slice(b * D, (b + 1) * D)
            value = inv_i * gain[:, at_b] * grad[:, at_b] - raw[:, at_b].astype(F32) * scale
            out[:, at_b] = value.astype(BF16)

    video_pass(o, False)
    stats_merge(0, level0)
    level1 = stats_start(1, ring_p)
    video_pass(c, True)
    stats_merge(1, level1)
    level2 = stats_start(2, ring_q)
    video_rows(0)
    a2 = rs_q2(0)
    video_rows(1)
    inner0 = inner_start(0)
    stats_merge(2, level2)

    total = ST[3, 1]
    safe = jnp.where(total == 0.0, 1.0, total)
    WT[0] = jnp.exp2(ST[0, 0] - ST[3, 0]) / safe
    WT[1] = ST[3, 2] / safe

    def audio_probs(h, part):
        j, t = part
        head = 3 * h + j
        row = pl.ds(head, 1)
        weight, shift = (
            jnp.concatenate([WT[n, 2 * t, row, :], WT[n, 2 * t + 1, row, :]], axis=1)
            for n in (0, 1)
        )
        chunk = slice(256 * t, 256 * (t + 1))
        probs = E[head, :, chunk] * weight
        ds = (probs * (DP[head, :, chunk] - shift)).astype(BF16)
        return probs.astype(BF16), ds

    def audio_pass(h, own):
        def use(part, made):
            j, t = part
            low, ds = made
            lanes = lanes_of(3 * h + j)
            chunks = slice(2 * t, 2 * t + 2)
            numer = jnp.transpose(dot(vvT[lanes, :], low, NN))
            grad_q = jnp.transpose(dot(vkT[lanes, :], ds, NN)) * FACTOR
            if own and t == 0:
                cross(1, j).wait()
            put(1, j, own, chunks, 0, numer)
            put(1, j, own, chunks, 1, grad_q)
            if t == 1:
                finish(1, j, own)

        staged(units, lambda part: audio_probs(h, part), use)

    def row_pass(h):
        sums = {}

        def use(part, made):
            j, t = part
            low, ds = made
            lanes = lanes_of(3 * h + j)
            ids = (2 * t, 2 * t + 1)
            grads = dot(ds, some_rows(1, h, ids, 0, j), NN), dot(low, some_rows(0, h, ids, 1, j), NN)
            if t == 0:
                sums[j] = grads
                return
            grad_k = (sums[j][0] + grads[0]) * FACTOR
            out_gvv[:, lanes] = (sums[j][1] + grads[1]).astype(BF16)
            GK[:, lanes] = grad_k
            IA[1] += vk[:, lanes].astype(F32) * gvk_gain[:, lanes] * grad_k

        staged(units, lambda part: audio_probs(h, part), use)

    audio_pass(o, False)
    a3 = rs_p(0, a2)
    audio_pass(c, True)
    b2 = rs_q2(1)
    a4 = rs_last(0, a3)
    row_pass(0)
    b3 = rs_p(1, b2)
    row_pass(1)
    inner1 = inner_start(1)
    b4 = rs_last(1, b3)
    video_final(0, inner0, vq, gvq_gain, GQ, out_gvq)
    video_final(1, inner1, vk, gvk_gain, GK, out_gvk)
    rs_end(0, a4, (3, 4))
    rs_end(1, b4, (5, 2))
    out_small[0] = sm[5]
    out_small[3] = sm[4]
    parts = ((aq, gaq_gain, sm[2]), (ak, gak_gain, sm[3]))
    for i, (raw, gain, grad) in enumerate(parts):
        total = HAr[1 - i, 0]
        for k in range(1, 16):
            total = total + HAr[1 - i, k]
        total = total / WIDTH
        wide = jnp.concatenate([inv_a[i]] * NH, axis=1)
        scale = jnp.concatenate([inv_a[i] * inv_a[i] * inv_a[i] * total] * NH, axis=1)
        out_small[1 + i] = wide * gain[...] * grad - raw[...].astype(F32) * scale


def write_kernel(
    a, b, c, d, small, out_a, out_b, out_c, out_d, small_0, small_1, small_2, small_3, sems
):
    parts = ROWS // 4
    copies = []
    for i, (src, dst) in enumerate(((a, out_a), (b, out_b), (c, out_c), (d, out_d))):
        for k in range(4):
            rows = slice(k * parts, (k + 1) * parts)
            copies.append(pltpu.make_async_copy(src.at[rows], dst.at[rows], sems.at[4 * i + k]))
    for one in copies:
        one.start()
    for i, out in enumerate((small_0, small_1, small_2, small_3)):
        out[...] = small[i].astype(BF16)
    for one in copies:
        one.wait()


def shards(*args):
    big = jax.ShapeDtypeStruct((ROWS, LOCAL), BF16)
    vmem = pltpu.VMEM
    wide = vmem((ROWS, LOCAL), BF16)
    scratch = [wide] * 4 + [
        vmem((8, LOCAL), F32),
        vmem((2, 2, 16, HALF), F32),
        vmem((2, 2, 4, 4, 2, 2, 16, HALF), BF16),
        vmem((3, 2, 16, HALF), BF16),
        vmem((3, 3, 16, HALF), BF16),
        vmem((4, 2, 8, D), F32),
        vmem((4, 8, 512), F32),
        vmem((2, 4, 8, 512), F32),
        vmem((2, 2, 2, 8, D), F32),
        vmem((2, 16, 8, D), F32),
        vmem((ROWS, LOCAL), BF16),
        vmem((ROWS, LOCAL), BF16),
        vmem((LOCAL, ROWS), BF16),
        vmem((LOCAL, ROWS), BF16),
        vmem((2, ROWS, D), F32),
        vmem((NH, ROWS, TOK), F32),
        vmem((NH, ROWS, TOK), F32),
        vmem((NH, TOK, ROWS), F32),
        vmem((NH, TOK, ROWS), F32),
        vmem((3, NH, 4, ROWS), F32),
        vmem((4, 3, 4, 8, D), F32),
        vmem((3, 3, 3, 4, 8, D), F32),
        vmem((2, 4, 8, D), F32),
        vmem((ROWS, LOCAL), F32),
        vmem((ROWS, LOCAL), F32),
        vmem((2, ROWS, D), F32),
        vmem((2, 3, 2, TOK, D), BF16),
        vmem((2, 3, 2, TOK, D), BF16),
        vmem((2, 3, 4, 4, 2, 2, 16, D), BF16),
        vmem((2, 2, 3, 2, 2, 2, 16, D), BF16),
        vmem((2, 2, 3, 4, 2, 2, 16, D), BF16),
        vmem((2, 4, 3, 2, 2, 16, D), BF16),
        vmem((2, 3, 3, 2, 2, 16, D), BF16),
        vmem((2, 2, 2, 16, HALF), F32),
        vmem((2, 2, 2, 16, HALF), BF16),
        vmem((2, 3, 16, HALF), BF16),
        vmem((6, 8, LOCAL), F32),
        pltpu.SemaphoreType.DMA((160,)),
        pltpu.SemaphoreType.DMA((160,)),
        pltpu.SemaphoreType.DMA((8,)),
    ]
    spec = pl.BlockSpec(memory_space=pltpu.VMEM)
    anywhere = pl.BlockSpec(memory_space=pl.ANY)
    made = pl.pallas_call(
        kernel,
        out_shape=(vmem((ROWS, LOCAL), BF16),) * 4 + (vmem((4, 8, LOCAL), F32),),
        in_specs=[anywhere] * 4 + [spec] * 8,
        out_specs=(spec,) * 5,
        scratch_shapes=scratch,
        compiler_params=pltpu.CompilerParams(
            collective_id=0, has_side_effects=True, vmem_limit_bytes=57 * 1024 * 1024
        ),
    )(*args)
    small = jax.ShapeDtypeStruct((8, LOCAL), BF16)
    wrote = pl.pallas_call(
        write_kernel,
        out_shape=(big,) * 4 + (small,) * 4,
        in_specs=[spec] * 5,
        out_specs=(anywhere,) * 4 + (spec,) * 4,
        scratch_shapes=[pltpu.SemaphoreType.DMA((16,))],
    )(*made)
    video_out, gvq, gvk, gvv, audio_out, gaq, gak, gav = wrote
    return video_out, audio_out, gvq, gvk, gvv, gaq, gak, gav


def solution(mesh):
    both = P("seq", "head")
    return jax.shard_map(
        shards,
        mesh=mesh,
        in_specs=(both,) * 8 + (P("head"),) * 4,
        out_specs=(both,) * 8,
        check_vma=False,
    )
```

```python
import math

import jax
import jax.numpy as jnp
from jax import lax
from jax.experimental import pallas as pl
from jax.experimental.pallas import tpu as pltpu
from jax.sharding import PartitionSpec as P

HEADS = 24
D = 128
WIDTH = HEADS * D
EPS = 1e-06
FACTOR = 1.0 / math.sqrt(D)
KLOG = FACTOR * math.log2(math.e)
ROWS = 512
TOK = 512
LOCAL = 768
HALF = 384
NH = 6
F32 = jnp.float32
BF16 = jnp.bfloat16
MESH = pl.DeviceIdType.MESH
NT = (((1,), (1,)), ((), ()))
TN = (((0,), (0,)), ((), ()))
NN = (((1,), (0,)), ((), ()))


def dot(a, b, dims):
    return lax.dot_general(a, b, dims, preferred_element_type=F32)


def col(row):
    return jnp.transpose(jnp.broadcast_to(row, (D, ROWS)))


def row_of(square):
    return jnp.sum(jnp.transpose(square), axis=0, keepdims=True)


def fold(op, array):
    while array.shape[0] > 8:
        half = array.shape[0] // 2
        array = op(array[:half], array[half:])
    if op is jnp.maximum:
        return jnp.max(array, axis=0, keepdims=True)
    return jnp.sum(array, axis=0, keepdims=True)


def kernel(
    vq_in, vk_in, vv_in, vdo_in, aq, ak, av, ado, gain0, gain1, gain2, gain3,
    video_out, out_gvq, out_gvk, out_gvv, out_small,
    vq, vk, vv, vdo, GN, RA,
    G, PK, PR, HSA, HS, HI, HAs, HAr, vqn, vkn, vvT, vkT, inv_col, E, DP, EV, DV, SV, ST, SR, WT,
    GQ, GK, IA, Xs, Xr, R, RB1, RB2, S, RB3, TF, TZ, RB4, sm,
    send, recv, local,
):
    s = lax.axis_index("seq")
    hd = lax.axis_index("head")
    c = s % 2
    y = (s // 2) % 4
    x = (s // 8) % 4
    zh = s // 32
    p = x + c * (y - x)
    q = y + c * (x - y)
    o = 1 - c

    def at(zz, pp, qq):
        xx = pp + c * (qq - pp)
        yy = qq + c * (pp - qq)
        return {"seq": ((zz * 4 + xx) * 4 + yy) * 2 + c}

    sib = {"seq": s + 1 - 2 * c}
    opp = at(1 - zh, p, q)
    opp_sib = {"seq": s + 1 - 2 * c + 32 - 64 * zh}
    ring_p = [at(zh, (p + k) % 4, q) for k in (1, 2, 3)]
    ring_q = [at(zh, p, (q + k) % 4) for k in (1, 2, 3)]
    heads = [{"head": (hd + k) % 4} for k in (1, 2, 3)]
    near = [sib, opp, opp_sib]
    far = [[dict(to, head=(hd + k) % 4) for k in (1, 2, 3)] for to in near]
    pn, pb, p2 = (p + 1) % 4, (p + 3) % 4, (p + 2) % 4
    qn, qb, q2 = (q + 1) % 4, (q + 3) % 4, (q + 2) % 4
    right_q, left_q = ring_q[0], ring_q[2]

    barrier = pltpu.get_barrier_semaphore()
    partners = near + ring_p + ring_q + heads + far[0] + far[1] + far[2]
    for partner in partners:
        pl.semaphore_signal(barrier, inc=1, device_id=partner, device_id_type=MESH)
    loads = [
        pltpu.make_async_copy(src, dst, local.at[i])
        for i, (src, dst) in enumerate(((vq_in, vq), (vk_in, vk), (vv_in, vv), (vdo_in, vdo)))
    ]
    for one in loads:
        one.start()
    for i, gain in enumerate((gain0, gain1, gain2, gain3)):
        GN[i : i + 1, :] = gain[...].reshape(1, LOCAL)
    gvq_gain, gvk_gain, gaq_gain, gak_gain = (GN.at[i : i + 1] for i in range(4))

    count = [0]

    def slots(n):
        first = count[0]
        count[0] += n
        return first

    def copy(src, dst, to, slot=None):
        slot = slots(1) if slot is None else slot
        return pltpu.make_async_remote_copy(
            src_ref=src,
            dst_ref=dst,
            send_sem=send.at[slot],
            recv_sem=recv.at[slot],
            device_id=to,
            device_id_type=MESH,
        )

    def go(*copies):
        for one in copies:
            one.start()
        return copies

    def done(copies):
        for one in copies:
            one.wait()

    half_of = [pl.ds(pl.multiple_of(i * HALF, D), HALF) for i in (c, o)]

    def pack(n, refs):
        for i, half in enumerate(half_of):
            rows = [ref[:, half].astype(F32) for ref in refs]
            PK[n, i] = jnp.concatenate(rows, axis=0).astype(BF16)

    def ag_first(n):
        return go(
            copy(PK.at[n, 1], PR.at[n, 0], sib),
            copy(PK.at[n, 0], PR.at[n, 1], opp),
            copy(PK.at[n, 1], PR.at[n, 2], opp_sib),
        )

    def chip_rows(mine, other, a):
        mine = mine.astype(F32)[8 * a : 8 * a + 8]
        other = other.astype(F32)[8 * a : 8 * a + 8]
        low = jnp.where(c == 0, mine, other)
        high = jnp.where(c == 0, other, mine)
        return jnp.concatenate([low, high], axis=0)

    def ag_p(ch, copies):
        done(copies)
        for a in range(2):
            G[c, ch, q, p, zh, a] = chip_rows(PK[ch, 0], PR[ch, 0], a).astype(BF16)
            G[c, ch, q, p, 1 - zh, a] = chip_rows(PR[ch, 1], PR[ch, 2], a).astype(BF16)
        block = G.at[c, ch, q, p]
        return go(*[copy(block, block, to) for to in ring_p])

    base_f = slots(8)

    def forward(ch, n):
        i = (q + n + (n // 2) * (5 - 2 * n)) % 4
        block = G.at[c, ch, i]
        return copy(block, block, sib, slot=base_f + 4 * ch + n)

    def ag_q1(ch, copies):
        done(copies)
        block = G.at[c, ch, q]
        return go(copy(block, block, right_q), copy(block, block, left_q))

    def ag_q2(ch, copies):
        done(copies)
        one, two = G.at[c, ch, qb, 0:2], G.at[c, ch, qn, 2:4]
        return go(copy(one, one, right_q), copy(two, two, left_q))

    pack(0, (av, ado))
    for i, raw in enumerate((aq, ak)):
        block = raw[...].astype(F32)
        total = jnp.sum(block * block, axis=1, keepdims=True)
        HSA[hd, i] = jnp.broadcast_to(total, (8, D))
    pl.semaphore_wait(barrier, len(partners))
    sums_a = go(*[copy(HSA.at[hd], HSA.at[hd], to) for to in heads])
    first0 = ag_first(0)
    pack(2, (aq, ak))
    raws = ag_first(2)

    HS[hd] = jnp.zeros((8, 512), F32)

    def video_sum(i, raw):
        loads[i].wait()
        total = jnp.zeros((ROWS, D), F32)
        for b in range(NH):
            block = raw[:, b * D : (b + 1) * D].astype(F32)
            total = total + block * block
        HS[hd, i : i + 1, :] = row_of(total)

    video_sum(0, vq)
    done(sums_a)
    inv_a = []
    for i, (raw, gain) in enumerate(((aq, gaq_gain), (ak, gak_gain))):
        total = HSA[0, i] + HSA[1, i] + HSA[2, i] + HSA[3, i]
        inv_a.append(lax.rsqrt(total / WIDTH + EPS))
        wide = jnp.concatenate([inv_a[i]] * NH, axis=1)
        sm[i] = (raw[...].astype(F32) * wide * gain[...]).astype(BF16).astype(F32)
    pack(1, (sm.at[0], sm.at[1]))
    first1 = ag_first(1)
    ring0 = ag_p(0, first0)
    video_sum(1, vk)
    sums = go(*[copy(HS.at[hd], HS.at[hd], to) for to in heads])
    ring1 = ag_p(1, first1)
    q10 = ag_q1(0, ring0)
    go(forward(0, 0))
    done(sums)
    total = HS[0] + HS[1] + HS[2] + HS[3]
    inv = lax.rsqrt(total / WIDTH + EPS)

    def norm_video(i, raw, gain, out):
        inv_col[i] = col(inv[i : i + 1, :])
        for b in range(NH):
            at_b = slice(b * D, (b + 1) * D)
            out[:, at_b] = (raw[:, at_b].astype(F32) * inv_col[i] * gain[:, at_b]).astype(BF16)

    norm_video(1, vk, gvk_gain, vkn)
    q11 = ag_q1(1, ring1)
    go(forward(1, 0))
    norm_video(0, vq, gvq_gain, vqn)
    for b in range(NH):
        at_b = slice(b * D, (b + 1) * D)
        vkT[at_b, :] = jnp.transpose(vkn[:, at_b])

    def lanes_of(i):
        return pl.ds(pl.multiple_of(i * D, D), D)

    ST[...] = jnp.zeros_like(ST)

    def staged(units, make, use):
        held = None
        for unit in units:
            made = make(unit)
            if held is not None:
                use(*held)
            held = (unit, made)
        use(*held)

    def rows_of(ch, h, i, a, j):
        return G[h, ch, i, :, :, a, :, j * D : j * D + D].reshape(D, D)

    def some_rows(ch, h, ids, a, j):
        return jnp.concatenate([rows_of(ch, h, i, a, j) for i in ids], axis=0)

    def video(h, *ids):
        def make(j):
            lanes = lanes_of(3 * h + j)
            scores = dot(some_rows(1, h, ids, 1, j), vqn[:, lanes], NT) * KLOG
            return scores, dot(some_rows(0, h, ids, 0, j), vdo[:, lanes], NT)

        def use(j, made):
            scores, dprob = made
            head = 3 * h + j
            top = fold(jnp.maximum, scores)
            expo = jnp.exp2(scores - top)
            nothing = jnp.zeros_like(top)
            values = [top, fold(jnp.add, expo), fold(jnp.add, expo * dprob)]
            for n, i in enumerate(ids):
                part = slice(D * n, D * n + D)
                EV[head, lanes_of(i), :] = expo[part]
                DV[head, lanes_of(i), :] = dprob[part]
                for k in range(3):
                    SV[k, head, pl.ds(i, 1), :] = nothing if n and k else values[k]

        staged(range(3), make, use)

    def audio(h, *ids):
        def make(j):
            lanes = lanes_of(3 * h + j)
            scores = dot(vkn[:, lanes], some_rows(1, h, ids, 0, j), NT) * KLOG
            return scores, dot(vv[:, lanes], some_rows(0, h, ids, 1, j), NT)

        def use(j, made):
            scores, dprob = made
            head = 3 * h + j
            top = fold(jnp.maximum, scores)
            expo = jnp.exp2(scores - top)
            values = [top, fold(jnp.add, expo), fold(jnp.add, expo * dprob)]
            for n, i in enumerate(ids):
                part = slice(D * n, D * n + D)
                E[head, :, lanes_of(i)] = expo[:, part]
                DP[head, :, lanes_of(i)] = dprob[:, part]
                for k in range(3):
                    ST[0, k, i, pl.ds(head, 1), :] = values[k][:, part]

        staged(range(3), make, use)

    def pair(n):
        return (p + 3 * n) % 4, (p + 1 + n) % 4

    def twice(body):
        def step(n, carry):
            body(n)
            return carry

        lax.fori_loop(0, 2, step, 0)

    loads[2].wait()
    for b in range(NH):
        at_b = slice(b * D, (b + 1) * D)
        vvT[at_b, :] = jnp.transpose(vv[:, at_b])
    audio(c, q)
    loads[3].wait()
    video(c, q)
    q20 = ag_q2(0, q10)
    go(*[forward(0, n) for n in (1, 2)])
    q21 = ag_q2(1, q11)
    go(*[forward(1, n) for n in (1, 2)])
    audio(c, qn, qb)
    done(q20)
    go(forward(0, 3))
    done(q21)
    go(forward(1, 3))
    video(c, qn, qb)
    audio(c, q2)

    def their_audio(n):
        done([forward(ch, 2 * n + k) for ch in range(2) for k in range(2)])
        audio(o, *pair(n))

    twice(their_audio)

    def stats_start(level, to):
        return go(*[copy(ST.at[level], SR.at[level, k], one) for k, one in enumerate(to)])

    def stats_merge(level, copies):
        done(copies)
        tops = [ST[level, 0]] + [SR[level, k, 0] for k in range(3)]
        top = jnp.maximum(jnp.maximum(tops[0], tops[1]), jnp.maximum(tops[2], tops[3]))
        weights = [jnp.exp2(one - top) for one in tops]
        ST[level + 1, 0] = top
        for n in (1, 2):
            total = ST[level, n] * weights[0]
            for k in range(3):
                total = total + SR[level, k, n] * weights[k + 1]
            ST[level + 1, n] = total

    level0 = stats_start(0, (sib, opp, opp_sib))
    video(c, q2)
    twice(lambda n: video(o, *pair(n)))
    done(raws)
    for i, gain in enumerate((gaq_gain, gak_gain)):
        RA[zh, i] = chip_rows(PK[2, 0], PR[2, 0], i) * gain[:, half_of[0]]
        RA[1 - zh, i] = chip_rows(PR[2, 1], PR[2, 2], i) * gain[:, half_of[0]]

    IA[...] = jnp.zeros_like(IA)
    base_cross = slots(6)

    def cross(ch, j):
        return copy(Xs.at[ch, j], Xr.at[ch, j], sib, slot=base_cross + 3 * ch + j)

    def put(ch, j, own, chunks, a, value):
        rows = slice(128 * chunks.start, 128 * chunks.stop)
        if own:
            value = value + Xr[ch, j, a, rows].astype(F32)
            shape = (chunks.stop - chunks.start, 4, 2, 16, D)
            R[ch, j, chunks, :, :, a] = value.reshape(shape).astype(BF16)
        else:
            Xs[ch, j, a, rows] = value.astype(BF16)

    base_q1 = slots(12)

    def rs_q1(ch, j):
        slot = base_q1 + 6 * ch + 2 * j
        return (
            copy(R.at[ch, j, q2, 0:2], RB1.at[ch, 0, j], right_q, slot=slot),
            copy(R.at[ch, j, q2, 2:4], RB1.at[ch, 1, j], left_q, slot=slot + 1),
        )

    def rs_q2(ch, heads_done):
        copies = []
        for j in heads_done:
            done(rs_q1(ch, j))
            one = R[ch, j, qn, 0:2].astype(F32) + RB1[ch, 0, j].astype(F32)
            R[ch, j, qn, 0:2] = one.astype(BF16)
            two = R[ch, j, qb, 2:4].astype(F32) + RB1[ch, 1, j].astype(F32)
            R[ch, j, qb, 2:4] = two.astype(BF16)
            copies += go(
                copy(R.at[ch, j, qn], RB2.at[ch, 0, j], right_q),
                copy(R.at[ch, j, qb], RB2.at[ch, 1, j], left_q),
            )
        return copies

    def rs_p(ch, copies):
        for j in range(3):
            done(copies[2 * j : 2 * j + 2])
            total = R[ch, j, q].astype(F32) + RB2[ch, 0, j].astype(F32) + RB2[ch, 1, j].astype(F32)
            S[ch, :, j] = total.astype(BF16)
        return go(
            *[copy(S.at[ch, (p + k + 1) % 4], RB3.at[ch, k], ring_p[k]) for k in range(3)]
        )

    def rs_last(ch, copies):
        done(copies)
        total = S[ch, p].astype(F32)
        for k in range(3):
            total = total + RB3[ch, k].astype(F32)
        for zz in range(2):
            both = [jnp.concatenate([total[j, zz, a] for j in range(3)], axis=1) for a in range(2)]
            for cc in range(2):
                rows = slice(8 * cc, 8 * cc + 8)
                tile = jnp.concatenate([both[0][rows], both[1][rows]], axis=0)
                TF[ch, zz, cc] = tile
                TZ[ch, zz, cc] = tile.astype(BF16)
            inner = jnp.sum(RA[zz, 1 - ch] * both[ch], axis=1, keepdims=True)
            HAs[ch, zz] = jnp.broadcast_to(inner, (16, D)).reshape(2, 8, D)
        place = ((zh, c), (zh, o), (1 - zh, c), (1 - zh, o))
        rows = go(
            *[copy(TZ.at[ch, zz, cc], RB4.at[ch, k], near[k]) for k, (zz, cc) in enumerate(place[1:])]
        )
        sender = 4 * hd + 2 * zh + c
        slot = HAr.at[ch, sender]
        HAr[ch, sender] = HAs[ch, zh, c]
        targets = [(place[0], to) for to in heads]
        for k in range(3):
            targets += [(place[k + 1], to) for to in [near[k]] + far[k]]
        return rows + go(*[copy(HAs.at[ch, zz, cc], slot, to) for (zz, cc), to in targets])

    def rs_end(ch, copies, slots):
        done(copies)
        mine = TF[ch, zh, c] + RB4[ch, 1].astype(F32)
        other = RB4[ch, 0].astype(F32) + RB4[ch, 2].astype(F32)
        for a, slot in enumerate(slots):
            sm[slot, :, half_of[0]] = mine[8 * a : 8 * a + 8]
            sm[slot, :, half_of[1]] = other[8 * a : 8 * a + 8]

    units = [(j, t) for j in range(3) for t in range(2)]

    def video_probs(h, part):
        j, t = part
        head = 3 * h + j
        tops = SV[0, head]
        weights = jnp.exp2(tops - jnp.max(tops, axis=0, keepdims=True))
        over = 1.0 / jnp.sum(weights * SV[1, head], axis=0, keepdims=True)
        weights = weights * over
        inner = jnp.sum(weights * SV[2, head], axis=0, keepdims=True)
        chunk = slice(256 * t, 256 * (t + 1))
        probs = jnp.concatenate(
            [EV[head, D * i : D * i + D, chunk] * weights[i : i + 1, chunk] for i in range(4)],
            axis=0,
        )
        ds = (probs * (DV[head, :, chunk] - inner[:, chunk])).astype(BF16)
        return probs.astype(BF16), ds

    def finish(ch, j, own):
        go(*(rs_q1(ch, j) if own else (cross(ch, j),)))

    def video_pass(h, own):
        sums = {}

        def use(part, made):
            j, t = part
            low, ds = made
            chunk, lanes = slice(256 * t, 256 * (t + 1)), lanes_of(3 * h + j)
            grads = dot(ds, vqn[chunk, lanes], NN), dot(low, vdo[chunk, lanes], NN)
            if t == 0:
                keys = jnp.transpose(some_rows(1, h, range(4), 1, j))
                values = jnp.transpose(some_rows(0, h, range(4), 0, j))
                sums[j] = grads + (keys, values)
            keys, values = sums[j][2:]
            video_out[chunk, lanes] = jnp.transpose(dot(values, low, NN)).astype(BF16)
            grad_q = jnp.transpose(dot(keys, ds, NN)) * FACTOR
            GQ[chunk, lanes] = grad_q
            IA[0, chunk] += vq[chunk, lanes].astype(F32) * gvq_gain[:, lanes] * grad_q
            if t == 0:
                return
            if own:
                cross(0, j).wait()
            put(0, j, own, slice(0, 4), 0, (sums[j][0] + grads[0]) * FACTOR)
            put(0, j, own, slice(0, 4), 1, sums[j][1] + grads[1])
            finish(0, j, own)

        staged(units, lambda part: video_probs(h, part), use)

    def inner_start(i):
        HI[i, hd] = jnp.zeros((8, 512), F32)
        HI[i, hd, 0:1, :] = row_of(IA[i])
        return go(*[copy(HI.at[i, hd], HI.at[i, hd], to) for to in heads])

    def video_final(i, copies, raw, gain, grad, out):
        done(copies)
        inner = (HI[i, 0] + HI[i, 1] + HI[i, 2] + HI[i, 3]) / WIDTH
        inv_i = inv_col[i]
        scale = inv_i * inv_i * inv_i * col(inner[0:1, :])
        for b in range(NH):
            at_b = slice(b * D, (b + 1) * D)
            value = inv_i * gain[:, at_b] * grad[:, at_b] - raw[:, at_b].astype(F32) * scale
            out[:, at_b] = value.astype(BF16)

    stats_merge(0, level0)
    level1 = stats_start(1, ring_p)
    video_pass(o, False)
    stats_merge(1, level1)
    level2 = stats_start(2, ring_q)
    video_pass(c, True)
    inner0 = inner_start(0)
    stats_merge(2, level2)

    total = ST[3, 1]
    safe = jnp.where(total == 0.0, 1.0, total)
    WT[0] = jnp.exp2(ST[0, 0] - ST[3, 0]) / safe
    WT[1] = ST[3, 2] / safe

    def audio_probs(h, part):
        j, t = part
        head = 3 * h + j
        row = pl.ds(head, 1)
        weight, shift = (
            jnp.concatenate([WT[n, 2 * t, row, :], WT[n, 2 * t + 1, row, :]], axis=1)
            for n in (0, 1)
        )
        chunk = slice(256 * t, 256 * (t + 1))
        probs = E[head, :, chunk] * weight
        ds = (probs * (DP[head, :, chunk] - shift)).astype(BF16)
        return probs.astype(BF16), ds

    def audio_pass(h, own):
        def use(part, made):
            j, t = part
            low, ds = made
            lanes = lanes_of(3 * h + j)
            chunks = slice(2 * t, 2 * t + 2)
            numer = jnp.transpose(dot(vvT[lanes, :], low, NN))
            grad_q = jnp.transpose(dot(vkT[lanes, :], ds, NN)) * FACTOR
            if own and t == 0:
                cross(1, j).wait()
            put(1, j, own, chunks, 0, numer)
            put(1, j, own, chunks, 1, grad_q)
            if t == 1:
                finish(1, j, own)

        staged(units, lambda part: audio_probs(h, part), use)

    def row_pass(h):
        sums = {}

        def use(part, made):
            j, t = part
            low, ds = made
            lanes = lanes_of(3 * h + j)
            ids = (2 * t, 2 * t + 1)
            grads = dot(ds, some_rows(1, h, ids, 0, j), NN), dot(low, some_rows(0, h, ids, 1, j), NN)
            if t == 0:
                sums[j] = grads
                return
            grad_k = (sums[j][0] + grads[0]) * FACTOR
            out_gvv[:, lanes] = (sums[j][1] + grads[1]).astype(BF16)
            GK[:, lanes] = grad_k
            IA[1] += vk[:, lanes].astype(F32) * gvk_gain[:, lanes] * grad_k

        staged(units, lambda part: audio_probs(h, part), use)

    audio_pass(o, False)
    a2 = rs_q2(0, (0, 1, 2))
    audio_pass(c, True)
    b2 = rs_q2(1, (0,))
    a3 = rs_p(0, a2)
    row_pass(0)
    b2 += rs_q2(1, (1, 2))
    a4 = rs_last(0, a3)
    row_pass(1)
    b3 = rs_p(1, b2)
    inner1 = inner_start(1)
    b4 = rs_last(1, b3)
    video_final(0, inner0, vq, gvq_gain, GQ, out_gvq)
    video_final(1, inner1, vk, gvk_gain, GK, out_gvk)
    rs_end(0, a4, (3, 4))
    rs_end(1, b4, (5, 2))
    out_small[0] = sm[5]
    out_small[3] = sm[4]
    parts = ((aq, gaq_gain, sm[2]), (ak, gak_gain, sm[3]))
    for i, (raw, gain, grad) in enumerate(parts):
        total = HAr[1 - i, 0]
        for k in range(1, 16):
            total = total + HAr[1 - i, k]
        total = total / WIDTH
        wide = jnp.concatenate([inv_a[i]] * NH, axis=1)
        scale = jnp.concatenate([inv_a[i] * inv_a[i] * inv_a[i] * total] * NH, axis=1)
        out_small[1 + i] = wide * gain[...] * grad - raw[...].astype(F32) * scale


def write_kernel(
    a, b, c, d, small, out_a, out_b, out_c, out_d, small_0, small_1, small_2, small_3, sems
):
    parts = ROWS // 4
    copies = []
    for i, (src, dst) in enumerate(((a, out_a), (b, out_b), (c, out_c), (d, out_d))):
        for k in range(4):
            rows = slice(k * parts, (k + 1) * parts)
            copies.append(pltpu.make_async_copy(src.at[rows], dst.at[rows], sems.at[4 * i + k]))
    for one in copies:
        one.start()
    for i, out in enumerate((small_0, small_1, small_2, small_3)):
        out[...] = small[i].astype(BF16)
    for one in copies:
        one.wait()


def shards(*args):
    big = jax.ShapeDtypeStruct((ROWS, LOCAL), BF16)
    vmem = pltpu.VMEM
    wide = vmem((ROWS, LOCAL), BF16)
    scratch = [wide] * 4 + [
        vmem((8, LOCAL), F32),
        vmem((2, 2, 16, HALF), F32),
        vmem((2, 2, 4, 4, 2, 2, 16, HALF), BF16),
        vmem((3, 2, 16, HALF), BF16),
        vmem((3, 3, 16, HALF), BF16),
        vmem((4, 2, 8, D), F32),
        vmem((4, 8, 512), F32),
        vmem((2, 4, 8, 512), F32),
        vmem((2, 2, 2, 8, D), F32),
        vmem((2, 16, 8, D), F32),
        vmem((ROWS, LOCAL), BF16),
        vmem((ROWS, LOCAL), BF16),
        vmem((LOCAL, ROWS), BF16),
        vmem((LOCAL, ROWS), BF16),
        vmem((2, ROWS, D), F32),
        vmem((NH, ROWS, TOK), F32),
        vmem((NH, ROWS, TOK), F32),
        vmem((NH, TOK, ROWS), F32),
        vmem((NH, TOK, ROWS), F32),
        vmem((3, NH, 4, ROWS), F32),
        vmem((4, 3, 4, 8, D), F32),
        vmem((3, 3, 3, 4, 8, D), F32),
        vmem((2, 4, 8, D), F32),
        vmem((ROWS, LOCAL), F32),
        vmem((ROWS, LOCAL), F32),
        vmem((2, ROWS, D), F32),
        vmem((2, 3, 2, TOK, D), BF16),
        vmem((2, 3, 2, TOK, D), BF16),
        vmem((2, 3, 4, 4, 2, 2, 16, D), BF16),
        vmem((2, 2, 3, 2, 2, 2, 16, D), BF16),
        vmem((2, 2, 3, 4, 2, 2, 16, D), BF16),
        vmem((2, 4, 3, 2, 2, 16, D), BF16),
        vmem((2, 3, 3, 2, 2, 16, D), BF16),
        vmem((2, 2, 2, 16, HALF), F32),
        vmem((2, 2, 2, 16, HALF), BF16),
        vmem((2, 3, 16, HALF), BF16),
        vmem((6, 8, LOCAL), F32),
        pltpu.SemaphoreType.DMA((160,)),
        pltpu.SemaphoreType.DMA((160,)),
        pltpu.SemaphoreType.DMA((8,)),
    ]
    spec = pl.BlockSpec(memory_space=pltpu.VMEM)
    anywhere = pl.BlockSpec(memory_space=pl.ANY)
    made = pl.pallas_call(
        kernel,
        out_shape=(vmem((ROWS, LOCAL), BF16),) * 4 + (vmem((4, 8, LOCAL), F32),),
        in_specs=[anywhere] * 4 + [spec] * 8,
        out_specs=(spec,) * 5,
        scratch_shapes=scratch,
        compiler_params=pltpu.CompilerParams(
            collective_id=0, has_side_effects=True, vmem_limit_bytes=57 * 1024 * 1024
        ),
    )(*args)
    small = jax.ShapeDtypeStruct((8, LOCAL), BF16)
    wrote = pl.pallas_call(
        write_kernel,
        out_shape=(big,) * 4 + (small,) * 4,
        in_specs=[spec] * 5,
        out_specs=(anywhere,) * 4 + (spec,) * 4,
        scratch_shapes=[pltpu.SemaphoreType.DMA((16,))],
        compiler_params=pltpu.CompilerParams(vmem_limit_bytes=4 * 1024 * 1024),
    )(*[pltpu.with_memory_space_constraint(one, pltpu.VMEM) for one in made])
    video_out, gvq, gvk, gvv, audio_out, gaq, gak, gav = wrote
    return video_out, audio_out, gvq, gvk, gvv, gaq, gak, gav


def solution(mesh):
    both = P("seq", "head")
    return jax.shard_map(
        shards,
        mesh=mesh,
        in_specs=(both,) * 8 + (P("head"),) * 4,
        out_specs=(both,) * 8,
        check_vma=False,
    )
```

```python
import math

import jax
import jax.numpy as jnp
from jax import lax
from jax.experimental import pallas as pl
from jax.experimental.pallas import tpu as pltpu
from jax.sharding import PartitionSpec as P

HEADS = 24
D = 128
WIDTH = HEADS * D
EPS = 1e-06
FACTOR = 1.0 / math.sqrt(D)
KLOG = FACTOR * math.log2(math.e)
ROWS = 512
TOK = 512
LOCAL = 768
HALF = 384
NH = 6
F32 = jnp.float32
BF16 = jnp.bfloat16
MESH = pl.DeviceIdType.MESH
NT = (((1,), (1,)), ((), ()))
TN = (((0,), (0,)), ((), ()))
NN = (((1,), (0,)), ((), ()))


def dot(a, b, dims):
    return lax.dot_general(a, b, dims, preferred_element_type=F32)


def col(row):
    return jnp.transpose(jnp.broadcast_to(row, (D, ROWS)))


def row_of(square):
    return jnp.sum(jnp.transpose(square), axis=0, keepdims=True)


def fold(op, array):
    while array.shape[0] > 8:
        half = array.shape[0] // 2
        array = op(array[:half], array[half:])
    if op is jnp.maximum:
        return jnp.max(array, axis=0, keepdims=True)
    return jnp.sum(array, axis=0, keepdims=True)


def kernel(
    vq_in, vk_in, vv_in, vdo_in, aq, ak, av, ado, gain0, gain1, gain2, gain3,
    video_out, out_gvq, out_gvk, out_gvv, out_small,
    vq, vk, vv, vdo, GN, RA,
    G, PK, PR, HSA, HS, HI, HAs, HAr, vqn, vkn, vvT, vkT, inv_col, E, DP, EV, DV, SV, ST, SR, WT,
    GQ, GK, IA, Xs, Xr, R, RB1, RB2, S, RB3, TF, TZ, RB4, sm,
    send, recv, local,
):
    s = lax.axis_index("seq")
    hd = lax.axis_index("head")
    c = s % 2
    y = (s // 2) % 4
    x = (s // 8) % 4
    zh = s // 32
    p = x + c * (y - x)
    q = y + c * (x - y)
    o = 1 - c

    def at(zz, pp, qq):
        xx = pp + c * (qq - pp)
        yy = qq + c * (pp - qq)
        return {"seq": ((zz * 4 + xx) * 4 + yy) * 2 + c}

    sib = {"seq": s + 1 - 2 * c}
    opp = at(1 - zh, p, q)
    opp_sib = {"seq": s + 1 - 2 * c + 32 - 64 * zh}
    ring_p = [at(zh, (p + k) % 4, q) for k in (1, 2, 3)]
    ring_q = [at(zh, p, (q + k) % 4) for k in (1, 2, 3)]
    heads = [{"head": (hd + k) % 4} for k in (1, 2, 3)]
    near = [sib, opp, opp_sib]
    far = [[dict(to, head=(hd + k) % 4) for k in (1, 2, 3)] for to in near]
    pn, pb, p2 = (p + 1) % 4, (p + 3) % 4, (p + 2) % 4
    qn, qb, q2 = (q + 1) % 4, (q + 3) % 4, (q + 2) % 4
    right_q, left_q = ring_q[0], ring_q[2]

    barrier = pltpu.get_barrier_semaphore()
    partners = near + ring_p + ring_q + heads + far[0] + far[1] + far[2]
    for partner in partners:
        pl.semaphore_signal(barrier, inc=1, device_id=partner, device_id_type=MESH)
    loads = [
        pltpu.make_async_copy(src, dst, local.at[i])
        for i, (src, dst) in enumerate(((vq_in, vq), (vk_in, vk), (vv_in, vv), (vdo_in, vdo)))
    ]
    for one in loads:
        one.start()
    for i, gain in enumerate((gain0, gain1, gain2, gain3)):
        GN[i : i + 1, :] = gain[...].reshape(1, LOCAL)
    gvq_gain, gvk_gain, gaq_gain, gak_gain = (GN.at[i : i + 1] for i in range(4))

    count = [0]

    def slots(n):
        first = count[0]
        count[0] += n
        return first

    def copy(src, dst, to, slot=None):
        slot = slots(1) if slot is None else slot
        return pltpu.make_async_remote_copy(
            src_ref=src,
            dst_ref=dst,
            send_sem=send.at[slot],
            recv_sem=recv.at[slot],
            device_id=to,
            device_id_type=MESH,
        )

    def go(*copies):
        for one in copies:
            one.start()
        return copies

    def done(copies):
        for one in copies:
            one.wait()

    half_of = [pl.ds(pl.multiple_of(i * HALF, D), HALF) for i in (c, o)]

    def pack(n, refs):
        for i, half in enumerate(half_of):
            rows = [ref[:, half].astype(F32) for ref in refs]
            PK[n, i] = jnp.concatenate(rows, axis=0).astype(BF16)

    def ag_first(n):
        return go(
            copy(PK.at[n, 1], PR.at[n, 0], sib),
            copy(PK.at[n, 0], PR.at[n, 1], opp),
            copy(PK.at[n, 1], PR.at[n, 2], opp_sib),
        )

    def chip_rows(mine, other, a):
        mine = mine.astype(F32)[8 * a : 8 * a + 8]
        other = other.astype(F32)[8 * a : 8 * a + 8]
        low = jnp.where(c == 0, mine, other)
        high = jnp.where(c == 0, other, mine)
        return jnp.concatenate([low, high], axis=0)

    def ag_p(ch):
        block = G.at[c, ch, q, p]
        return go(*[copy(block, block, to) for to in ring_p])

    base_f = slots(8)

    def forward(ch, n):
        i = (q + n + (n // 2) * (5 - 2 * n)) % 4
        block = G.at[c, ch, i]
        return copy(block, block, sib, slot=base_f + 4 * ch + n)

    def ag_q1(ch, copies):
        done(copies)
        block = G.at[c, ch, q]
        return go(copy(block, block, right_q), copy(block, block, left_q))

    def ag_q2(ch, copies):
        done(copies)
        one, two = G.at[c, ch, qb, 0:2], G.at[c, ch, qn, 2:4]
        return go(copy(one, one, right_q), copy(two, two, left_q))

    pack(0, (av, ado))
    pack(1, (aq, ak))
    sender = 4 * hd + 2 * zh + c
    for i, raw in enumerate((aq, ak)):
        block = raw[...].astype(F32)
        total = jnp.sum(block * block, axis=1, keepdims=True)
        HSA[sender, i] = jnp.broadcast_to(total, (8, D))
    pl.semaphore_wait(barrier, len(partners))
    first0 = ag_first(0)
    first1 = ag_first(1)
    mine = HSA.at[sender]
    first1 += go(*[copy(mine, mine, to) for to in near + heads + far[0] + far[1] + far[2]])

    HS[hd] = jnp.zeros((8, 512), F32)
    for i, raw in enumerate((vq, vk)):
        loads[i].wait()
        total = jnp.zeros((ROWS, D), F32)
        for b in range(NH):
            block = raw[:, b * D : (b + 1) * D].astype(F32)
            total = total + block * block
        HS[hd, i : i + 1, :] = row_of(total)
    sums = go(*[copy(HS.at[hd], HS.at[hd], to) for to in heads])

    done(first0)
    for a in range(2):
        G[c, 0, q, p, zh, a] = chip_rows(PK[0, 0], PR[0, 0], a).astype(BF16)
        G[c, 0, q, p, 1 - zh, a] = chip_rows(PR[0, 1], PR[0, 2], a).astype(BF16)
    ring0 = ag_p(0)

    done(first1)

    def inverse(zz, cc, i):
        total = HSA[2 * zz + cc, i]
        for k in range(1, 4):
            total = total + HSA[4 * k + 2 * zz + cc, i]
        return lax.rsqrt(total / WIDTH + EPS)

    for i, gain in enumerate((gaq_gain, gak_gain)):
        raws = chip_rows(PK[1, 0], PR[1, 0], i), chip_rows(PR[1, 1], PR[1, 2], i)
        for zz, raw in zip((zh, 1 - zh), raws):
            inv_row = jnp.concatenate([inverse(zz, cc, i) for cc in range(2)], axis=0)
            wide = jnp.concatenate([inv_row] * 3, axis=1)
            half = gain[:, half_of[0]]
            G[c, 1, q, p, zz, i] = (raw * wide * half).astype(BF16)
            RA[zz, i] = raw * half
    ring1 = ag_p(1)
    inv_a = [inverse(zh, c, i) for i in range(2)]

    loads[2].wait()
    for b in range(NH):
        at_b = slice(b * D, (b + 1) * D)
        vvT[at_b, :] = jnp.transpose(vv[:, at_b])
    done(sums)
    total = HS[0] + HS[1] + HS[2] + HS[3]
    inv = lax.rsqrt(total / WIDTH + EPS)

    def norm_video(i, raw, gain, out):
        inv_col[i] = col(inv[i : i + 1, :])
        for b in range(NH):
            at_b = slice(b * D, (b + 1) * D)
            out[:, at_b] = (raw[:, at_b].astype(F32) * inv_col[i] * gain[:, at_b]).astype(BF16)

    norm_video(1, vk, gvk_gain, vkn)
    q10 = ag_q1(0, ring0)
    go(forward(0, 0))
    norm_video(0, vq, gvq_gain, vqn)
    q11 = ag_q1(1, ring1)
    go(forward(1, 0))
    for b in range(NH):
        at_b = slice(b * D, (b + 1) * D)
        vkT[at_b, :] = jnp.transpose(vkn[:, at_b])

    def lanes_of(i):
        return pl.ds(pl.multiple_of(i * D, D), D)

    ST[...] = jnp.zeros_like(ST)

    def staged(units, make, use):
        held = None
        for unit in units:
            made = make(unit)
            if held is not None:
                use(*held)
            held = (unit, made)
        use(*held)

    def rows_of(ch, h, i, a, j):
        return G[h, ch, i, :, :, a, :, j * D : j * D + D].reshape(D, D)

    def some_rows(ch, h, ids, a, j):
        return jnp.concatenate([rows_of(ch, h, i, a, j) for i in ids], axis=0)

    def video(h, *ids):
        def make(j):
            lanes = lanes_of(3 * h + j)
            scores = dot(some_rows(1, h, ids, 1, j), vqn[:, lanes], NT) * KLOG
            return scores, dot(some_rows(0, h, ids, 0, j), vdo[:, lanes], NT)

        def use(j, made):
            scores, dprob = made
            head = 3 * h + j
            top = fold(jnp.maximum, scores)
            expo = jnp.exp2(scores - top)
            nothing = jnp.zeros_like(top)
            values = [top, fold(jnp.add, expo), fold(jnp.add, expo * dprob)]
            for n, i in enumerate(ids):
                part = slice(D * n, D * n + D)
                EV[head, lanes_of(i), :] = expo[part]
                DV[head, lanes_of(i), :] = dprob[part]
                for k in range(3):
                    SV[k, head, pl.ds(i, 1), :] = nothing if n and k else values[k]

        staged(range(3), make, use)

    def audio(h, *ids):
        def make(j):
            lanes = lanes_of(3 * h + j)
            scores = dot(vkn[:, lanes], some_rows(1, h, ids, 0, j), NT) * KLOG
            return scores, dot(vv[:, lanes], some_rows(0, h, ids, 1, j), NT)

        def use(j, made):
            scores, dprob = made
            head = 3 * h + j
            top = fold(jnp.maximum, scores)
            expo = jnp.exp2(scores - top)
            values = [top, fold(jnp.add, expo), fold(jnp.add, expo * dprob)]
            for n, i in enumerate(ids):
                part = slice(D * n, D * n + D)
                E[head, :, lanes_of(i)] = expo[:, part]
                DP[head, :, lanes_of(i)] = dprob[:, part]
                for k in range(3):
                    ST[0, k, i, pl.ds(head, 1), :] = values[k][:, part]

        staged(range(3), make, use)

    def pair(n):
        return (p + 3 * n) % 4, (p + 1 + n) % 4

    def twice(body):
        def step(n, carry):
            body(n)
            return carry

        lax.fori_loop(0, 2, step, 0)

    audio(c, q)
    loads[3].wait()
    video(c, q)
    q20 = ag_q2(0, q10)
    go(*[forward(0, n) for n in (1, 2)])
    q21 = ag_q2(1, q11)
    go(*[forward(1, n) for n in (1, 2)])
    audio(c, qn, qb)
    done(q20)
    go(forward(0, 3))
    done(q21)
    go(forward(1, 3))
    video(c, qn, qb)
    audio(c, q2)

    def their_audio(n):
        done([forward(ch, 2 * n + k) for ch in range(2) for k in range(2)])
        audio(o, *pair(n))

    twice(their_audio)

    def stats_start(level, to):
        return go(*[copy(ST.at[level], SR.at[level, k], one) for k, one in enumerate(to)])

    def stats_merge(level, copies):
        done(copies)
        tops = [ST[level, 0]] + [SR[level, k, 0] for k in range(3)]
        top = jnp.maximum(jnp.maximum(tops[0], tops[1]), jnp.maximum(tops[2], tops[3]))
        weights = [jnp.exp2(one - top) for one in tops]
        ST[level + 1, 0] = top
        for n in (1, 2):
            total = ST[level, n] * weights[0]
            for k in range(3):
                total = total + SR[level, k, n] * weights[k + 1]
            ST[level + 1, n] = total

    level0 = stats_start(0, (sib, opp, opp_sib))
    video(c, q2)
    twice(lambda n: video(o, *pair(n)))

    IA[...] = jnp.zeros_like(IA)
    base_cross = slots(6)

    def cross(ch, j):
        return copy(Xs.at[ch, j], Xr.at[ch, j], sib, slot=base_cross + 3 * ch + j)

    def put(ch, j, own, chunks, a, value):
        rows = slice(128 * chunks.start, 128 * chunks.stop)
        if own:
            value = value + Xr[ch, j, a, rows].astype(F32)
            shape = (chunks.stop - chunks.start, 4, 2, 16, D)
            R[ch, j, chunks, :, :, a] = value.reshape(shape).astype(BF16)
        else:
            Xs[ch, j, a, rows] = value.astype(BF16)

    base_q1 = slots(12)

    def rs_q1(ch, j):
        slot = base_q1 + 6 * ch + 2 * j
        return (
            copy(R.at[ch, j, q2, 0:2], RB1.at[ch, 0, j], right_q, slot=slot),
            copy(R.at[ch, j, q2, 2:4], RB1.at[ch, 1, j], left_q, slot=slot + 1),
        )

    def rs_q2(ch, heads_done):
        copies = []
        for j in heads_done:
            done(rs_q1(ch, j))
            one = R[ch, j, qn, 0:2].astype(F32) + RB1[ch, 0, j].astype(F32)
            R[ch, j, qn, 0:2] = one.astype(BF16)
            two = R[ch, j, qb, 2:4].astype(F32) + RB1[ch, 1, j].astype(F32)
            R[ch, j, qb, 2:4] = two.astype(BF16)
            copies += go(
                copy(R.at[ch, j, qn], RB2.at[ch, 0, j], right_q),
                copy(R.at[ch, j, qb], RB2.at[ch, 1, j], left_q),
            )
        return copies

    def rs_p(ch, copies):
        for j in range(3):
            done(copies[2 * j : 2 * j + 2])
            total = R[ch, j, q].astype(F32) + RB2[ch, 0, j].astype(F32) + RB2[ch, 1, j].astype(F32)
            S[ch, :, j] = total.astype(BF16)
        return go(
            *[copy(S.at[ch, (p + k + 1) % 4], RB3.at[ch, k], ring_p[k]) for k in range(3)]
        )

    def rs_last(ch, copies):
        done(copies)
        total = S[ch, p].astype(F32)
        for k in range(3):
            total = total + RB3[ch, k].astype(F32)
        for zz in range(2):
            both = [jnp.concatenate([total[j, zz, a] for j in range(3)], axis=1) for a in range(2)]
            for cc in range(2):
                rows = slice(8 * cc, 8 * cc + 8)
                tile = jnp.concatenate([both[0][rows], both[1][rows]], axis=0)
                TF[ch, zz, cc] = tile
                TZ[ch, zz, cc] = tile.astype(BF16)
            inner = jnp.sum(RA[zz, 1 - ch] * both[ch], axis=1, keepdims=True)
            HAs[ch, zz] = jnp.broadcast_to(inner, (16, D)).reshape(2, 8, D)
        place = ((zh, c), (zh, o), (1 - zh, c), (1 - zh, o))
        rows = go(
            *[copy(TZ.at[ch, zz, cc], RB4.at[ch, k], near[k]) for k, (zz, cc) in enumerate(place[1:])]
        )
        slot = HAr.at[ch, sender]
        HAr[ch, sender] = HAs[ch, zh, c]
        targets = [(place[0], to) for to in heads]
        for k in range(3):
            targets += [(place[k + 1], to) for to in [near[k]] + far[k]]
        return rows + go(*[copy(HAs.at[ch, zz, cc], slot, to) for (zz, cc), to in targets])

    def rs_end(ch, copies, slots):
        done(copies)
        mine = TF[ch, zh, c] + RB4[ch, 1].astype(F32)
        other = RB4[ch, 0].astype(F32) + RB4[ch, 2].astype(F32)
        for a, slot in enumerate(slots):
            sm[slot, :, half_of[0]] = mine[8 * a : 8 * a + 8]
            sm[slot, :, half_of[1]] = other[8 * a : 8 * a + 8]

    units = [(j, t) for j in range(3) for t in range(2)]

    def video_probs(h, part):
        j, t = part
        head = 3 * h + j
        tops = SV[0, head]
        weights = jnp.exp2(tops - jnp.max(tops, axis=0, keepdims=True))
        over = 1.0 / jnp.sum(weights * SV[1, head], axis=0, keepdims=True)
        weights = weights * over
        inner = jnp.sum(weights * SV[2, head], axis=0, keepdims=True)
        chunk = slice(256 * t, 256 * (t + 1))
        probs = jnp.concatenate(
            [EV[head, D * i : D * i + D, chunk] * weights[i : i + 1, chunk] for i in range(4)],
            axis=0,
        )
        ds = (probs * (DV[head, :, chunk] - inner[:, chunk])).astype(BF16)
        return probs.astype(BF16), ds

    def finish(ch, j, own):
        go(*(rs_q1(ch, j) if own else (cross(ch, j),)))

    def video_pass(h, own):
        sums = {}

        def use(part, made):
            j, t = part
            low, ds = made
            chunk, lanes = slice(256 * t, 256 * (t + 1)), lanes_of(3 * h + j)
            grads = dot(ds, vqn[chunk, lanes], NN), dot(low, vdo[chunk, lanes], NN)
            if t == 0:
                keys = jnp.transpose(some_rows(1, h, range(4), 1, j))
                values = jnp.transpose(some_rows(0, h, range(4), 0, j))
                sums[j] = grads + (keys, values)
            keys, values = sums[j][2:]
            video_out[chunk, lanes] = jnp.transpose(dot(values, low, NN)).astype(BF16)
            grad_q = jnp.transpose(dot(keys, ds, NN)) * FACTOR
            GQ[chunk, lanes] = grad_q
            IA[0, chunk] += vq[chunk, lanes].astype(F32) * gvq_gain[:, lanes] * grad_q
            if t == 0:
                return
            if own:
                cross(0, j).wait()
            put(0, j, own, slice(0, 4), 0, (sums[j][0] + grads[0]) * FACTOR)
            put(0, j, own, slice(0, 4), 1, sums[j][1] + grads[1])
            finish(0, j, own)

        staged(units, lambda part: video_probs(h, part), use)

    def inner_start(i):
        HI[i, hd] = jnp.zeros((8, 512), F32)
        HI[i, hd, 0:1, :] = row_of(IA[i])
        return go(*[copy(HI.at[i, hd], HI.at[i, hd], to) for to in heads])

    def video_final(i, copies, raw, gain, grad, out):
        done(copies)
        inner = (HI[i, 0] + HI[i, 1] + HI[i, 2] + HI[i, 3]) / WIDTH
        inv_i = inv_col[i]
        scale = inv_i * inv_i * inv_i * col(inner[0:1, :])
        for b in range(NH):
            at_b = slice(b * D, (b + 1) * D)
            value = inv_i * gain[:, at_b] * grad[:, at_b] - raw[:, at_b].astype(F32) * scale
            out[:, at_b] = value.astype(BF16)

    stats_merge(0, level0)
    level1 = stats_start(1, ring_p)
    video_pass(o, False)
    stats_merge(1, level1)
    level2 = stats_start(2, ring_q)
    video_pass(c, True)
    inner0 = inner_start(0)
    stats_merge(2, level2)

    total = ST[3, 1]
    safe = jnp.where(total == 0.0, 1.0, total)
    WT[0] = jnp.exp2(ST[0, 0] - ST[3, 0]) / safe
    WT[1] = ST[3, 2] / safe

    def audio_probs(h, part):
        j, t = part
        head = 3 * h + j
        row = pl.ds(head, 1)
        weight, shift = (
            jnp.concatenate([WT[n, 2 * t, row, :], WT[n, 2 * t + 1, row, :]], axis=1)
            for n in (0, 1)
        )
        chunk = slice(256 * t, 256 * (t + 1))
        probs = E[head, :, chunk] * weight
        ds = (probs * (DP[head, :, chunk] - shift)).astype(BF16)
        return probs.astype(BF16), ds

    def audio_pass(h, own):
        def use(part, made):
            j, t = part
            low, ds = made
            lanes = lanes_of(3 * h + j)
            chunks = slice(2 * t, 2 * t + 2)
            numer = jnp.transpose(dot(vvT[lanes, :], low, NN))
            grad_q = jnp.transpose(dot(vkT[lanes, :], ds, NN)) * FACTOR
            if own and t == 0:
                cross(1, j).wait()
            put(1, j, own, chunks, 0, numer)
            put(1, j, own, chunks, 1, grad_q)
            if t == 1:
                finish(1, j, own)

        staged(units, lambda part: audio_probs(h, part), use)

    def row_pass(h):
        sums = {}

        def use(part, made):
            j, t = part
            low, ds = made
            lanes = lanes_of(3 * h + j)
            ids = (2 * t, 2 * t + 1)
            grads = dot(ds, some_rows(1, h, ids, 0, j), NN), dot(low, some_rows(0, h, ids, 1, j), NN)
            if t == 0:
                sums[j] = grads
                return
            grad_k = (sums[j][0] + grads[0]) * FACTOR
            out_gvv[:, lanes] = (sums[j][1] + grads[1]).astype(BF16)
            GK[:, lanes] = grad_k
            IA[1] += vk[:, lanes].astype(F32) * gvk_gain[:, lanes] * grad_k

        staged(units, lambda part: audio_probs(h, part), use)

    audio_pass(o, False)
    a2 = rs_q2(0, (0, 1, 2))
    audio_pass(c, True)
    b2 = rs_q2(1, (0,))
    a3 = rs_p(0, a2)
    row_pass(0)
    b2 += rs_q2(1, (1, 2))
    a4 = rs_last(0, a3)
    row_pass(1)
    b3 = rs_p(1, b2)
    inner1 = inner_start(1)
    b4 = rs_last(1, b3)
    video_final(0, inner0, vq, gvq_gain, GQ, out_gvq)
    video_final(1, inner1, vk, gvk_gain, GK, out_gvk)
    rs_end(0, a4, (3, 4))
    rs_end(1, b4, (5, 2))
    out_small[0] = sm[5]
    out_small[3] = sm[4]
    parts = ((aq, gaq_gain, sm[2]), (ak, gak_gain, sm[3]))
    for i, (raw, gain, grad) in enumerate(parts):
        total = HAr[1 - i, 0]
        for k in range(1, 16):
            total = total + HAr[1 - i, k]
        total = total / WIDTH
        wide = jnp.concatenate([inv_a[i]] * NH, axis=1)
        scale = jnp.concatenate([inv_a[i] * inv_a[i] * inv_a[i] * total] * NH, axis=1)
        out_small[1 + i] = wide * gain[...] * grad - raw[...].astype(F32) * scale


def write_kernel(
    a, b, c, d, small, out_a, out_b, out_c, out_d, small_0, small_1, small_2, small_3, sems
):
    parts = ROWS // 4
    copies = []
    for i, (src, dst) in enumerate(((a, out_a), (b, out_b), (c, out_c), (d, out_d))):
        for k in range(4):
            rows = slice(k * parts, (k + 1) * parts)
            copies.append(pltpu.make_async_copy(src.at[rows], dst.at[rows], sems.at[4 * i + k]))
    for one in copies:
        one.start()
    for i, out in enumerate((small_0, small_1, small_2, small_3)):
        out[...] = small[i].astype(BF16)
    for one in copies:
        one.wait()


def shards(*args):
    big = jax.ShapeDtypeStruct((ROWS, LOCAL), BF16)
    vmem = pltpu.VMEM
    wide = vmem((ROWS, LOCAL), BF16)
    scratch = [wide] * 4 + [
        vmem((8, LOCAL), F32),
        vmem((2, 2, 16, HALF), F32),
        vmem((2, 2, 4, 4, 2, 2, 16, HALF), BF16),
        vmem((2, 2, 16, HALF), BF16),
        vmem((2, 3, 16, HALF), BF16),
        vmem((16, 2, 8, D), F32),
        vmem((4, 8, 512), F32),
        vmem((2, 4, 8, 512), F32),
        vmem((2, 2, 2, 8, D), F32),
        vmem((2, 16, 8, D), F32),
        vmem((ROWS, LOCAL), BF16),
        vmem((ROWS, LOCAL), BF16),
        vmem((LOCAL, ROWS), BF16),
        vmem((LOCAL, ROWS), BF16),
        vmem((2, ROWS, D), F32),
        vmem((NH, ROWS, TOK), F32),
        vmem((NH, ROWS, TOK), F32),
        vmem((NH, TOK, ROWS), F32),
        vmem((NH, TOK, ROWS), F32),
        vmem((3, NH, 4, ROWS), F32),
        vmem((4, 3, 4, 8, D), F32),
        vmem((3, 3, 3, 4, 8, D), F32),
        vmem((2, 4, 8, D), F32),
        vmem((ROWS, LOCAL), F32),
        vmem((ROWS, LOCAL), F32),
        vmem((2, ROWS, D), F32),
        vmem((2, 3, 2, TOK, D), BF16),
        vmem((2, 3, 2, TOK, D), BF16),
        vmem((2, 3, 4, 4, 2, 2, 16, D), BF16),
        vmem((2, 2, 3, 2, 2, 2, 16, D), BF16),
        vmem((2, 2, 3, 4, 2, 2, 16, D), BF16),
        vmem((2, 4, 3, 2, 2, 16, D), BF16),
        vmem((2, 3, 3, 2, 2, 16, D), BF16),
        vmem((2, 2, 2, 16, HALF), F32),
        vmem((2, 2, 2, 16, HALF), BF16),
        vmem((2, 3, 16, HALF), BF16),
        vmem((6, 8, LOCAL), F32),
        pltpu.SemaphoreType.DMA((160,)),
        pltpu.SemaphoreType.DMA((160,)),
        pltpu.SemaphoreType.DMA((8,)),
    ]
    spec = pl.BlockSpec(memory_space=pltpu.VMEM)
    anywhere = pl.BlockSpec(memory_space=pl.ANY)
    made = pl.pallas_call(
        kernel,
        out_shape=(vmem((ROWS, LOCAL), BF16),) * 4 + (vmem((4, 8, LOCAL), F32),),
        in_specs=[anywhere] * 4 + [spec] * 8,
        out_specs=(spec,) * 5,
        scratch_shapes=scratch,
        compiler_params=pltpu.CompilerParams(
            collective_id=0, has_side_effects=True, vmem_limit_bytes=57 * 1024 * 1024
        ),
    )(*args)
    small = jax.ShapeDtypeStruct((8, LOCAL), BF16)
    wrote = pl.pallas_call(
        write_kernel,
        out_shape=(big,) * 4 + (small,) * 4,
        in_specs=[spec] * 5,
        out_specs=(anywhere,) * 4 + (spec,) * 4,
        scratch_shapes=[pltpu.SemaphoreType.DMA((16,))],
        compiler_params=pltpu.CompilerParams(vmem_limit_bytes=4 * 1024 * 1024),
    )(*[pltpu.with_memory_space_constraint(one, pltpu.VMEM) for one in made])
    video_out, gvq, gvk, gvv, audio_out, gaq, gak, gav = wrote
    return video_out, audio_out, gvq, gvk, gvv, gaq, gak, gav


def solution(mesh):
    both = P("seq", "head")
    return jax.shard_map(
        shards,
        mesh=mesh,
        in_specs=(both,) * 8 + (P("head"),) * 4,
        out_specs=(both,) * 8,
        check_vma=False,
    )
```

```python
import math

import jax
import jax.numpy as jnp
from jax import lax
from jax.experimental import pallas as pl
from jax.experimental.pallas import tpu as pltpu
from jax.sharding import PartitionSpec as P

HEADS = 24
D = 128
WIDTH = HEADS * D
EPS = 1e-06
FACTOR = 1.0 / math.sqrt(D)
KLOG = FACTOR * math.log2(math.e)
ROWS = 512
TOK = 512
LOCAL = 768
HALF = 384
NH = 6
F32 = jnp.float32
BF16 = jnp.bfloat16
MESH = pl.DeviceIdType.MESH
NT = (((1,), (1,)), ((), ()))
TN = (((0,), (0,)), ((), ()))
NN = (((1,), (0,)), ((), ()))


def dot(a, b, dims):
    return lax.dot_general(a, b, dims, preferred_element_type=F32)


def col(row):
    return jnp.transpose(jnp.broadcast_to(row, (D, ROWS)))


def row_of(square):
    return jnp.sum(jnp.transpose(square), axis=0, keepdims=True)


def fold(op, array):
    while array.shape[0] > 8:
        half = array.shape[0] // 2
        array = op(array[:half], array[half:])
    if op is jnp.maximum:
        return jnp.max(array, axis=0, keepdims=True)
    return jnp.sum(array, axis=0, keepdims=True)


def kernel(
    vq_in, vk_in, vv_in, vdo_in, aq, ak, av, ado, gain0, gain1, gain2, gain3,
    video_out, out_gvq, out_gvk, out_gvv, out_small,
    vq, vk, vv, vdo, GN, RA,
    G, PK, PR, HSA, HS, HI, HAs, HAr, vqn, vkn, inv_col, E, DP, EV, DV, SV, ST, SR, WT,
    GQ, GK, IA, Xs, Xr, R, RB1, RB2, S, RB3, TF, TZ, RB4, sm,
    send, recv, local,
):
    s = lax.axis_index("seq")
    hd = lax.axis_index("head")
    c = s % 2
    y = (s // 2) % 4
    x = (s // 8) % 4
    zh = s // 32
    p = x + c * (y - x)
    q = y + c * (x - y)
    o = 1 - c

    def at(zz, pp, qq):
        xx = pp + c * (qq - pp)
        yy = qq + c * (pp - qq)
        return {"seq": ((zz * 4 + xx) * 4 + yy) * 2 + c}

    sib = {"seq": s + 1 - 2 * c}
    opp = at(1 - zh, p, q)
    opp_sib = {"seq": s + 1 - 2 * c + 32 - 64 * zh}
    ring_p = [at(zh, (p + k) % 4, q) for k in (1, 2, 3)]
    ring_q = [at(zh, p, (q + k) % 4) for k in (1, 2, 3)]
    heads = [{"head": (hd + k) % 4} for k in (1, 2, 3)]
    near = [sib, opp, opp_sib]
    far = [[dict(to, head=(hd + k) % 4) for k in (1, 2, 3)] for to in near]
    pn, pb, p2 = (p + 1) % 4, (p + 3) % 4, (p + 2) % 4
    qn, qb, q2 = (q + 1) % 4, (q + 3) % 4, (q + 2) % 4
    right_q, left_q = ring_q[0], ring_q[2]

    barrier = pltpu.get_barrier_semaphore()
    partners = near + ring_p + ring_q + heads + far[0] + far[1] + far[2]
    for partner in partners:
        pl.semaphore_signal(barrier, inc=1, device_id=partner, device_id_type=MESH)
    loads = [
        pltpu.make_async_copy(src, dst, local.at[i])
        for i, (src, dst) in enumerate(((vq_in, vq), (vk_in, vk), (vv_in, vv), (vdo_in, vdo)))
    ]
    for one in loads:
        one.start()
    for i, gain in enumerate((gain0, gain1, gain2, gain3)):
        GN[i : i + 1, :] = gain[...].reshape(1, LOCAL)
    gvq_gain, gvk_gain, gaq_gain, gak_gain = (GN.at[i : i + 1] for i in range(4))

    count = [0]

    def slots(n):
        first = count[0]
        count[0] += n
        return first

    def copy(src, dst, to, slot=None):
        slot = slots(1) if slot is None else slot
        return pltpu.make_async_remote_copy(
            src_ref=src,
            dst_ref=dst,
            send_sem=send.at[slot],
            recv_sem=recv.at[slot],
            device_id=to,
            device_id_type=MESH,
        )

    def go(*copies):
        for one in copies:
            one.start()
        return copies

    def done(copies):
        for one in copies:
            one.wait()

    half_of = [pl.ds(pl.multiple_of(i * HALF, D), HALF) for i in (c, o)]

    def pack(n, refs):
        for i, half in enumerate(half_of):
            rows = [ref[:, half].astype(F32) for ref in refs]
            PK[n, i] = jnp.concatenate(rows, axis=0).astype(BF16)

    def ag_first(n):
        return go(
            copy(PK.at[n, 1], PR.at[n, 0], sib),
            copy(PK.at[n, 0], PR.at[n, 1], opp),
            copy(PK.at[n, 1], PR.at[n, 2], opp_sib),
        )

    def chip_rows(mine, other, a):
        mine = mine.astype(F32)[8 * a : 8 * a + 8]
        other = other.astype(F32)[8 * a : 8 * a + 8]
        low = jnp.where(c == 0, mine, other)
        high = jnp.where(c == 0, other, mine)
        return jnp.concatenate([low, high], axis=0)

    def ag_p(ch):
        block = G.at[c, ch, q, p]
        return go(*[copy(block, block, to) for to in ring_p])

    base_f = slots(8)

    def forward(ch, n):
        i = (q + n + (n // 2) * (5 - 2 * n)) % 4
        block = G.at[c, ch, i]
        return copy(block, block, sib, slot=base_f + 4 * ch + n)

    def ag_q1(ch, copies):
        done(copies)
        block = G.at[c, ch, q]
        return go(copy(block, block, right_q), copy(block, block, left_q))

    def ag_q2(ch, copies):
        done(copies)
        one, two = G.at[c, ch, qb, 0:2], G.at[c, ch, qn, 2:4]
        return go(copy(one, one, right_q), copy(two, two, left_q))

    pack(0, (av, ado))
    pack(1, (aq, ak))
    sender = 4 * hd + 2 * zh + c
    for i, raw in enumerate((aq, ak)):
        block = raw[...].astype(F32)
        total = jnp.sum(block * block, axis=1, keepdims=True)
        HSA[sender, i] = jnp.broadcast_to(total, (8, D))
    pl.semaphore_wait(barrier, len(partners))
    first0 = ag_first(0)
    first1 = ag_first(1)
    mine = HSA.at[sender]
    first1 += go(*[copy(mine, mine, to) for to in near + heads + far[0] + far[1] + far[2]])

    HS[hd] = jnp.zeros((8, 512), F32)
    for i, raw in enumerate((vq, vk)):
        loads[i].wait()
        total = jnp.zeros((ROWS, D), F32)
        for b in range(NH):
            block = raw[:, b * D : (b + 1) * D].astype(F32)
            total = total + block * block
        HS[hd, i : i + 1, :] = row_of(total)
    sums = go(*[copy(HS.at[hd], HS.at[hd], to) for to in heads])

    done(first0)
    for a in range(2):
        G[c, 0, q, p, zh, a] = chip_rows(PK[0, 0], PR[0, 0], a).astype(BF16)
        G[c, 0, q, p, 1 - zh, a] = chip_rows(PR[0, 1], PR[0, 2], a).astype(BF16)
    ring0 = ag_p(0)

    done(first1)

    def inverse(zz, cc, i):
        total = HSA[2 * zz + cc, i]
        for k in range(1, 4):
            total = total + HSA[4 * k + 2 * zz + cc, i]
        return lax.rsqrt(total / WIDTH + EPS)

    for i, gain in enumerate((gaq_gain, gak_gain)):
        raws = chip_rows(PK[1, 0], PR[1, 0], i), chip_rows(PR[1, 1], PR[1, 2], i)
        for zz, raw in zip((zh, 1 - zh), raws):
            inv_row = jnp.concatenate([inverse(zz, cc, i) for cc in range(2)], axis=0)
            wide = jnp.concatenate([inv_row] * 3, axis=1)
            half = gain[:, half_of[0]]
            G[c, 1, q, p, zz, i] = (raw * wide * half).astype(BF16)
            RA[zz, i] = raw * half
    ring1 = ag_p(1)
    inv_a = [inverse(zh, c, i) for i in range(2)]

    loads[2].wait()
    done(sums)
    total = HS[0] + HS[1] + HS[2] + HS[3]
    inv = lax.rsqrt(total / WIDTH + EPS)

    def norm_video(i, raw, gain, out):
        inv_col[i] = col(inv[i : i + 1, :])
        for b in range(NH):
            at_b = slice(b * D, (b + 1) * D)
            out[:, at_b] = (raw[:, at_b].astype(F32) * inv_col[i] * gain[:, at_b]).astype(BF16)

    norm_video(1, vk, gvk_gain, vkn)
    q10 = ag_q1(0, ring0)
    go(forward(0, 0))
    norm_video(0, vq, gvq_gain, vqn)
    q11 = ag_q1(1, ring1)
    go(forward(1, 0))

    def lanes_of(i):
        return pl.ds(pl.multiple_of(i * D, D), D)

    ST[...] = jnp.zeros_like(ST)

    def staged(units, make, use):
        held = None
        for unit in units:
            made = make(unit)
            if held is not None:
                use(*held)
            held = (unit, made)
        use(*held)

    def rows_of(ch, h, i, a, j):
        return G[h, ch, i, :, :, a, :, j * D : j * D + D].reshape(D, D)

    def some_rows(ch, h, ids, a, j):
        return jnp.concatenate([rows_of(ch, h, i, a, j) for i in ids], axis=0)

    def video(h, *ids):
        def make(j):
            lanes = lanes_of(3 * h + j)
            scores = dot(some_rows(1, h, ids, 1, j), vqn[:, lanes], NT) * KLOG
            return scores, dot(some_rows(0, h, ids, 0, j), vdo[:, lanes], NT)

        def use(j, made):
            scores, dprob = made
            head = 3 * h + j
            top = fold(jnp.maximum, scores)
            expo = jnp.exp2(scores - top)
            nothing = jnp.zeros_like(top)
            values = [top, fold(jnp.add, expo), fold(jnp.add, expo * dprob)]
            for n, i in enumerate(ids):
                part = slice(D * n, D * n + D)
                EV[head, lanes_of(i), :] = expo[part]
                DV[head, lanes_of(i), :] = dprob[part]
                for k in range(3):
                    SV[k, head, pl.ds(i, 1), :] = nothing if n and k else values[k]

        staged(range(3), make, use)

    def audio(h, *ids):
        def make(j):
            lanes = lanes_of(3 * h + j)
            scores = dot(vkn[:, lanes], some_rows(1, h, ids, 0, j), NT) * KLOG
            return scores, dot(vv[:, lanes], some_rows(0, h, ids, 1, j), NT)

        def use(j, made):
            scores, dprob = made
            head = 3 * h + j
            top = fold(jnp.maximum, scores)
            expo = jnp.exp2(scores - top)
            values = [top, fold(jnp.add, expo), fold(jnp.add, expo * dprob)]
            for n, i in enumerate(ids):
                part = slice(D * n, D * n + D)
                E[head, :, lanes_of(i)] = expo[:, part]
                DP[head, :, lanes_of(i)] = dprob[:, part]
                for k in range(3):
                    ST[0, k, i, pl.ds(head, 1), :] = values[k][:, part]

        staged(range(3), make, use)

    def pair(n):
        return (p + 3 * n) % 4, (p + 1 + n) % 4

    def twice(body):
        def step(n, carry):
            body(n)
            return carry

        lax.fori_loop(0, 2, step, 0)

    audio(c, q)
    loads[3].wait()
    video(c, q)
    q20 = ag_q2(0, q10)
    go(*[forward(0, n) for n in (1, 2)])
    q21 = ag_q2(1, q11)
    go(*[forward(1, n) for n in (1, 2)])
    audio(c, qn, qb)
    done(q20)
    go(forward(0, 3))
    done(q21)
    go(forward(1, 3))
    video(c, qn, qb)
    audio(c, q2)

    def their_audio(n):
        done([forward(ch, 2 * n + k) for ch in range(2) for k in range(2)])
        audio(o, *pair(n))

    twice(their_audio)

    def stats_start(level, to):
        return go(*[copy(ST.at[level], SR.at[level, k], one) for k, one in enumerate(to)])

    def stats_merge(level, copies):
        done(copies)
        tops = [ST[level, 0]] + [SR[level, k, 0] for k in range(3)]
        top = jnp.maximum(jnp.maximum(tops[0], tops[1]), jnp.maximum(tops[2], tops[3]))
        weights = [jnp.exp2(one - top) for one in tops]
        ST[level + 1, 0] = top
        for n in (1, 2):
            total = ST[level, n] * weights[0]
            for k in range(3):
                total = total + SR[level, k, n] * weights[k + 1]
            ST[level + 1, n] = total

    level0 = stats_start(0, (sib, opp, opp_sib))
    video(c, q2)
    twice(lambda n: video(o, *pair(n)))

    IA[...] = jnp.zeros_like(IA)
    base_cross = slots(6)

    def cross(ch, j):
        return copy(Xs.at[ch, j], Xr.at[ch, j], sib, slot=base_cross + 3 * ch + j)

    def put(ch, j, own, chunks, a, value):
        rows = slice(128 * chunks.start, 128 * chunks.stop)
        if own:
            value = value + Xr[ch, j, a, rows].astype(F32)
            shape = (chunks.stop - chunks.start, 4, 2, 16, D)
            R[ch, j, chunks, :, :, a] = value.reshape(shape).astype(BF16)
        else:
            Xs[ch, j, a, rows] = value.astype(BF16)

    base_q1 = slots(12)

    def rs_q1(ch, j):
        slot = base_q1 + 6 * ch + 2 * j
        return (
            copy(R.at[ch, j, q2, 0:2], RB1.at[ch, 0, j], right_q, slot=slot),
            copy(R.at[ch, j, q2, 2:4], RB1.at[ch, 1, j], left_q, slot=slot + 1),
        )

    def rs_q2(ch, heads_done):
        copies = []
        for j in heads_done:
            done(rs_q1(ch, j))
            one = R[ch, j, qn, 0:2].astype(F32) + RB1[ch, 0, j].astype(F32)
            R[ch, j, qn, 0:2] = one.astype(BF16)
            two = R[ch, j, qb, 2:4].astype(F32) + RB1[ch, 1, j].astype(F32)
            R[ch, j, qb, 2:4] = two.astype(BF16)
            copies += go(
                copy(R.at[ch, j, qn], RB2.at[ch, 0, j], right_q),
                copy(R.at[ch, j, qb], RB2.at[ch, 1, j], left_q),
            )
        return copies

    def rs_p(ch, copies):
        for j in range(3):
            done(copies[2 * j : 2 * j + 2])
            total = R[ch, j, q].astype(F32) + RB2[ch, 0, j].astype(F32) + RB2[ch, 1, j].astype(F32)
            S[ch, :, j] = total.astype(BF16)
        return go(
            *[copy(S.at[ch, (p + k + 1) % 4], RB3.at[ch, k], ring_p[k]) for k in range(3)]
        )

    def rs_last(ch, copies):
        done(copies)
        total = S[ch, p].astype(F32)
        for k in range(3):
            total = total + RB3[ch, k].astype(F32)
        for zz in range(2):
            both = [jnp.concatenate([total[j, zz, a] for j in range(3)], axis=1) for a in range(2)]
            for cc in range(2):
                rows = slice(8 * cc, 8 * cc + 8)
                tile = jnp.concatenate([both[0][rows], both[1][rows]], axis=0)
                TF[ch, zz, cc] = tile
                TZ[ch, zz, cc] = tile.astype(BF16)
            inner = jnp.sum(RA[zz, 1 - ch] * both[ch], axis=1, keepdims=True)
            HAs[zz, :, ch] = jnp.broadcast_to(inner, (16, D)).reshape(2, 8, D)
        place = ((zh, c), (zh, o), (1 - zh, c), (1 - zh, o))
        rows = go(
            *[copy(TZ.at[ch, zz, cc], RB4.at[ch, k], near[k]) for k, (zz, cc) in enumerate(place[1:])]
        )
        if ch == 0:
            return rows
        slot = HAr.at[sender]
        HAr[sender] = HAs[zh, c]
        targets = [(place[0], to) for to in heads]
        for k in range(3):
            targets += [(place[k + 1], to) for to in [near[k]] + far[k]]
        return rows + go(*[copy(HAs.at[zz, cc], slot, to) for (zz, cc), to in targets])

    def rs_end(ch, copies, slots):
        done(copies)
        mine = TF[ch, zh, c] + RB4[ch, 1].astype(F32)
        other = RB4[ch, 0].astype(F32) + RB4[ch, 2].astype(F32)
        for a, slot in enumerate(slots):
            sm[slot, :, half_of[0]] = mine[8 * a : 8 * a + 8]
            sm[slot, :, half_of[1]] = other[8 * a : 8 * a + 8]

    units = [(j, t) for j in range(3) for t in range(2)]

    def video_probs(h, part):
        j, t = part
        head = 3 * h + j
        tops = SV[0, head]
        weights = jnp.exp2(tops - jnp.max(tops, axis=0, keepdims=True))
        over = 1.0 / jnp.sum(weights * SV[1, head], axis=0, keepdims=True)
        weights = weights * over
        inner = jnp.sum(weights * SV[2, head], axis=0, keepdims=True)
        chunk = slice(256 * t, 256 * (t + 1))
        probs = jnp.concatenate(
            [EV[head, D * i : D * i + D, chunk] * weights[i : i + 1, chunk] for i in range(4)],
            axis=0,
        )
        ds = (probs * (DV[head, :, chunk] - inner[:, chunk])).astype(BF16)
        return probs.astype(BF16), ds

    def finish(ch, j, own):
        go(*(rs_q1(ch, j) if own else (cross(ch, j),)))

    def video_pass(h, own):
        sums = {}

        def use(part, made):
            j, t = part
            low, ds = made
            chunk, lanes = slice(256 * t, 256 * (t + 1)), lanes_of(3 * h + j)
            grads = dot(ds, vqn[chunk, lanes], NN), dot(low, vdo[chunk, lanes], NN)
            if t == 0:
                keys, values = some_rows(1, h, range(4), 1, j), some_rows(0, h, range(4), 0, j)
                sums[j] = grads + (keys, values)
            keys, values = sums[j][2:]
            video_out[chunk, lanes] = dot(low, values, TN).astype(BF16)
            grad_q = dot(ds, keys, TN) * FACTOR
            GQ[chunk, lanes] = grad_q
            IA[0, chunk] += vq[chunk, lanes].astype(F32) * gvq_gain[:, lanes] * grad_q
            if t == 0:
                return
            if own:
                cross(0, j).wait()
            put(0, j, own, slice(0, 4), 0, (sums[j][0] + grads[0]) * FACTOR)
            put(0, j, own, slice(0, 4), 1, sums[j][1] + grads[1])
            finish(0, j, own)

        staged(units, lambda part: video_probs(h, part), use)

    def inner_start(i):
        HI[i, hd] = jnp.zeros((8, 512), F32)
        HI[i, hd, 0:1, :] = row_of(IA[i])
        return go(*[copy(HI.at[i, hd], HI.at[i, hd], to) for to in heads])

    def video_final(i, copies, raw, gain, grad, out):
        done(copies)
        inner = (HI[i, 0] + HI[i, 1] + HI[i, 2] + HI[i, 3]) / WIDTH
        inv_i = inv_col[i]
        scale = inv_i * inv_i * inv_i * col(inner[0:1, :])
        for b in range(NH):
            at_b = slice(b * D, (b + 1) * D)
            value = inv_i * gain[:, at_b] * grad[:, at_b] - raw[:, at_b].astype(F32) * scale
            out[:, at_b] = value.astype(BF16)

    stats_merge(0, level0)
    level1 = stats_start(1, ring_p)
    video_pass(o, False)
    stats_merge(1, level1)
    level2 = stats_start(2, ring_q)
    video_pass(c, True)
    inner0 = inner_start(0)
    stats_merge(2, level2)

    total = ST[3, 1]
    safe = jnp.where(total == 0.0, 1.0, total)
    WT[0] = jnp.exp2(ST[0, 0] - ST[3, 0]) / safe
    WT[1] = ST[3, 2] / safe

    def audio_probs(h, part):
        j, t = part
        head = 3 * h + j
        row = pl.ds(head, 1)
        weight, shift = (
            jnp.concatenate([WT[n, 2 * t, row, :], WT[n, 2 * t + 1, row, :]], axis=1)
            for n in (0, 1)
        )
        chunk = slice(256 * t, 256 * (t + 1))
        probs = E[head, :, chunk] * weight
        ds = (probs * (DP[head, :, chunk] - shift)).astype(BF16)
        return probs.astype(BF16), ds

    def audio_pass(h, own):
        def use(part, made):
            j, t = part
            low, ds = made
            lanes = lanes_of(3 * h + j)
            chunks = slice(2 * t, 2 * t + 2)
            numer = dot(low, vv[:, lanes], TN)
            grad_q = dot(ds, vkn[:, lanes], TN) * FACTOR
            if own and t == 0:
                cross(1, j).wait()
            put(1, j, own, chunks, 0, numer)
            put(1, j, own, chunks, 1, grad_q)
            if t == 1:
                finish(1, j, own)

        staged(units, lambda part: audio_probs(h, part), use)

    def row_pass(h):
        sums = {}

        def use(part, made):
            j, t = part
            low, ds = made
            lanes = lanes_of(3 * h + j)
            ids = (2 * t, 2 * t + 1)
            grads = dot(ds, some_rows(1, h, ids, 0, j), NN), dot(low, some_rows(0, h, ids, 1, j), NN)
            if t == 0:
                sums[j] = grads
                return
            grad_k = (sums[j][0] + grads[0]) * FACTOR
            out_gvv[:, lanes] = (sums[j][1] + grads[1]).astype(BF16)
            GK[:, lanes] = grad_k
            IA[1] += vk[:, lanes].astype(F32) * gvk_gain[:, lanes] * grad_k

        staged(units, lambda part: audio_probs(h, part), use)

    audio_pass(o, False)
    a2 = rs_q2(0, (0, 1, 2))
    audio_pass(c, True)
    b2 = rs_q2(1, (0,))
    a3 = rs_p(0, a2)
    row_pass(0)
    b2 += rs_q2(1, (1, 2))
    a4 = rs_last(0, a3)
    row_pass(1)
    b3 = rs_p(1, b2)
    inner1 = inner_start(1)
    b4 = rs_last(1, b3)
    video_final(0, inner0, vq, gvq_gain, GQ, out_gvq)
    video_final(1, inner1, vk, gvk_gain, GK, out_gvk)
    rs_end(0, a4, (3, 4))
    rs_end(1, b4, (5, 2))
    out_small[0] = sm[5]
    out_small[3] = sm[4]
    parts = ((aq, gaq_gain, sm[2]), (ak, gak_gain, sm[3]))
    for i, (raw, gain, grad) in enumerate(parts):
        total = HAr[0, 1 - i]
        for k in range(1, 16):
            total = total + HAr[k, 1 - i]
        total = total / WIDTH
        wide = jnp.concatenate([inv_a[i]] * NH, axis=1)
        scale = jnp.concatenate([inv_a[i] * inv_a[i] * inv_a[i] * total] * NH, axis=1)
        out_small[1 + i] = wide * gain[...] * grad - raw[...].astype(F32) * scale


def write_kernel(
    a, b, c, d, small, out_a, out_b, out_c, out_d, small_0, small_1, small_2, small_3, sems
):
    parts = ROWS // 4
    copies = []
    for i, (src, dst) in enumerate(((a, out_a), (b, out_b), (c, out_c), (d, out_d))):
        for k in range(4):
            rows = slice(k * parts, (k + 1) * parts)
            copies.append(pltpu.make_async_copy(src.at[rows], dst.at[rows], sems.at[4 * i + k]))
    for one in copies:
        one.start()
    for i, out in enumerate((small_0, small_1, small_2, small_3)):
        out[...] = small[i].astype(BF16)
    for one in copies:
        one.wait()


def shards(*args):
    big = jax.ShapeDtypeStruct((ROWS, LOCAL), BF16)
    vmem = pltpu.VMEM
    wide = vmem((ROWS, LOCAL), BF16)
    scratch = [wide] * 4 + [
        vmem((8, LOCAL), F32),
        vmem((2, 2, 16, HALF), F32),
        vmem((2, 2, 4, 4, 2, 2, 16, HALF), BF16),
        vmem((2, 2, 16, HALF), BF16),
        vmem((2, 3, 16, HALF), BF16),
        vmem((16, 2, 8, D), F32),
        vmem((4, 8, 512), F32),
        vmem((2, 4, 8, 512), F32),
        vmem((2, 2, 2, 8, D), F32),
        vmem((16, 2, 8, D), F32),
        vmem((ROWS, LOCAL), BF16),
        vmem((ROWS, LOCAL), BF16),
        vmem((2, ROWS, D), F32),
        vmem((NH, ROWS, TOK), F32),
        vmem((NH, ROWS, TOK), F32),
        vmem((NH, TOK, ROWS), F32),
        vmem((NH, TOK, ROWS), F32),
        vmem((3, NH, 4, ROWS), F32),
        vmem((4, 3, 4, 8, D), F32),
        vmem((3, 3, 3, 4, 8, D), F32),
        vmem((2, 4, 8, D), F32),
        vmem((ROWS, LOCAL), F32),
        vmem((ROWS, LOCAL), F32),
        vmem((2, ROWS, D), F32),
        vmem((2, 3, 2, TOK, D), BF16),
        vmem((2, 3, 2, TOK, D), BF16),
        vmem((2, 3, 4, 4, 2, 2, 16, D), BF16),
        vmem((2, 2, 3, 2, 2, 2, 16, D), BF16),
        vmem((2, 2, 3, 4, 2, 2, 16, D), BF16),
        vmem((2, 4, 3, 2, 2, 16, D), BF16),
        vmem((2, 3, 3, 2, 2, 16, D), BF16),
        vmem((2, 2, 2, 16, HALF), F32),
        vmem((2, 2, 2, 16, HALF), BF16),
        vmem((2, 3, 16, HALF), BF16),
        vmem((6, 8, LOCAL), F32),
        pltpu.SemaphoreType.DMA((160,)),
        pltpu.SemaphoreType.DMA((160,)),
        pltpu.SemaphoreType.DMA((8,)),
    ]
    spec = pl.BlockSpec(memory_space=pltpu.VMEM)
    anywhere = pl.BlockSpec(memory_space=pl.ANY)
    made = pl.pallas_call(
        kernel,
        out_shape=(vmem((ROWS, LOCAL), BF16),) * 4 + (vmem((4, 8, LOCAL), F32),),
        in_specs=[anywhere] * 4 + [spec] * 8,
        out_specs=(spec,) * 5,
        scratch_shapes=scratch,
        compiler_params=pltpu.CompilerParams(
            collective_id=0, has_side_effects=True, vmem_limit_bytes=57 * 1024 * 1024
        ),
    )(*args)
    small = jax.ShapeDtypeStruct((8, LOCAL), BF16)
    wrote = pl.pallas_call(
        write_kernel,
        out_shape=(big,) * 4 + (small,) * 4,
        in_specs=[spec] * 5,
        out_specs=(anywhere,) * 4 + (spec,) * 4,
        scratch_shapes=[pltpu.SemaphoreType.DMA((16,))],
        compiler_params=pltpu.CompilerParams(vmem_limit_bytes=4 * 1024 * 1024),
    )(*[pltpu.with_memory_space_constraint(one, pltpu.VMEM) for one in made])
    video_out, gvq, gvk, gvv, audio_out, gaq, gak, gav = wrote
    return video_out, audio_out, gvq, gvk, gvv, gaq, gak, gav


def solution(mesh):
    both = P("seq", "head")
    return jax.shard_map(
        shards,
        mesh=mesh,
        in_specs=(both,) * 8 + (P("head"),) * 4,
        out_specs=(both,) * 8,
        check_vma=False,
    )
```

```python
import math

import jax
import jax.numpy as jnp
from jax import lax
from jax.experimental import pallas as pl
from jax.experimental.pallas import tpu as pltpu
from jax.sharding import PartitionSpec as P

HEADS = 24
D = 128
WIDTH = HEADS * D
EPS = 1e-06
FACTOR = 1.0 / math.sqrt(D)
KLOG = FACTOR * math.log2(math.e)
ROWS = 512
TOK = 512
LOCAL = 768
HALF = 384
NH = 6
F32 = jnp.float32
BF16 = jnp.bfloat16
MESH = pl.DeviceIdType.MESH
NT = (((1,), (1,)), ((), ()))
TN = (((0,), (0,)), ((), ()))
NN = (((1,), (0,)), ((), ()))


def dot(a, b, dims):
    return lax.dot_general(a, b, dims, preferred_element_type=F32)


def col(row):
    return jnp.transpose(jnp.broadcast_to(row, (D, ROWS)))


def row_of(square):
    return jnp.sum(jnp.transpose(square), axis=0, keepdims=True)


def fold(op, array):
    while array.shape[0] > 8:
        half = array.shape[0] // 2
        array = op(array[:half], array[half:])
    if op is jnp.maximum:
        return jnp.max(array, axis=0, keepdims=True)
    return jnp.sum(array, axis=0, keepdims=True)


def kernel(
    vq_in, vk_in, vv_in, vdo_in, aq, ak, av, ado, gain0, gain1, gain2, gain3,
    video_out, out_gvq, out_gvk, out_gvv, out_small,
    vq, vk, vv, vdo, GN, RA,
    G, PK, PR, HSA, HS, HI, HAs, HAr, vqn, vkn, vvT, vkT, inv_col, E, DP, EV, DV, SV, ST, SR, WT,
    GQ, GK, IA, Xs, Xr, R, RB1, RB2, S, RB3, TF, TZ, RB4, sm,
    send, recv, local,
):
    s = lax.axis_index("seq")
    hd = lax.axis_index("head")
    c = s % 2
    y = (s // 2) % 4
    x = (s // 8) % 4
    zh = s // 32
    p = x + c * (y - x)
    q = y + c * (x - y)
    o = 1 - c

    def at(zz, pp, qq):
        xx = pp + c * (qq - pp)
        yy = qq + c * (pp - qq)
        return {"seq": ((zz * 4 + xx) * 4 + yy) * 2 + c}

    sib = {"seq": s + 1 - 2 * c}
    opp = at(1 - zh, p, q)
    opp_sib = {"seq": s + 1 - 2 * c + 32 - 64 * zh}
    ring_p = [at(zh, (p + k) % 4, q) for k in (1, 2, 3)]
    ring_q = [at(zh, p, (q + k) % 4) for k in (1, 2, 3)]
    heads = [{"head": (hd + k) % 4} for k in (1, 2, 3)]
    near = [sib, opp, opp_sib]
    far = [[dict(to, head=(hd + k) % 4) for k in (1, 2, 3)] for to in near]
    pn, pb, p2 = (p + 1) % 4, (p + 3) % 4, (p + 2) % 4
    qn, qb, q2 = (q + 1) % 4, (q + 3) % 4, (q + 2) % 4
    right_q, left_q = ring_q[0], ring_q[2]

    loads = [
        pltpu.make_async_copy(src, dst, local.at[i])
        for i, (src, dst) in enumerate(((vq_in, vq), (vk_in, vk), (vv_in, vv), (vdo_in, vdo)))
    ]
    for one in loads:
        one.start()
    barrier = pltpu.get_barrier_semaphore()
    partners = near + ring_p + ring_q + heads + far[0] + far[1] + far[2]
    for partner in partners:
        pl.semaphore_signal(barrier, inc=1, device_id=partner, device_id_type=MESH)
    for i, gain in enumerate((gain0, gain1, gain2, gain3)):
        GN[i : i + 1, :] = gain[...].reshape(1, LOCAL)
    gvq_gain, gvk_gain, gaq_gain, gak_gain = (GN.at[i : i + 1] for i in range(4))

    count = [0]

    def slots(n):
        first = count[0]
        count[0] += n
        return first

    def copy(src, dst, to, slot=None):
        slot = slots(1) if slot is None else slot
        return pltpu.make_async_remote_copy(
            src_ref=src,
            dst_ref=dst,
            send_sem=send.at[slot],
            recv_sem=recv.at[slot],
            device_id=to,
            device_id_type=MESH,
        )

    def go(*copies):
        for one in copies:
            one.start()
        return copies

    def done(copies):
        for one in copies:
            one.wait()

    half_of = [pl.ds(pl.multiple_of(i * HALF, D), HALF) for i in (c, o)]

    def pack(n, refs):
        for i, half in enumerate(half_of):
            rows = [ref[:, half].astype(F32) for ref in refs]
            PK[n, i] = jnp.concatenate(rows, axis=0).astype(BF16)

    def ag_first(n):
        return go(
            copy(PK.at[n, 1], PR.at[n, 0], sib),
            copy(PK.at[n, 0], PR.at[n, 1], opp),
            copy(PK.at[n, 1], PR.at[n, 2], opp_sib),
        )

    def chip_rows(mine, other, a):
        mine = mine.astype(F32)[8 * a : 8 * a + 8]
        other = other.astype(F32)[8 * a : 8 * a + 8]
        low = jnp.where(c == 0, mine, other)
        high = jnp.where(c == 0, other, mine)
        return jnp.concatenate([low, high], axis=0)

    def ag_p(ch):
        block = G.at[c, ch, q, p]
        return go(*[copy(block, block, to) for to in ring_p])

    base_f = slots(8)

    def forward(ch, n):
        i = (q + n + (n // 2) * (5 - 2 * n)) % 4
        block = G.at[c, ch, i]
        return copy(block, block, sib, slot=base_f + 4 * ch + n)

    def ag_q1(ch, copies):
        done(copies)
        block = G.at[c, ch, q]
        return go(copy(block, block, right_q), copy(block, block, left_q))

    def ag_q2(ch, copies):
        done(copies)
        one, two = G.at[c, ch, qb, 0:2], G.at[c, ch, qn, 2:4]
        return go(copy(one, one, right_q), copy(two, two, left_q))

    pack(0, (av, ado))
    pack(1, (aq, ak))
    sender = 4 * hd + 2 * zh + c
    for i, raw in enumerate((aq, ak)):
        block = raw[...].astype(F32)
        total = jnp.sum(block * block, axis=1, keepdims=True)
        HSA[sender, i] = jnp.broadcast_to(total, (8, D))
    pl.semaphore_wait(barrier, len(partners))
    first0 = ag_first(0)
    first1 = ag_first(1)
    mine = HSA.at[sender]
    first1 += go(*[copy(mine, mine, to) for to in near + heads + far[0] + far[1] + far[2]])

    HS[hd] = jnp.zeros((8, 512), F32)
    for i, raw in enumerate((vq, vk)):
        loads[i].wait()
        total = jnp.zeros((ROWS, D), F32)
        for b in range(NH):
            block = raw[:, b * D : (b + 1) * D].astype(F32)
            total = total + block * block
        HS[hd, i : i + 1, :] = row_of(total)
    sums = go(*[copy(HS.at[hd], HS.at[hd], to) for to in heads])

    done(first0)
    for a in range(2):
        G[c, 0, q, p, zh, a] = chip_rows(PK[0, 0], PR[0, 0], a).astype(BF16)
        G[c, 0, q, p, 1 - zh, a] = chip_rows(PR[0, 1], PR[0, 2], a).astype(BF16)
    ring0 = ag_p(0)

    done(first1)

    def inverse(zz, cc, i):
        total = HSA[2 * zz + cc, i]
        for k in range(1, 4):
            total = total + HSA[4 * k + 2 * zz + cc, i]
        return lax.rsqrt(total / WIDTH + EPS)

    for i, gain in enumerate((gaq_gain, gak_gain)):
        raws = chip_rows(PK[1, 0], PR[1, 0], i), chip_rows(PR[1, 1], PR[1, 2], i)
        for zz, raw in zip((zh, 1 - zh), raws):
            inv_row = jnp.concatenate([inverse(zz, cc, i) for cc in range(2)], axis=0)
            wide = jnp.concatenate([inv_row] * 3, axis=1)
            half = gain[:, half_of[0]]
            G[c, 1, q, p, zz, i] = (raw * wide * half).astype(BF16)
            RA[zz, i] = raw * half
    ring1 = ag_p(1)
    inv_a = [inverse(zh, c, i) for i in range(2)]

    loads[2].wait()
    for b in range(NH):
        at_b = slice(b * D, (b + 1) * D)
        vvT[at_b, :] = jnp.transpose(vv[:, at_b])
    done(sums)
    total = HS[0] + HS[1] + HS[2] + HS[3]
    inv = lax.rsqrt(total / WIDTH + EPS)

    def norm_video(i, raw, gain, out):
        inv_col[i] = col(inv[i : i + 1, :])
        for b in range(NH):
            at_b = slice(b * D, (b + 1) * D)
            out[:, at_b] = (raw[:, at_b].astype(F32) * inv_col[i] * gain[:, at_b]).astype(BF16)

    norm_video(1, vk, gvk_gain, vkn)
    q10 = ag_q1(0, ring0)
    go(forward(0, 0))
    norm_video(0, vq, gvq_gain, vqn)
    q11 = ag_q1(1, ring1)
    go(forward(1, 0))
    for b in range(NH):
        at_b = slice(b * D, (b + 1) * D)
        vkT[at_b, :] = jnp.transpose(vkn[:, at_b])

    def lanes_of(i):
        return pl.ds(pl.multiple_of(i * D, D), D)

    ST[...] = jnp.zeros_like(ST)

    def staged(units, make, use):
        held = None
        for unit in units:
            made = make(unit)
            if held is not None:
                use(*held)
            held = (unit, made)
        use(*held)

    def rows_of(ch, h, i, a, j):
        return G[h, ch, i, :, :, a, :, j * D : j * D + D].reshape(D, D)

    def some_rows(ch, h, ids, a, j):
        return jnp.concatenate([rows_of(ch, h, i, a, j) for i in ids], axis=0)

    def video(h, *ids):
        def make(j):
            lanes = lanes_of(3 * h + j)
            scores = dot(some_rows(1, h, ids, 1, j), vqn[:, lanes], NT) * KLOG
            return scores, dot(some_rows(0, h, ids, 0, j), vdo[:, lanes], NT)

        def use(j, made):
            scores, dprob = made
            head = 3 * h + j
            top = fold(jnp.maximum, scores)
            expo = jnp.exp2(scores - top)
            nothing = jnp.zeros_like(top)
            values = [top, fold(jnp.add, expo), fold(jnp.add, expo * dprob)]
            for n, i in enumerate(ids):
                part = slice(D * n, D * n + D)
                EV[head, lanes_of(i), :] = expo[part]
                DV[head, lanes_of(i), :] = dprob[part]
                for k in range(3):
                    SV[k, head, pl.ds(i, 1), :] = nothing if n and k else values[k]

        staged(range(3), make, use)

    def audio(h, *ids):
        def make(j):
            lanes = lanes_of(3 * h + j)
            scores = dot(vkn[:, lanes], some_rows(1, h, ids, 0, j), NT) * KLOG
            return scores, dot(vv[:, lanes], some_rows(0, h, ids, 1, j), NT)

        def use(j, made):
            scores, dprob = made
            head = 3 * h + j
            top = fold(jnp.maximum, scores)
            expo = jnp.exp2(scores - top)
            values = [top, fold(jnp.add, expo), fold(jnp.add, expo * dprob)]
            for n, i in enumerate(ids):
                part = slice(D * n, D * n + D)
                E[head, :, lanes_of(i)] = expo[:, part]
                DP[head, :, lanes_of(i)] = dprob[:, part]
                for k in range(3):
                    ST[0, k, i, pl.ds(head, 1), :] = values[k][:, part]

        staged(range(3), make, use)

    def pair(n):
        return (p + 3 * n) % 4, (p + 1 + n) % 4

    def twice(body):
        def step(n, carry):
            body(n)
            return carry

        lax.fori_loop(0, 2, step, 0)

    audio(c, q)
    loads[3].wait()
    video(c, q)
    q20 = ag_q2(0, q10)
    go(*[forward(0, n) for n in (1, 2)])
    q21 = ag_q2(1, q11)
    go(*[forward(1, n) for n in (1, 2)])
    audio(c, qn, qb)
    done(q20)
    go(forward(0, 3))
    done(q21)
    go(forward(1, 3))
    video(c, qn, qb)
    audio(c, q2)

    def their_audio(n):
        done([forward(ch, 2 * n + k) for ch in range(2) for k in range(2)])
        audio(o, *pair(n))

    twice(their_audio)

    def stats_start(level, to):
        return go(*[copy(ST.at[level], SR.at[level, k], one) for k, one in enumerate(to)])

    def stats_merge(level, copies):
        done(copies)
        tops = [ST[level, 0]] + [SR[level, k, 0] for k in range(3)]
        top = jnp.maximum(jnp.maximum(tops[0], tops[1]), jnp.maximum(tops[2], tops[3]))
        weights = [jnp.exp2(one - top) for one in tops]
        ST[level + 1, 0] = top
        for n in (1, 2):
            total = ST[level, n] * weights[0]
            for k in range(3):
                total = total + SR[level, k, n] * weights[k + 1]
            ST[level + 1, n] = total

    level0 = stats_start(0, (sib, opp, opp_sib))
    video(c, q2)
    twice(lambda n: video(o, *pair(n)))

    IA[...] = jnp.zeros_like(IA)
    base_cross = slots(6)

    def cross(ch, j):
        return copy(Xs.at[ch, j], Xr.at[ch, j], sib, slot=base_cross + 3 * ch + j)

    def put(ch, j, own, chunks, a, value):
        rows = slice(128 * chunks.start, 128 * chunks.stop)
        if own:
            value = value + Xr[ch, j, a, rows].astype(F32)
            shape = (chunks.stop - chunks.start, 4, 2, 16, D)
            R[ch, j, chunks, :, :, a] = value.reshape(shape).astype(BF16)
        else:
            Xs[ch, j, a, rows] = value.astype(BF16)

    base_q1 = slots(12)

    def rs_q1(ch, j):
        slot = base_q1 + 6 * ch + 2 * j
        return (
            copy(R.at[ch, j, q2, 0:2], RB1.at[ch, 0, j], right_q, slot=slot),
            copy(R.at[ch, j, q2, 2:4], RB1.at[ch, 1, j], left_q, slot=slot + 1),
        )

    def rs_q2(ch, heads_done):
        copies = []
        for j in heads_done:
            done(rs_q1(ch, j))
            one = R[ch, j, qn, 0:2].astype(F32) + RB1[ch, 0, j].astype(F32)
            R[ch, j, qn, 0:2] = one.astype(BF16)
            two = R[ch, j, qb, 2:4].astype(F32) + RB1[ch, 1, j].astype(F32)
            R[ch, j, qb, 2:4] = two.astype(BF16)
            copies += go(
                copy(R.at[ch, j, qn], RB2.at[ch, 0, j], right_q),
                copy(R.at[ch, j, qb], RB2.at[ch, 1, j], left_q),
            )
        return copies

    def rs_p(ch, copies):
        for j in range(3):
            done(copies[2 * j : 2 * j + 2])
            total = R[ch, j, q].astype(F32) + RB2[ch, 0, j].astype(F32) + RB2[ch, 1, j].astype(F32)
            S[ch, :, j] = total.astype(BF16)
        return go(
            *[copy(S.at[ch, (p + k + 1) % 4], RB3.at[ch, k], ring_p[k]) for k in range(3)]
        )

    def rs_last(ch, copies):
        done(copies)
        total = S[ch, p].astype(F32)
        for k in range(3):
            total = total + RB3[ch, k].astype(F32)
        for zz in range(2):
            both = [jnp.concatenate([total[j, zz, a] for j in range(3)], axis=1) for a in range(2)]
            for cc in range(2):
                rows = slice(8 * cc, 8 * cc + 8)
                tile = jnp.concatenate([both[0][rows], both[1][rows]], axis=0)
                TF[ch, zz, cc] = tile
                TZ[ch, zz, cc] = tile.astype(BF16)
            inner = jnp.sum(RA[zz, 1 - ch] * both[ch], axis=1, keepdims=True)
            HAs[zz, :, ch] = jnp.broadcast_to(inner, (16, D)).reshape(2, 8, D)
        place = ((zh, c), (zh, o), (1 - zh, c), (1 - zh, o))
        rows = go(
            *[copy(TZ.at[ch, zz, cc], RB4.at[ch, k], near[k]) for k, (zz, cc) in enumerate(place[1:])]
        )
        if ch == 0:
            return rows
        slot = HAr.at[sender]
        HAr[sender] = HAs[zh, c]
        targets = [(place[0], to) for to in heads]
        for k in range(3):
            targets += [(place[k + 1], to) for to in [near[k]] + far[k]]
        return rows + go(*[copy(HAs.at[zz, cc], slot, to) for (zz, cc), to in targets])

    def rs_end(ch, copies, slots):
        done(copies)
        mine = TF[ch, zh, c] + RB4[ch, 1].astype(F32)
        other = RB4[ch, 0].astype(F32) + RB4[ch, 2].astype(F32)
        for a, slot in enumerate(slots):
            sm[slot, :, half_of[0]] = mine[8 * a : 8 * a + 8]
            sm[slot, :, half_of[1]] = other[8 * a : 8 * a + 8]

    units = [(j, t) for j in range(3) for t in range(2)]

    def video_probs(h, part):
        j, t = part
        head = 3 * h + j
        tops = SV[0, head]
        weights = jnp.exp2(tops - jnp.max(tops, axis=0, keepdims=True))
        over = 1.0 / jnp.sum(weights * SV[1, head], axis=0, keepdims=True)
        weights = weights * over
        inner = jnp.sum(weights * SV[2, head], axis=0, keepdims=True)
        chunk = slice(256 * t, 256 * (t + 1))
        probs = jnp.concatenate(
            [EV[head, D * i : D * i + D, chunk] * weights[i : i + 1, chunk] for i in range(4)],
            axis=0,
        )
        ds = (probs * (DV[head, :, chunk] - inner[:, chunk])).astype(BF16)
        return probs.astype(BF16), ds

    def finish(ch, j, own):
        go(*(rs_q1(ch, j) if own else (cross(ch, j),)))

    def video_pass(h, own):
        sums = {}

        def use(part, made):
            j, t = part
            low, ds = made
            chunk, lanes = slice(256 * t, 256 * (t + 1)), lanes_of(3 * h + j)
            grads = dot(ds, vqn[chunk, lanes], NN), dot(low, vdo[chunk, lanes], NN)
            if t == 0:
                keys = jnp.transpose(some_rows(1, h, range(4), 1, j))
                values = jnp.transpose(some_rows(0, h, range(4), 0, j))
                sums[j] = grads + (keys, values)
            keys, values = sums[j][2:]
            video_out[chunk, lanes] = jnp.transpose(dot(values, low, NN)).astype(BF16)
            grad_q = jnp.transpose(dot(keys, ds, NN)) * FACTOR
            GQ[chunk, lanes] = grad_q
            IA[0, chunk] += vq[chunk, lanes].astype(F32) * gvq_gain[:, lanes] * grad_q
            if t == 0:
                return
            if own:
                cross(0, j).wait()
            put(0, j, own, slice(0, 4), 0, (sums[j][0] + grads[0]) * FACTOR)
            put(0, j, own, slice(0, 4), 1, sums[j][1] + grads[1])
            finish(0, j, own)

        staged(units, lambda part: video_probs(h, part), use)

    def inner_start(i):
        HI[i, hd] = jnp.zeros((8, 512), F32)
        HI[i, hd, 0:1, :] = row_of(IA[i])
        return go(*[copy(HI.at[i, hd], HI.at[i, hd], to) for to in heads])

    def video_final(i, copies, raw, gain, grad, out):
        done(copies)
        inner = (HI[i, 0] + HI[i, 1] + HI[i, 2] + HI[i, 3]) / WIDTH
        inv_i = inv_col[i]
        scale = inv_i * inv_i * inv_i * col(inner[0:1, :])
        for b in range(NH):
            at_b = slice(b * D, (b + 1) * D)
            value = inv_i * gain[:, at_b] * grad[:, at_b] - raw[:, at_b].astype(F32) * scale
            out[:, at_b] = value.astype(BF16)

    stats_merge(0, level0)
    level1 = stats_start(1, ring_p)
    video_pass(o, False)
    stats_merge(1, level1)
    level2 = stats_start(2, ring_q)
    video_pass(c, True)
    inner0 = inner_start(0)
    stats_merge(2, level2)

    total = ST[3, 1]
    safe = jnp.where(total == 0.0, 1.0, total)
    WT[0] = jnp.exp2(ST[0, 0] - ST[3, 0]) / safe
    WT[1] = ST[3, 2] / safe

    def audio_probs(h, part):
        j, t = part
        head = 3 * h + j
        row = pl.ds(head, 1)
        weight, shift = (
            jnp.concatenate([WT[n, 2 * t, row, :], WT[n, 2 * t + 1, row, :]], axis=1)
            for n in (0, 1)
        )
        chunk = slice(256 * t, 256 * (t + 1))
        probs = E[head, :, chunk] * weight
        ds = (probs * (DP[head, :, chunk] - shift)).astype(BF16)
        return probs.astype(BF16), ds

    def audio_pass(h, own):
        def use(part, made):
            j, t = part
            low, ds = made
            lanes = lanes_of(3 * h + j)
            chunks = slice(2 * t, 2 * t + 2)
            numer = jnp.transpose(dot(vvT[lanes, :], low, NN))
            grad_q = jnp.transpose(dot(vkT[lanes, :], ds, NN)) * FACTOR
            if own and t == 0:
                cross(1, j).wait()
            put(1, j, own, chunks, 0, numer)
            put(1, j, own, chunks, 1, grad_q)
            if t == 1:
                finish(1, j, own)

        staged(units, lambda part: audio_probs(h, part), use)

    def row_pass(h):
        sums = {}

        def use(part, made):
            j, t = part
            low, ds = made
            lanes = lanes_of(3 * h + j)
            ids = (2 * t, 2 * t + 1)
            grads = dot(ds, some_rows(1, h, ids, 0, j), NN), dot(low, some_rows(0, h, ids, 1, j), NN)
            if t == 0:
                sums[j] = grads
                return
            grad_k = (sums[j][0] + grads[0]) * FACTOR
            out_gvv[:, lanes] = (sums[j][1] + grads[1]).astype(BF16)
            GK[:, lanes] = grad_k
            IA[1] += vk[:, lanes].astype(F32) * gvk_gain[:, lanes] * grad_k

        staged(units, lambda part: audio_probs(h, part), use)

    audio_pass(o, False)
    a2 = rs_q2(0, (0, 1, 2))
    audio_pass(c, True)
    b2 = rs_q2(1, (0,))
    a3 = rs_p(0, a2)
    row_pass(0)
    b2 += rs_q2(1, (1, 2))
    a4 = rs_last(0, a3)
    row_pass(1)
    b3 = rs_p(1, b2)
    inner1 = inner_start(1)
    b4 = rs_last(1, b3)
    video_final(0, inner0, vq, gvq_gain, GQ, out_gvq)
    video_final(1, inner1, vk, gvk_gain, GK, out_gvk)
    rs_end(0, a4, (3, 4))
    rs_end(1, b4, (5, 2))
    out_small[0] = sm[5]
    out_small[3] = sm[4]
    parts = ((aq, gaq_gain, sm[2]), (ak, gak_gain, sm[3]))
    for i, (raw, gain, grad) in enumerate(parts):
        total = HAr[0, 1 - i]
        for k in range(1, 16):
            total = total + HAr[k, 1 - i]
        total = total / WIDTH
        wide = jnp.concatenate([inv_a[i]] * NH, axis=1)
        scale = jnp.concatenate([inv_a[i] * inv_a[i] * inv_a[i] * total] * NH, axis=1)
        out_small[1 + i] = wide * gain[...] * grad - raw[...].astype(F32) * scale


def write_kernel(
    a, b, c, d, small, out_a, out_b, out_c, out_d, small_0, small_1, small_2, small_3, sems
):
    pairs = ((a, out_a), (b, out_b), (c, out_c), (d, out_d))
    copies = [pltpu.make_async_copy(src, dst, sems.at[i]) for i, (src, dst) in enumerate(pairs)]
    for one in copies:
        one.start()
    for i, out in enumerate((small_0, small_1, small_2, small_3)):
        out[...] = small[i].astype(BF16)
    for one in copies:
        one.wait()


def shards(*args):
    big = jax.ShapeDtypeStruct((ROWS, LOCAL), BF16)
    vmem = pltpu.VMEM
    wide = vmem((ROWS, LOCAL), BF16)
    scratch = [wide] * 4 + [
        vmem((8, LOCAL), F32),
        vmem((2, 2, 16, HALF), F32),
        vmem((2, 2, 4, 4, 2, 2, 16, HALF), BF16),
        vmem((2, 2, 16, HALF), BF16),
        vmem((2, 3, 16, HALF), BF16),
        vmem((16, 2, 8, D), F32),
        vmem((4, 8, 512), F32),
        vmem((2, 4, 8, 512), F32),
        vmem((2, 2, 2, 8, D), F32),
        vmem((16, 2, 8, D), F32),
        vmem((ROWS, LOCAL), BF16),
        vmem((ROWS, LOCAL), BF16),
        vmem((LOCAL, ROWS), BF16),
        vmem((LOCAL, ROWS), BF16),
        vmem((2, ROWS, D), F32),
        vmem((NH, ROWS, TOK), F32),
        vmem((NH, ROWS, TOK), F32),
        vmem((NH, TOK, ROWS), F32),
        vmem((NH, TOK, ROWS), F32),
        vmem((3, NH, 4, ROWS), F32),
        vmem((4, 3, 4, 8, D), F32),
        vmem((3, 3, 3, 4, 8, D), F32),
        vmem((2, 4, 8, D), F32),
        vmem((ROWS, LOCAL), F32),
        vmem((ROWS, LOCAL), F32),
        vmem((2, ROWS, D), F32),
        vmem((2, 3, 2, TOK, D), BF16),
        vmem((2, 3, 2, TOK, D), BF16),
        vmem((2, 3, 4, 4, 2, 2, 16, D), BF16),
        vmem((2, 2, 3, 2, 2, 2, 16, D), BF16),
        vmem((2, 2, 3, 4, 2, 2, 16, D), BF16),
        vmem((2, 4, 3, 2, 2, 16, D), BF16),
        vmem((2, 3, 3, 2, 2, 16, D), BF16),
        vmem((2, 2, 2, 16, HALF), F32),
        vmem((2, 2, 2, 16, HALF), BF16),
        vmem((2, 3, 16, HALF), BF16),
        vmem((6, 8, LOCAL), F32),
        pltpu.SemaphoreType.DMA((160,)),
        pltpu.SemaphoreType.DMA((160,)),
        pltpu.SemaphoreType.DMA((8,)),
    ]
    spec = pl.BlockSpec(memory_space=pltpu.VMEM)
    anywhere = pl.BlockSpec(memory_space=pl.ANY)
    made = pl.pallas_call(
        kernel,
        out_shape=(vmem((ROWS, LOCAL), BF16),) * 4 + (vmem((4, 8, LOCAL), F32),),
        in_specs=[anywhere] * 4 + [spec] * 8,
        out_specs=(spec,) * 5,
        scratch_shapes=scratch,
        compiler_params=pltpu.CompilerParams(
            collective_id=0, has_side_effects=True, vmem_limit_bytes=57 * 1024 * 1024
        ),
    )(*args)
    small = jax.ShapeDtypeStruct((8, LOCAL), BF16)
    wrote = pl.pallas_call(
        write_kernel,
        out_shape=(big,) * 4 + (small,) * 4,
        in_specs=[spec] * 5,
        out_specs=(anywhere,) * 4 + (spec,) * 4,
        scratch_shapes=[pltpu.SemaphoreType.DMA((4,))],
        compiler_params=pltpu.CompilerParams(vmem_limit_bytes=4 * 1024 * 1024),
    )(*[pltpu.with_memory_space_constraint(one, pltpu.VMEM) for one in made])
    video_out, gvq, gvk, gvv, audio_out, gaq, gak, gav = wrote
    return video_out, audio_out, gvq, gvk, gvv, gaq, gak, gav


def solution(mesh):
    both = P("seq", "head")
    return jax.shard_map(
        shards,
        mesh=mesh,
        in_specs=(both,) * 8 + (P("head"),) * 4,
        out_specs=(both,) * 8,
        check_vma=False,
    )
```
